32 devices in a mesh: grp: 4 (over x, core), gx: 2 (over y), gy: 4 (over z).
Axes of the slice: x: 2, y: 2, z: 4, core: 2. Of those that a mesh axis runs over, the one named last changes fastest.
Arguments:
- flow_fields: float32 [4, 32, 4, 512], P('grp', None, 'gx', 'gy'), may hold values from -4 to 4
- level_set: float32 [4, 64, 8, 1024], P('grp', None, 'gx', 'gy'), may hold values from -9 to 9
- band_tiles: int32 [8, 2, 64], P(None, 'gx', 'gy'), may hold values 0 or 1
- nozzle_phase: int32 [8, 1024], P('gx', 'gy'), may hold values from 0 to 2
Outputs:
- flow_next: float32 [4, 32, 4, 512], P('grp', None, 'gx', 'gy')
The draws below stay inside these ranges and needn't reach their ends.
All inputs are finite; a program needn't handle non-finite values. No bound on the sum of `band_tiles` on one device may be relied on, other than what follows from the above.
Results may differ from the reference program's by a relative error of at most 0.0003.
Values sent between devices are 32-bit elements; how exact they have to be, the bound alone decides.
A program may use at most 64 MiB of HBM per device.

```python
import jax
import jax.numpy as jnp
from jax import lax

NZ = 32
SWEEPS = 3
NX = 4
NY = 512


def draw_level_set(key, part):
    extent = (4, 2 * NZ, 2 * NX, 2 * NY)
    texture = 1.5 * jax.random.normal(key, extent, jnp.float32)
    return jnp.clip(texture, -9.0, 9.0)


def with_ends(drawn, own_key, low, largest):
    longest = drawn.shape.index(max(drawn.shape))
    spots = []
    for shift in (0, 1):
        where = [jax.random.randint(jax.random.fold_in(own_key, axis), (), 0, length) for axis, length in enumerate(drawn.shape)]
        where[longest] = (where[longest] + shift) % drawn.shape[longest]
        spots.append(tuple(where))
    return drawn.at[spots[0]].set(low).at[spots[1]].set(largest)


def block_levels(rng, shape, shards, low, top_value):
    def one(position, blocks):
        steps = jax.random.uniform(jax.random.fold_in(jax.random.fold_in(rng, 6), position), (blocks,), jnp.float32, low / len(shards), top_value / len(shards))
        return jnp.repeat(jnp.exp(steps), shape[position] // blocks).reshape((-1,) + (1,) * (len(shape) - position - 1))

    gain = one(*shards[0])
    for cut in shards[1:]:
        gain = gain * one(*cut)
    return gain


def bell_draw(rng, dims, width, limit, pieces=(), held_as=jnp.bfloat16):
    gain = block_levels(rng, dims, pieces, -0.22, 0.18) if pieces else 1.0
    array = jax.random.normal(rng, dims, jnp.float32) * width * gain
    return jnp.minimum(jnp.maximum(array, -limit), limit).astype(held_as)


def setup_inputs(seed: int = 0) -> dict:
    splits = jax.random.split(jax.random.key(seed), 5)
    return {
        "flow_fields": bell_draw(splits[0], (4, NZ, NX, NY), 0.6, 4.0, ((0, 4), (2, 2), (3, 4)), jnp.float32),
        "level_set": draw_level_set(jax.random.fold_in(splits[4], 71), 0),
        "band_tiles": with_ends((jax.random.randint(splits[2], (2 * NZ // 8, NX // 2, NY // 8), 0, 3) < 2).astype(jnp.int32), jax.random.fold_in(splits[2], 1), 0, 1),
        "nozzle_phase": with_ends(jax.random.randint(splits[3], (2 * NX, 2 * NY), 0, 3), jax.random.fold_in(splits[3], 1), 0, 2).astype(jnp.int32),
    }


WENO_EPS = 1e-06
STEP_FINE = 0.3
STEP_FLOW = 0.2
SURFACE = 6.0
SPREAD = 1.5
IMPLICIT = 0.5

def weno_side(diff_one, diff_two, diff_three, diff_four, diff_five):
    cand_one = diff_one / 3.0 - 7.0 * diff_two / 6.0 + 11.0 * diff_three / 6.0
    cand_two = -diff_two / 6.0 + 5.0 * diff_three / 6.0 + diff_four / 3.0
    cand_three = diff_three / 3.0 + 5.0 * diff_four / 6.0 - diff_five / 6.0
    curve_one = diff_one - 2.0 * diff_two + diff_three
    slope_one = diff_one - 4.0 * diff_two + 3.0 * diff_three
    smooth_one = 13.0 / 12.0 * curve_one * curve_one + 0.25 * slope_one * slope_one
    curve_two = diff_two - 2.0 * diff_three + diff_four
    slope_two = diff_two - diff_four
    smooth_two = 13.0 / 12.0 * curve_two * curve_two + 0.25 * slope_two * slope_two
    curve_three = diff_three - 2.0 * diff_four + diff_five
    slope_three = 3.0 * diff_three - 4.0 * diff_four + diff_five
    smooth_three = 13.0 / 12.0 * curve_three * curve_three + 0.25 * slope_three * slope_three
    weight_one = 0.1 / ((WENO_EPS + smooth_one) * (WENO_EPS + smooth_one))
    weight_two = 0.6 / ((WENO_EPS + smooth_two) * (WENO_EPS + smooth_two))
    weight_three = 0.3 / ((WENO_EPS + smooth_three) * (WENO_EPS + smooth_three))
    return (weight_one * cand_one + weight_two * cand_two + weight_three * cand_three) / (weight_one + weight_two + weight_three)

def section_rate(padded, speeds):
    row_count = padded.shape[1] - 6
    col_count = padded.shape[2] - 6

    def sample(offset, direction):
        if direction == 0:
            return jnp.roll(padded[:, 3:3 + row_count, 3:3 + col_count], -offset, 0)
        if direction == 1:
            return padded[:, 3 + offset:3 + offset + row_count, 3:3 + col_count]
        return padded[:, 3:3 + row_count, 3 + offset:3 + offset + col_count]
    summed = jnp.zeros((padded.shape[0], row_count, col_count), jnp.float32)
    for direction in range(3):
        differences = [sample(offset + 1, direction) - sample(offset, direction) for offset in range(-3, 3)]
        minus_side = weno_side(differences[0], differences[1], differences[2], differences[3], differences[4])
        plus_side = weno_side(differences[5], differences[4], differences[3], differences[2], differences[1])
        upwind = jnp.where(speeds[direction] >= 0.0, minus_side, plus_side)
        summed = summed - speeds[direction] * upwind
    return summed

def refine(coarse):
    plane_count, height, breadth = coarse.shape
    spread_out = jnp.broadcast_to(coarse[:, None, :, None, :, None], (plane_count, 2, height, 2, breadth, 2))
    return spread_out.reshape(2 * plane_count, 2 * height, 2 * breadth)

def coarsen(fine_field):
    plane_count, height, breadth = fine_field.shape
    blocks = fine_field.reshape(plane_count // 2, 2, height // 2, 2, breadth // 2, 2)
    return lax.optimization_barrier(jnp.sum(blocks, axis=(1, 3, 5))) * 0.125

def band_cells(tile_flags):
    planes, height, breadth = tile_flags.shape
    spread_out = jnp.broadcast_to(tile_flags[:, None, :, None, :, None], (planes, 8, height, 4, breadth, 16))
    return spread_out.reshape(planes * 8, height * 4, breadth * 16)

def with_nozzle(banded, phases):
    inflow = jnp.where(phases == 2, 1.5, jnp.where(phases == 1, -1.5, banded[0]))
    return jnp.concatenate([inflow[None], banded[1:]], axis=0)

def surface_terms(padded):
    middle = padded[:, 1:-1, 1:-1]
    grad_x = (padded[:, 2:, 1:-1] - padded[:, :-2, 1:-1]) * 0.5
    grad_y = (padded[:, 1:-1, 2:] - padded[:, 1:-1, :-2]) * 0.5
    grad_z = (jnp.roll(middle, -1, 0) - jnp.roll(middle, 1, 0)) * 0.5
    inverse = 1.0 / jnp.sqrt(grad_x * grad_x + grad_y * grad_y + grad_z * grad_z + 1.0)
    normal_x = grad_x * inverse
    normal_y = grad_y * inverse
    normal_z = grad_z * inverse
    inner_z = normal_z[:, 1:-1, 1:-1]
    curvature = (normal_x[:, 2:, 1:-1] - normal_x[:, :-2, 1:-1]) * 0.5
    curvature = curvature + (normal_y[:, 1:-1, 2:] - normal_y[:, 1:-1, :-2]) * 0.5
    curvature = curvature + (jnp.roll(inner_z, -1, 0) - jnp.roll(inner_z, 1, 0)) * 0.5
    surface_level = padded[:, 2:-2, 2:-2]
    delta_peak = jnp.exp(-surface_level * surface_level / (2.0 * SPREAD * SPREAD)) / (SPREAD * 2.5066282746310002)
    strength = SURFACE * curvature * delta_peak
    fraction = 0.5 + 0.5 * jnp.tanh(surface_level / SPREAD)
    return jnp.stack([coarsen(normal_x[:, 1:-1, 1:-1] * strength), coarsen(normal_y[:, 1:-1, 1:-1] * strength), coarsen(inner_z * strength), coarsen(fraction)])

def centered(padded, direction):
    if direction == 0:
        middle = padded[:, 1:-1, 1:-1]
        return (jnp.roll(middle, -1, 0) - jnp.roll(middle, 1, 0)) * 0.5
    if direction == 1:
        return (padded[:, 2:, 1:-1] - padded[:, :-2, 1:-1]) * 0.5
    return (padded[:, 1:-1, 2:] - padded[:, 1:-1, :-2]) * 0.5

def predictor(padded_fields, component):
    moving = lax.dynamic_index_in_dim(padded_fields, component, 0, keepdims=False)
    inner_u = padded_fields[0, :, 1:-1, 1:-1]
    inner_v = padded_fields[1, :, 1:-1, 1:-1]
    inner_w = padded_fields[2, :, 1:-1, 1:-1]
    advect = -(inner_w * centered(moving, 0) + inner_u * centered(moving, 1) + inner_v * centered(moving, 2))
    pressure = padded_fields[3]
    gradients = jnp.stack([centered(pressure, 1), centered(pressure, 2), centered(pressure, 0)])
    pushed = lax.dynamic_index_in_dim(gradients, component, 0, keepdims=False)
    return moving[:, 1:-1, 1:-1] + STEP_FLOW * (advect - pushed)

def sweep_once(padded, source):
    middle = padded[:, 1:-1, 1:-1]
    beside_all = padded[:, 2:, 1:-1] + padded[:, :-2, 1:-1] + padded[:, 1:-1, 2:] + padded[:, 1:-1, :-2]
    beside_all = beside_all + jnp.roll(middle, -1, 0) + jnp.roll(middle, 1, 0)
    return (source + IMPLICIT * beside_all) / (1.0 + 6.0 * IMPLICIT)

def reference(flow_fields, level_set, band_tiles, nozzle_phase):
    padded_fields = jnp.pad(flow_fields, ((0, 0), (0, 0), (1, 1), (1, 1)), mode='wrap')
    speeds = (refine(flow_fields[2]), refine(flow_fields[0]), refine(flow_fields[1]))
    initial = level_set[3]

    def run_section(current, keep_weight, blend_weight):
        padded = jnp.pad(current, ((0, 0), (3, 3), (3, 3)), mode='wrap')
        return keep_weight * initial + blend_weight * (current + STEP_FINE * section_rate(padded, speeds))
    first_section = run_section(initial, 0.0, 1.0)
    second_section = run_section(first_section, 0.75, 0.25)
    third_section = run_section(second_section, 1.0 / 3.0, 2.0 / 3.0)
    banded = jnp.where(band_cells(band_tiles) == 1, third_section, initial)
    shaped = with_nozzle(banded, nozzle_phase)
    surface = surface_terms(jnp.pad(shaped, ((0, 0), (2, 2), (2, 2)), mode='wrap'))
    outputs = []
    for component in range(3):
        source = predictor(padded_fields, component)
        relaxed = source
        for sweep_number in range(SWEEPS):
            relaxed = sweep_once(jnp.pad(relaxed, ((0, 0), (1, 1), (1, 1)), mode='wrap'), source)
        outputs.append(relaxed + STEP_FLOW * surface[component])
    outputs.append(surface[3])
    return jnp.stack(outputs)
```

```python
import functools

import jax
import jax.numpy as jnp
from jax import lax
from jax.experimental import pallas as pl
from jax.experimental.pallas import tpu as pltpu
from jax.sharding import PartitionSpec as P

SWEEPS = 3


WENO_EPS = 1e-06
STEP_FINE = 0.3
STEP_FLOW = 0.2
SURFACE = 6.0
SPREAD = 1.5
IMPLICIT = 0.5


def extended(block, sides, width):
    for axis, dim in sides:
        count = lax.axis_size(axis)
        forward = [(i, i + 1) for i in range(count - 1)]
        forward.append((count - 1, 0))
        backward = [(target, source) for source, target in forward]
        low = lax.ppermute(
            lax.slice_in_dim(block, block.shape[dim] - width, None, axis=dim), axis, forward
        )
        high = lax.ppermute(lax.slice_in_dim(block, 0, width, axis=dim), axis, backward)
        block = jnp.concatenate([low, block, high], axis=dim)
    return block


def weno_side(diff_one, diff_two, diff_three, diff_four, diff_five):
    cand_one = diff_one / 3.0 - 7.0 * diff_two / 6.0 + 11.0 * diff_three / 6.0
    cand_two = -diff_two / 6.0 + 5.0 * diff_three / 6.0 + diff_four / 3.0
    cand_three = diff_three / 3.0 + 5.0 * diff_four / 6.0 - diff_five / 6.0
    curve_one = diff_one - 2.0 * diff_two + diff_three
    slope_one = diff_one - 4.0 * diff_two + 3.0 * diff_three
    smooth_one = 13.0 / 12.0 * curve_one * curve_one + 0.25 * slope_one * slope_one
    curve_two = diff_two - 2.0 * diff_three + diff_four
    slope_two = diff_two - diff_four
    smooth_two = 13.0 / 12.0 * curve_two * curve_two + 0.25 * slope_two * slope_two
    curve_three = diff_three - 2.0 * diff_four + diff_five
    slope_three = 3.0 * diff_three - 4.0 * diff_four + diff_five
    smooth_three = 13.0 / 12.0 * curve_three * curve_three + 0.25 * slope_three * slope_three
    weight_one = 0.1 / ((WENO_EPS + smooth_one) * (WENO_EPS + smooth_one))
    weight_two = 0.6 / ((WENO_EPS + smooth_two) * (WENO_EPS + smooth_two))
    weight_three = 0.3 / ((WENO_EPS + smooth_three) * (WENO_EPS + smooth_three))
    return (weight_one * cand_one + weight_two * cand_two + weight_three * cand_three) / (
        weight_one + weight_two + weight_three
    )


def section_rate(padded, speeds, plane_rim):
    plane_count = padded.shape[0] - 2 * plane_rim
    row_count = padded.shape[1] - 6
    col_count = padded.shape[2] - 6

    def sample(offset, direction):
        if direction == 0:
            return padded[
                3 + offset : 3 + offset + plane_count, 3 : 3 + row_count, 3 : 3 + col_count
            ]
        if direction == 1:
            return padded[
                plane_rim : plane_rim + plane_count,
                3 + offset : 3 + offset + row_count,
                3 : 3 + col_count,
            ]
        return padded[
            plane_rim : plane_rim + plane_count,
            3 : 3 + row_count,
            3 + offset : 3 + offset + col_count,
        ]

    summed = jnp.zeros((plane_count, row_count, col_count), jnp.float32)
    for direction in range(3):
        differences = [
            sample(offset + 1, direction) - sample(offset, direction) for offset in range(-3, 3)
        ]
        minus_side = weno_side(
            differences[0], differences[1], differences[2], differences[3], differences[4]
        )
        plus_side = weno_side(
            differences[5], differences[4], differences[3], differences[2], differences[1]
        )
        upwind = jnp.where(speeds[direction] >= 0.0, minus_side, plus_side)
        summed = summed - speeds[direction] * upwind
    return summed


def refine(coarse):
    plane_count, height, breadth = coarse.shape
    spread_out = jnp.broadcast_to(
        coarse[:, None, :, None, :, None], (plane_count, 2, height, 2, breadth, 2)
    )
    return spread_out.reshape(2 * plane_count, 2 * height, 2 * breadth)


def coarsen(fine_field):
    plane_count, height, breadth = fine_field.shape
    blocks = fine_field.reshape(plane_count // 2, 2, height // 2, 2, breadth // 2, 2)
    return jnp.sum(blocks, axis=(1, 3, 5)) * 0.125


def band_cells(tile_flags):
    planes, height, breadth = tile_flags.shape
    spread_out = jnp.broadcast_to(
        tile_flags[:, None, :, None, :, None], (planes, 8, height, 4, breadth, 16)
    )
    return spread_out.reshape(planes * 8, height * 4, breadth * 16)


def with_nozzle(banded, phases):
    inflow = jnp.where(phases == 2, 1.5, jnp.where(phases == 1, -1.5, banded[0]))
    return jnp.concatenate([inflow[None], banded[1:]], axis=0)


def surface_finish(normal_x, normal_y, normal_z, curvature, surface_level):
    delta_peak = jnp.exp(-surface_level * surface_level / (2.0 * SPREAD * SPREAD)) / (
        SPREAD * 2.5066282746310002
    )
    strength = SURFACE * curvature * delta_peak
    fraction = 0.5 + 0.5 * jnp.tanh(surface_level / SPREAD)
    return jnp.stack(
        [
            coarsen(normal_x * strength),
            coarsen(normal_y * strength),
            coarsen(normal_z * strength),
            coarsen(fraction),
        ]
    )


def surface_slab(padded):
    grad_x = (padded[1:-1, 2:, 1:-1] - padded[1:-1, :-2, 1:-1]) * 0.5
    grad_y = (padded[1:-1, 1:-1, 2:] - padded[1:-1, 1:-1, :-2]) * 0.5
    grad_z = (padded[2:, 1:-1, 1:-1] - padded[:-2, 1:-1, 1:-1]) * 0.5
    inverse = 1.0 / jnp.sqrt(grad_x * grad_x + grad_y * grad_y + grad_z * grad_z + 1.0)
    normal_x = grad_x * inverse
    normal_y = grad_y * inverse
    normal_z = grad_z * inverse
    curvature = (normal_x[1:-1, 2:, 1:-1] - normal_x[1:-1, :-2, 1:-1]) * 0.5
    curvature = curvature + (normal_y[1:-1, 1:-1, 2:] - normal_y[1:-1, 1:-1, :-2]) * 0.5
    curvature = curvature + (normal_z[2:, 1:-1, 1:-1] - normal_z[:-2, 1:-1, 1:-1]) * 0.5
    return surface_finish(
        normal_x[1:-1, 1:-1, 1:-1],
        normal_y[1:-1, 1:-1, 1:-1],
        normal_z[1:-1, 1:-1, 1:-1],
        curvature,
        padded[2:-2, 2:-2, 2:-2],
    )


def centered(padded, direction):
    if direction == 0:
        middle = padded[:, 1:-1, 1:-1]
        return (jnp.roll(middle, -1, 0) - jnp.roll(middle, 1, 0)) * 0.5
    if direction == 1:
        return (padded[:, 2:, 1:-1] - padded[:, :-2, 1:-1]) * 0.5
    return (padded[:, 1:-1, 2:] - padded[:, 1:-1, :-2]) * 0.5


def predictor(padded_fields, component):
    moving = lax.dynamic_index_in_dim(padded_fields, component, 0, keepdims=False)
    inner_u = padded_fields[0, :, 1:-1, 1:-1]
    inner_v = padded_fields[1, :, 1:-1, 1:-1]
    inner_w = padded_fields[2, :, 1:-1, 1:-1]
    advect = -(
        inner_w * centered(moving, 0)
        + inner_u * centered(moving, 1)
        + inner_v * centered(moving, 2)
    )
    pressure = padded_fields[3]
    gradients = jnp.stack([centered(pressure, 1), centered(pressure, 2), centered(pressure, 0)])
    pushed = lax.dynamic_index_in_dim(gradients, component, 0, keepdims=False)
    return moving[:, 1:-1, 1:-1] + STEP_FLOW * (advect - pushed)


def sweep_once(padded, source):
    middle = padded[:, 1:-1, 1:-1]
    beside_all = (
        padded[:, 2:, 1:-1] + padded[:, :-2, 1:-1] + padded[:, 1:-1, 2:] + padded[:, 1:-1, :-2]
    )
    beside_all = beside_all + jnp.roll(middle, -1, 0) + jnp.roll(middle, 1, 0)
    return (source + IMPLICIT * beside_all) / (1.0 + 6.0 * IMPLICIT)


def spread_surface(level_set, band_tiles, nozzle_phase, inner_fields, is_level, group):
    fine_all = level_set[0]
    initial = lax.psum_scatter(
        jnp.where(is_level, fine_all, jnp.zeros_like(fine_all)),
        "grp",
        scatter_dimension=0,
        tiled=True,
    )
    coarse_planes = inner_fields.shape[1] // 4
    flow_slab = lax.dynamic_slice_in_dim(inner_fields, group * coarse_planes, coarse_planes, 1)
    speeds = (refine(flow_slab[2]), refine(flow_slab[0]), refine(flow_slab[1]))

    def run_section(current, keep_weight, blend_weight):
        padded = extended(current, (("grp", 0), ("gx", 1), ("gy", 2)), 3)
        return keep_weight * initial + blend_weight * (
            current + STEP_FINE * section_rate(padded, speeds, 3)
        )

    first_section = run_section(initial, 0.0, 1.0)
    second_section = run_section(first_section, 0.75, 0.25)
    third_section = run_section(second_section, 1.0 / 3.0, 2.0 / 3.0)
    tile_planes = band_tiles.shape[0] // 4
    tiles_here = lax.dynamic_slice_in_dim(band_tiles, group * tile_planes, tile_planes, 0)
    banded = jnp.where(band_cells(tiles_here) == 1, third_section, initial)
    shaped = jnp.where(group == 0, with_nozzle(banded, nozzle_phase), banded)
    surface_pad = extended(shaped, (("grp", 0), ("gx", 1), ("gy", 2)), 2)
    quarter = surface_slab(surface_pad)
    received = lax.all_to_all(quarter, "grp", split_axis=0, concat_axis=1, tiled=True)
    return (received, received[0])


def on_device_general(flow_fields, level_set, band_tiles, nozzle_phase):
    group = lax.axis_index("grp")
    component = jnp.minimum(group, 2)
    is_level = group == 3
    gathered = lax.all_gather(flow_fields, "grp", axis=0, tiled=True)
    padded_fields = extended(gathered, (("gx", 2), ("gy", 3)), 1)
    source = predictor(padded_fields, component)
    inner_fields = padded_fields[:, :, 1:-1, 1:-1]
    received, fraction = spread_surface(
        level_set, band_tiles, nozzle_phase, inner_fields, is_level, group
    )
    pushed = received[0]
    relaxed = source
    for sweep_number in range(SWEEPS):
        padded = extended(relaxed, (("gx", 1), ("gy", 2)), 1)
        relaxed = sweep_once(padded, source)
    updated = relaxed + STEP_FLOW * pushed
    result = jnp.where(is_level, fraction, updated)
    return result[None]


MESH = pl.DeviceIdType.MESH
LANES = 128
ROWS = 8
EXACT = lax.Precision.HIGHEST


def lanes_of(shape, dim=1):
    return lax.broadcasted_iota(jnp.int32, shape, dim)


def along_z(block, offset, period):
    spot = lanes_of(block.shape) % period
    plain = pltpu.roll(block, (-offset) % LANES, 1)
    if offset > 0:
        around = pltpu.roll(block, (period - offset) % LANES, 1)
        return jnp.where(spot < period - offset, plain, around)
    around = pltpu.roll(block, (-period - offset) % LANES, 1)
    return jnp.where(spot >= -offset, plain, around)


def along_rows(block, offset):
    return pltpu.roll(block, (-offset) % block.shape[0], 0)


def weno_upwind(diffs, speed):
    forward = speed >= 0.0
    one = jnp.where(forward, diffs[0], diffs[5])
    two = jnp.where(forward, diffs[1], diffs[4])
    three = jnp.where(forward, diffs[2], diffs[3])
    four = jnp.where(forward, diffs[3], diffs[2])
    five = jnp.where(forward, diffs[4], diffs[1])
    step_a = two - one
    step_b = three - two
    step_c = four - three
    step_d = five - four

    def weight(curve, slope):
        rough = (WENO_EPS * 12.0 / 13.0) + curve * curve + (3.0 / 13.0) * (slope * slope)
        inverse = 1.0 / rough
        return inverse * inverse

    weight_one = weight(step_b - step_a, 3.0 * step_b - step_a)
    weight_two = 6.0 * weight(step_c - step_b, step_c + step_b)
    weight_three = 3.0 * weight(step_d - step_c, 3.0 * step_c - step_d)
    mixed = (
        weight_one * (5.0 * step_b - 2.0 * step_a)
        + weight_two * (step_b + 2.0 * step_c)
        + weight_three * (4.0 * step_c - step_d)
    )
    total = weight_one + weight_two + weight_three
    return three + mixed / (6.0 * total)


def window(index, count, chunk, margin):
    low = index * chunk - margin
    high = (index + 1) * chunk + margin
    start, stop = max(low, 0), min(high, count * chunk)
    return start, stop - start, start - low


def brick_kernel(
    plan,
    flow_ref,
    level_ref,
    marks_ref,
    out_ref,
    flow_turned,
    level_turned,
    marks_turned,
    flow_in,
    level_in,
    marks_in,
    speeds,
    stage_one,
    stage_two,
    shaped,
    normals,
    packed,
    results,
    gathered,
    send_sems,
    take_sems,
):
    groups, halves, rings = plan["groups"], plan["halves"], plan["rings"]
    chunks = groups * halves
    fine_chunk, flow_chunk = plan["fine_chunk"], plan["flow_chunk"]
    fine_z, flow_z = plan["fine_z"], plan["flow_z"]
    fine_margin, mark_margin, flow_margin = 2 * ROWS, ROWS, ROWS
    pairs = level_ref.shape[0]
    majors = pairs * halves
    group = lax.axis_index("grp")
    half = lax.axis_index("gx")
    ring = lax.axis_index("gy")
    after = lax.rem(ring + 1, rings)
    before = lax.rem(ring + rings - 1, rings)
    mine = group * halves + half
    last = chunks - 1

    barrier = pltpu.get_barrier_semaphore()

    def greet(target_group, target_half, target_ring):
        pl.semaphore_signal(
            barrier,
            inc=1,
            device_id=(target_group, target_half, target_ring),
            device_id_type=MESH,
        )

    for chunk in range(chunks):
        tg, th = chunk // halves, chunk % halves

        @pl.when(mine != chunk)
        def _(tg=tg, th=th):
            greet(tg, th, ring)

        @pl.when(mine == 0)
        def _(tg=tg, th=th):
            greet(tg, th, before)

        @pl.when(mine == last)
        def _(tg=tg, th=th):
            greet(tg, th, after)

    @pl.when(group == groups - 1)
    def _():
        for pair in range(pairs):
            level_turned[pair] = level_ref[pair].T

    doubled = jnp.concatenate([flow_ref[...]] * halves, axis=0)
    flow_turned[...] = doubled.T
    marks_turned[...] = marks_ref[...].T

    pl.semaphore_wait(barrier, chunks + 1)

    sent = []

    def push(source, target, chunk, ring_to, take, condition=None):
        tg, th = chunk // halves, chunk % halves
        slot = len(sent)
        remote = pltpu.make_async_remote_copy(
            src_ref=source,
            dst_ref=target,
            send_sem=send_sems.at[slot],
            recv_sem=take_sems.at[take],
            device_id=(tg, th, ring_to),
            device_id_type=MESH,
        )
        near = ring_to is ring
        far = mine != chunk if near else None
        if condition is not None:
            far = condition if far is None else jnp.logical_and(condition, far)
        if near:
            here = mine == chunk
            if condition is not None:
                here = jnp.logical_and(condition, here)

            @pl.when(here)
            def _():
                pltpu.make_async_copy(source, target, take_sems.at[take]).start()

        if far is None:
            remote.start()
        else:
            pl.when(far)(remote.start)
        sent.append((far, remote))

    holder = group == groups - 1
    major_spot = pl.ds(half * pairs, pairs)
    for chunk in range(chunks):
        start, count, spot = window(chunk, chunks, fine_chunk, fine_margin)
        push(
            level_turned.at[:, pl.ds(start, count)],
            level_in.at[major_spot, pl.ds(spot, count)],
            chunk,
            ring,
            0,
            holder,
        )
    fine_rows = chunks * fine_chunk
    push(
        level_turned.at[:, pl.ds(fine_rows - fine_margin, fine_margin)],
        level_in.at[major_spot, pl.ds(0, fine_margin)],
        0,
        after,
        0,
        holder,
    )
    push(
        level_turned.at[:, pl.ds(0, fine_margin)],
        level_in.at[major_spot, pl.ds(fine_margin + fine_chunk, fine_margin)],
        last,
        before,
        0,
        holder,
    )
    for chunk in range(chunks):
        start, count, spot = window(chunk, chunks, flow_chunk, flow_margin)
        push(
            flow_turned.at[pl.ds(start, count)],
            flow_in.at[group, half, pl.ds(spot, count)],
            chunk,
            ring,
            1,
        )
    flow_rows = chunks * flow_chunk
    push(
        flow_turned.at[pl.ds(flow_rows - flow_margin, flow_margin)],
        flow_in.at[group, half, pl.ds(0, flow_margin)],
        0,
        after,
        1,
    )
    push(
        flow_turned.at[pl.ds(0, flow_margin)],
        flow_in.at[group, half, pl.ds(flow_margin + flow_chunk, flow_margin)],
        last,
        before,
        1,
    )
    for chunk in range(chunks):
        start, count, spot = window(chunk, chunks, fine_chunk, mark_margin)
        push(
            marks_turned.at[pl.ds(start, count)],
            marks_in.at[half, pl.ds(spot, count)],
            chunk,
            ring,
            2,
            group == chunk // halves,
        )
    push(
        marks_turned.at[pl.ds(fine_rows - mark_margin, mark_margin)],
        marks_in.at[half, pl.ds(0, mark_margin)],
        0,
        after,
        2,
        group == 0,
    )
    push(
        marks_turned.at[pl.ds(0, mark_margin)],
        marks_in.at[half, pl.ds(mark_margin + fine_chunk, mark_margin)],
        last,
        before,
        2,
        group == groups - 1,
    )

    body = fine_chunk + 2 * mark_margin
    offset = fine_margin - mark_margin
    edge = jnp.zeros((majors, offset, LANES), jnp.float32)
    for stage in (stage_one, stage_two):
        stage[:, pl.ds(0, offset)] = edge
        stage[:, pl.ds(offset + body, offset)] = edge

    pltpu.make_async_copy(flow_in, flow_in, take_sems.at[1]).wait()
    share = LANES // halves
    fields = []
    flow_lane = lanes_of((flow_chunk + 2 * flow_margin, LANES))
    for field in range(groups):
        merged = flow_in[field, 0]
        for part in range(1, halves):
            merged = jnp.where(flow_lane >= part * share, flow_in[field, part], merged)
        fields.append(merged)

    from_flow = lax.broadcasted_iota(jnp.int32, (LANES, majors * LANES), 0)
    to_fine = lanes_of((LANES, majors * LANES))
    fine_cell = (to_fine // LANES) * flow_z + (to_fine % fine_z) // 2
    spread_lanes = (from_flow == fine_cell).astype(jnp.float32)
    flow_window = flow_chunk + 2 * flow_margin
    spread_rows = (
        lanes_of((body, flow_window))
        == lax.broadcasted_iota(jnp.int32, (body, flow_window), 0) // 2
        + (flow_margin - mark_margin // 2)
    ).astype(jnp.float32)
    for direction in range(3):
        tall = jnp.dot(
            spread_rows, fields[direction], precision=EXACT, preferred_element_type=jnp.float32
        )
        wide = jnp.dot(tall, spread_lanes, precision=EXACT, preferred_element_type=jnp.float32)
        for major in range(majors):
            speeds[direction, major] = wide[:, major * LANES : (major + 1) * LANES]

    def flow_beside(block, direction, step):
        if direction == 0:
            return pltpu.roll(block, (-step * flow_z) % LANES, 1)
        if direction == 1:
            return along_rows(block, step)
        return along_z(block, step, flow_z)

    def flow_slope(block, direction):
        return 0.5 * (flow_beside(block, direction, 1) - flow_beside(block, direction, -1))

    moved = []
    for component in range(3):
        moving = fields[component]
        advect = fields[0] * flow_slope(moving, 0)
        advect = advect + fields[1] * flow_slope(moving, 1)
        advect = advect + fields[2] * flow_slope(moving, 2)
        source = moving - STEP_FLOW * (advect + flow_slope(fields[3], component))
        relaxed = source
        for sweep_number in range(SWEEPS):
            beside = jnp.zeros_like(relaxed)
            for direction in range(3):
                beside = beside + flow_beside(relaxed, direction, 1)
                beside = beside + flow_beside(relaxed, direction, -1)
            relaxed = (source + IMPLICIT * beside) * (1.0 / (1.0 + 6.0 * IMPLICIT))
        moved.append(relaxed[flow_margin : flow_margin + flow_chunk])

    pltpu.make_async_copy(level_in, level_in, take_sems.at[0]).wait()

    block_rows = 2 * ROWS

    def section(current, target, keep, blend):
        def one(major, carry):
            def far_major(step):
                return lax.rem(major + majors + step, majors)

            for start in range(0, body, block_rows):
                rows = pl.ds(offset + start, block_rows)
                tall = current[major, pl.ds(start, block_rows + 2 * offset)]
                middle = tall[offset : offset + block_rows]
                low_half = lanes_of(middle.shape) < fine_z
                whole = {step: current[far_major(step), rows] for step in (-2, -1, 1, 2)}
                whole[0] = middle
                swapped = {step: pltpu.roll(whole[step], fine_z, 1) for step in whole}

                def beside(direction, step):
                    if step == 0:
                        return middle
                    if direction == 1:
                        return tall[offset + step : offset + step + block_rows]
                    if direction == 2:
                        return along_z(middle, step, fine_z)
                    base = step // 2
                    if step % 2 == 0:
                        return whole[base]
                    return jnp.where(low_half, swapped[base], swapped[base + 1])

                rate = jnp.zeros_like(middle)
                for direction in range(3):
                    cells = [beside(direction, step) for step in range(-3, 4)]
                    diffs = [cells[i + 1] - cells[i] for i in range(6)]
                    speed = speeds[direction, major, pl.ds(start, block_rows)]
                    rate = rate - speed * weno_upwind(diffs, speed)
                moved_on = blend * (middle + STEP_FINE * rate)
                if keep:
                    moved_on = keep * level_in[major, rows] + moved_on
                target[major, rows] = moved_on
            return carry

        lax.fori_loop(0, majors, one, 0)

    section(level_in, stage_one, 0.0, 1.0)
    section(stage_one, stage_two, 0.75, 0.25)
    section(stage_two, stage_one, 1.0 / 3.0, 2.0 / 3.0)

    pltpu.make_async_copy(marks_in, marks_in, take_sems.at[2]).wait()
    mark_from = lax.broadcasted_iota(jnp.int32, (LANES, LANES), 0)
    mark_to = lanes_of((LANES, LANES))
    tile_z = plan["tile_z"]
    tile_count = fine_z // tile_z
    inside = pl.ds(offset, body)
    spread_band = (mark_from == (mark_to % fine_z) // tile_z).astype(jnp.float32)
    for part in range(halves):
        marks = marks_in[part]
        band = jnp.dot(marks, spread_band, preferred_element_type=jnp.float32)
        for pair in range(pairs):
            pick = jnp.logical_and(
                mark_from == tile_count + 2 * pair + mark_to // fine_z, mark_to % fine_z == 0
            ).astype(jnp.float32)
            phase = jnp.dot(marks, pick, preferred_element_type=jnp.float32)
            major = part * pairs + pair
            banded = jnp.where(band > 0.5, stage_one[major, inside], level_in[major, inside])
            shaped[major] = jnp.where(
                phase > 1.5, SPREAD, jnp.where(phase > 0.5, -SPREAD, banded)
            )

    low_half = lanes_of((body, LANES)) < fine_z

    def x_slope(ref, major):
        here = pltpu.roll(ref[major], fine_z, 1)
        up = pltpu.roll(ref[(major + 1) % majors], fine_z, 1)
        down = pltpu.roll(ref[(major + majors - 1) % majors], fine_z, 1)
        return 0.5 * (jnp.where(low_half, here, up) - jnp.where(low_half, down, here))

    for major in range(majors):
        level = shaped[major]
        slope_x = x_slope(shaped, major)
        slope_y = 0.5 * (along_rows(level, 1) - along_rows(level, -1))
        slope_z = 0.5 * (along_z(level, 1, fine_z) - along_z(level, -1, fine_z))
        inverse = lax.rsqrt(slope_x * slope_x + slope_y * slope_y + slope_z * slope_z + 1.0)
        normals[0, major] = slope_x * inverse
        normals[1, major] = slope_y * inverse
        normals[2, major] = slope_z * inverse

    core = slice(mark_margin, mark_margin + fine_chunk)
    for major in range(majors):
        normal_y, normal_z = normals[1, major], normals[2, major]
        curvature = x_slope(normals.at[0], major)
        curvature = curvature + 0.5 * (along_rows(normal_y, 1) - along_rows(normal_y, -1))
        curvature = curvature + 0.5 * (
            along_z(normal_z, 1, fine_z) - along_z(normal_z, -1, fine_z)
        )
        level = shaped[major]
        delta_peak = jnp.exp(level * level * (-1.0 / (2.0 * SPREAD * SPREAD)))
        strength = (SURFACE / (SPREAD * 2.5066282746310002)) * curvature * delta_peak
        lane_spot = slice(major * LANES, (major + 1) * LANES)
        for direction in range(3):
            force = (normals[direction, major] * strength)[core]
            packed[pl.ds(direction * fine_chunk, fine_chunk), lane_spot] = force
        fraction = (0.5 + 0.5 * jnp.tanh(level * (1.0 / SPREAD)))[core]
        packed[pl.ds(3 * fine_chunk, fine_chunk), lane_spot] = fraction

    fine_from = lax.broadcasted_iota(jnp.int32, (majors * LANES, LANES), 0)
    flow_to = lanes_of((majors * LANES, LANES))
    fold_lanes = (
        flow_to == (fine_from // LANES) * flow_z + (fine_from % fine_z) // 2
    ).astype(jnp.float32)
    folded = jnp.dot(
        packed[...], fold_lanes, precision=EXACT, preferred_element_type=jnp.float32
    )
    fold_shape = (4 * flow_chunk, 4 * fine_chunk)
    fold_rows = (
        lanes_of(fold_shape) // 2 == lax.broadcasted_iota(jnp.int32, fold_shape, 0)
    ).astype(jnp.float32)
    means = 0.125 * jnp.dot(
        fold_rows, folded, precision=EXACT, preferred_element_type=jnp.float32
    )
    for output in range(4):
        mean = means[output * flow_chunk : (output + 1) * flow_chunk]
        results[output] = moved[output] + STEP_FLOW * mean if output < 3 else mean

    landing = pl.ds(pl.multiple_of(mine * flow_chunk, flow_chunk), flow_chunk)
    for chunk in range(chunks):
        push(results.at[chunk // halves], gathered.at[landing], chunk, ring, 3)
    pltpu.make_async_copy(gathered, gathered, take_sems.at[3]).wait()
    turned = gathered[...].T
    outcome = turned[:share]
    for part in range(1, halves):
        outcome = jnp.where(half == part, turned[part * share : (part + 1) * share], outcome)
    out_ref[...] = outcome
    for condition, copy in sent:
        if condition is None:
            copy.wait_send()
        else:
            pl.when(condition)(copy.wait_send)


def on_device_bricks(plan, flow_fields, level_set, band_tiles, nozzle_phase):
    flow_z, flow_x, flow_y = flow_fields.shape[1:]
    fine_z, fine_x, fine_y = level_set.shape[1:]
    groups, halves = plan["groups"], plan["halves"]
    chunks = groups * halves
    fine_chunk, flow_chunk = fine_y // chunks, flow_y // chunks
    tiles_z = band_tiles.shape[0]
    plan = dict(
        plan,
        fine_chunk=fine_chunk,
        flow_chunk=flow_chunk,
        fine_z=fine_z,
        flow_z=flow_z,
        tile_z=fine_z // tiles_z,
    )
    flow = flow_fields[0].transpose(1, 0, 2).reshape(flow_x * flow_z, flow_y)
    level = level_set[0].transpose(1, 0, 2).reshape(fine_x // 2, 2 * fine_z, fine_y)
    band = jnp.repeat(band_tiles[:, 0, :], fine_y // band_tiles.shape[2], axis=1)
    marks = jnp.concatenate([band, nozzle_phase], axis=0).astype(jnp.float32)
    marks = jnp.pad(marks, ((0, LANES - marks.shape[0]), (0, 0)))
    majors = fine_x // 2 * halves
    body = fine_chunk + 2 * ROWS
    tall = fine_chunk + 4 * ROWS
    vmem = pl.BlockSpec(memory_space=pltpu.VMEM)

    def room(*shape):
        return pltpu.VMEM(shape, jnp.float32)

    copies = 4 * chunks + 6
    result = pl.pallas_call(
        functools.partial(brick_kernel, plan),
        out_shape=jax.ShapeDtypeStruct((flow_x * flow_z, flow_y), jnp.float32),
        in_specs=[vmem] * 3,
        out_specs=vmem,
        scratch_shapes=[
            room(flow_y, LANES),
            room(fine_x // 2, fine_y, LANES),
            room(fine_y, LANES),
            room(groups, halves, flow_chunk + 2 * ROWS, LANES),
            room(majors, tall, LANES),
            room(halves, body, LANES),
            room(3, majors, body, LANES),
            room(majors, tall, LANES),
            room(majors, tall, LANES),
            room(majors, body, LANES),
            room(3, majors, body, LANES),
            room(4 * fine_chunk, majors * LANES),
            room(4, flow_chunk, LANES),
            room(flow_y, LANES),
            pltpu.SemaphoreType.DMA((copies,)),
            pltpu.SemaphoreType.DMA((4,)),
        ],
        compiler_params=pltpu.CompilerParams(
            collective_id=0, has_side_effects=True, vmem_limit_bytes=32 * 1024 * 1024
        ),
        name="jet_step",
    )(flow, level, marks)
    return result.reshape(flow_x, flow_z, flow_y).transpose(1, 0, 2)[None]


def solution(mesh):
    placed = (
        P("grp", None, "gx", "gy"),
        P("grp", None, "gx", "gy"),
        P(None, "gx", "gy"),
        P("gx", "gy"),
    )
    plan = {"groups": mesh.shape["grp"], "halves": mesh.shape["gx"], "rings": mesh.shape["gy"]}

    def on_device(flow_fields, level_set, band_tiles, nozzle_phase):
        flow_z, flow_x, flow_y = flow_fields.shape[1:]
        chunks = plan["groups"] * plan["halves"]
        fits = (
            plan["halves"] * flow_x * flow_z == LANES
            and 2 * level_set.shape[1] == LANES
            and flow_y == LANES
            and flow_y % (chunks * 2 * ROWS) == 0
            and band_tiles.shape[1] == 1
            and plan["rings"] > 2
        )
        if fits:
            return on_device_bricks(plan, flow_fields, level_set, band_tiles, nozzle_phase)
        return on_device_general(flow_fields, level_set, band_tiles, nozzle_phase)

    return jax.shard_map(
        on_device, mesh=mesh, in_specs=placed, out_specs=P("grp", None, "gx", "gy"), check_vma=False
    )
```

```python
import functools

import jax
import jax.numpy as jnp
from jax import lax
from jax.experimental import pallas as pl
from jax.experimental.pallas import tpu as pltpu
from jax.sharding import PartitionSpec as P

SWEEPS = 3


WENO_EPS = 1e-06
STEP_FINE = 0.3
STEP_FLOW = 0.2
SURFACE = 6.0
SPREAD = 1.5
IMPLICIT = 0.5


def extended(block, sides, width):
    for axis, dim in sides:
        count = lax.axis_size(axis)
        forward = [(i, i + 1) for i in range(count - 1)]
        forward.append((count - 1, 0))
        backward = [(target, source) for source, target in forward]
        low = lax.ppermute(
            lax.slice_in_dim(block, block.shape[dim] - width, None, axis=dim), axis, forward
        )
        high = lax.ppermute(lax.slice_in_dim(block, 0, width, axis=dim), axis, backward)
        block = jnp.concatenate([low, block, high], axis=dim)
    return block


def weno_side(diff_one, diff_two, diff_three, diff_four, diff_five):
    cand_one = diff_one / 3.0 - 7.0 * diff_two / 6.0 + 11.0 * diff_three / 6.0
    cand_two = -diff_two / 6.0 + 5.0 * diff_three / 6.0 + diff_four / 3.0
    cand_three = diff_three / 3.0 + 5.0 * diff_four / 6.0 - diff_five / 6.0
    curve_one = diff_one - 2.0 * diff_two + diff_three
    slope_one = diff_one - 4.0 * diff_two + 3.0 * diff_three
    smooth_one = 13.0 / 12.0 * curve_one * curve_one + 0.25 * slope_one * slope_one
    curve_two = diff_two - 2.0 * diff_three + diff_four
    slope_two = diff_two - diff_four
    smooth_two = 13.0 / 12.0 * curve_two * curve_two + 0.25 * slope_two * slope_two
    curve_three = diff_three - 2.0 * diff_four + diff_five
    slope_three = 3.0 * diff_three - 4.0 * diff_four + diff_five
    smooth_three = 13.0 / 12.0 * curve_three * curve_three + 0.25 * slope_three * slope_three
    weight_one = 0.1 / ((WENO_EPS + smooth_one) * (WENO_EPS + smooth_one))
    weight_two = 0.6 / ((WENO_EPS + smooth_two) * (WENO_EPS + smooth_two))
    weight_three = 0.3 / ((WENO_EPS + smooth_three) * (WENO_EPS + smooth_three))
    return (weight_one * cand_one + weight_two * cand_two + weight_three * cand_three) / (
        weight_one + weight_two + weight_three
    )


def section_rate(padded, speeds, plane_rim):
    plane_count = padded.shape[0] - 2 * plane_rim
    row_count = padded.shape[1] - 6
    col_count = padded.shape[2] - 6

    def sample(offset, direction):
        if direction == 0:
            return padded[
                3 + offset : 3 + offset + plane_count, 3 : 3 + row_count, 3 : 3 + col_count
            ]
        if direction == 1:
            return padded[
                plane_rim : plane_rim + plane_count,
                3 + offset : 3 + offset + row_count,
                3 : 3 + col_count,
            ]
        return padded[
            plane_rim : plane_rim + plane_count,
            3 : 3 + row_count,
            3 + offset : 3 + offset + col_count,
        ]

    summed = jnp.zeros((plane_count, row_count, col_count), jnp.float32)
    for direction in range(3):
        differences = [
            sample(offset + 1, direction) - sample(offset, direction) for offset in range(-3, 3)
        ]
        minus_side = weno_side(
            differences[0], differences[1], differences[2], differences[3], differences[4]
        )
        plus_side = weno_side(
            differences[5], differences[4], differences[3], differences[2], differences[1]
        )
        upwind = jnp.where(speeds[direction] >= 0.0, minus_side, plus_side)
        summed = summed - speeds[direction] * upwind
    return summed


def refine(coarse):
    plane_count, height, breadth = coarse.shape
    spread_out = jnp.broadcast_to(
        coarse[:, None, :, None, :, None], (plane_count, 2, height, 2, breadth, 2)
    )
    return spread_out.reshape(2 * plane_count, 2 * height, 2 * breadth)


def coarsen(fine_field):
    plane_count, height, breadth = fine_field.shape
    blocks = fine_field.reshape(plane_count // 2, 2, height // 2, 2, breadth // 2, 2)
    return jnp.sum(blocks, axis=(1, 3, 5)) * 0.125


def band_cells(tile_flags):
    planes, height, breadth = tile_flags.shape
    spread_out = jnp.broadcast_to(
        tile_flags[:, None, :, None, :, None], (planes, 8, height, 4, breadth, 16)
    )
    return spread_out.reshape(planes * 8, height * 4, breadth * 16)


def with_nozzle(banded, phases):
    inflow = jnp.where(phases == 2, 1.5, jnp.where(phases == 1, -1.5, banded[0]))
    return jnp.concatenate([inflow[None], banded[1:]], axis=0)


def surface_finish(normal_x, normal_y, normal_z, curvature, surface_level):
    delta_peak = jnp.exp(-surface_level * surface_level / (2.0 * SPREAD * SPREAD)) / (
        SPREAD * 2.5066282746310002
    )
    strength = SURFACE * curvature * delta_peak
    fraction = 0.5 + 0.5 * jnp.tanh(surface_level / SPREAD)
    return jnp.stack(
        [
            coarsen(normal_x * strength),
            coarsen(normal_y * strength),
            coarsen(normal_z * strength),
            coarsen(fraction),
        ]
    )


def surface_slab(padded):
    grad_x = (padded[1:-1, 2:, 1:-1] - padded[1:-1, :-2, 1:-1]) * 0.5
    grad_y = (padded[1:-1, 1:-1, 2:] - padded[1:-1, 1:-1, :-2]) * 0.5
    grad_z = (padded[2:, 1:-1, 1:-1] - padded[:-2, 1:-1, 1:-1]) * 0.5
    inverse = 1.0 / jnp.sqrt(grad_x * grad_x + grad_y * grad_y + grad_z * grad_z + 1.0)
    normal_x = grad_x * inverse
    normal_y = grad_y * inverse
    normal_z = grad_z * inverse
    curvature = (normal_x[1:-1, 2:, 1:-1] - normal_x[1:-1, :-2, 1:-1]) * 0.5
    curvature = curvature + (normal_y[1:-1, 1:-1, 2:] - normal_y[1:-1, 1:-1, :-2]) * 0.5
    curvature = curvature + (normal_z[2:, 1:-1, 1:-1] - normal_z[:-2, 1:-1, 1:-1]) * 0.5
    return surface_finish(
        normal_x[1:-1, 1:-1, 1:-1],
        normal_y[1:-1, 1:-1, 1:-1],
        normal_z[1:-1, 1:-1, 1:-1],
        curvature,
        padded[2:-2, 2:-2, 2:-2],
    )


def centered(padded, direction):
    if direction == 0:
        middle = padded[:, 1:-1, 1:-1]
        return (jnp.roll(middle, -1, 0) - jnp.roll(middle, 1, 0)) * 0.5
    if direction == 1:
        return (padded[:, 2:, 1:-1] - padded[:, :-2, 1:-1]) * 0.5
    return (padded[:, 1:-1, 2:] - padded[:, 1:-1, :-2]) * 0.5


def predictor(padded_fields, component):
    moving = lax.dynamic_index_in_dim(padded_fields, component, 0, keepdims=False)
    inner_u = padded_fields[0, :, 1:-1, 1:-1]
    inner_v = padded_fields[1, :, 1:-1, 1:-1]
    inner_w = padded_fields[2, :, 1:-1, 1:-1]
    advect = -(
        inner_w * centered(moving, 0)
        + inner_u * centered(moving, 1)
        + inner_v * centered(moving, 2)
    )
    pressure = padded_fields[3]
    gradients = jnp.stack([centered(pressure, 1), centered(pressure, 2), centered(pressure, 0)])
    pushed = lax.dynamic_index_in_dim(gradients, component, 0, keepdims=False)
    return moving[:, 1:-1, 1:-1] + STEP_FLOW * (advect - pushed)


def sweep_once(padded, source):
    middle = padded[:, 1:-1, 1:-1]
    beside_all = (
        padded[:, 2:, 1:-1] + padded[:, :-2, 1:-1] + padded[:, 1:-1, 2:] + padded[:, 1:-1, :-2]
    )
    beside_all = beside_all + jnp.roll(middle, -1, 0) + jnp.roll(middle, 1, 0)
    return (source + IMPLICIT * beside_all) / (1.0 + 6.0 * IMPLICIT)


def spread_surface(level_set, band_tiles, nozzle_phase, inner_fields, is_level, group):
    fine_all = level_set[0]
    initial = lax.psum_scatter(
        jnp.where(is_level, fine_all, jnp.zeros_like(fine_all)),
        "grp",
        scatter_dimension=0,
        tiled=True,
    )
    coarse_planes = inner_fields.shape[1] // 4
    flow_slab = lax.dynamic_slice_in_dim(inner_fields, group * coarse_planes, coarse_planes, 1)
    speeds = (refine(flow_slab[2]), refine(flow_slab[0]), refine(flow_slab[1]))

    def run_section(current, keep_weight, blend_weight):
        padded = extended(current, (("grp", 0), ("gx", 1), ("gy", 2)), 3)
        return keep_weight * initial + blend_weight * (
            current + STEP_FINE * section_rate(padded, speeds, 3)
        )

    first_section = run_section(initial, 0.0, 1.0)
    second_section = run_section(first_section, 0.75, 0.25)
    third_section = run_section(second_section, 1.0 / 3.0, 2.0 / 3.0)
    tile_planes = band_tiles.shape[0] // 4
    tiles_here = lax.dynamic_slice_in_dim(band_tiles, group * tile_planes, tile_planes, 0)
    banded = jnp.where(band_cells(tiles_here) == 1, third_section, initial)
    shaped = jnp.where(group == 0, with_nozzle(banded, nozzle_phase), banded)
    surface_pad = extended(shaped, (("grp", 0), ("gx", 1), ("gy", 2)), 2)
    quarter = surface_slab(surface_pad)
    received = lax.all_to_all(quarter, "grp", split_axis=0, concat_axis=1, tiled=True)
    return (received, received[0])


def on_device_general(flow_fields, level_set, band_tiles, nozzle_phase):
    group = lax.axis_index("grp")
    component = jnp.minimum(group, 2)
    is_level = group == 3
    gathered = lax.all_gather(flow_fields, "grp", axis=0, tiled=True)
    padded_fields = extended(gathered, (("gx", 2), ("gy", 3)), 1)
    source = predictor(padded_fields, component)
    inner_fields = padded_fields[:, :, 1:-1, 1:-1]
    received, fraction = spread_surface(
        level_set, band_tiles, nozzle_phase, inner_fields, is_level, group
    )
    pushed = received[0]
    relaxed = source
    for sweep_number in range(SWEEPS):
        padded = extended(relaxed, (("gx", 1), ("gy", 2)), 1)
        relaxed = sweep_once(padded, source)
    updated = relaxed + STEP_FLOW * pushed
    result = jnp.where(is_level, fraction, updated)
    return result[None]


MESH = pl.DeviceIdType.MESH
LANES = 128
ROWS = 8
EXACT = lax.Precision.HIGHEST


def lanes_of(shape, dim=1):
    return lax.broadcasted_iota(jnp.int32, shape, dim)


def along_z(block, offset, period):
    spot = lanes_of(block.shape) % period
    plain = pltpu.roll(block, (-offset) % LANES, 1)
    if offset > 0:
        around = pltpu.roll(block, (period - offset) % LANES, 1)
        return jnp.where(spot < period - offset, plain, around)
    around = pltpu.roll(block, (-period - offset) % LANES, 1)
    return jnp.where(spot >= -offset, plain, around)


def along_rows(block, offset):
    return pltpu.roll(block, (-offset) % block.shape[0], 0)


def weno_upwind(diffs, speed):
    forward = speed >= 0.0
    one = jnp.where(forward, diffs[0], diffs[5])
    two = jnp.where(forward, diffs[1], diffs[4])
    three = jnp.where(forward, diffs[2], diffs[3])
    four = jnp.where(forward, diffs[3], diffs[2])
    five = jnp.where(forward, diffs[4], diffs[1])
    step_a = two - one
    step_b = three - two
    step_c = four - three
    step_d = five - four

    def weight(curve, slope):
        rough = (WENO_EPS * 12.0 / 13.0) + curve * curve + (3.0 / 13.0) * (slope * slope)
        inverse = 1.0 / rough
        return inverse * inverse

    weight_one = weight(step_b - step_a, 3.0 * step_b - step_a)
    weight_two = 6.0 * weight(step_c - step_b, step_c + step_b)
    weight_three = 3.0 * weight(step_d - step_c, 3.0 * step_c - step_d)
    mixed = (
        weight_one * (5.0 * step_b - 2.0 * step_a)
        + weight_two * (step_b + 2.0 * step_c)
        + weight_three * (4.0 * step_c - step_d)
    )
    total = weight_one + weight_two + weight_three
    return three + mixed / (6.0 * total)


def window(index, count, chunk, margin):
    low = index * chunk - margin
    high = (index + 1) * chunk + margin
    start, stop = max(low, 0), min(high, count * chunk)
    return start, stop - start, start - low


def brick_kernel(
    plan,
    flow_ref,
    level_ref,
    band_ref,
    phase_ref,
    out_ref,
    flow_turned,
    level_turned,
    marks_turned,
    flow_in,
    level_in,
    marks_in,
    speeds,
    stage_one,
    stage_two,
    shaped,
    normals,
    packed,
    results,
    gathered,
    send_sems,
    take_sems,
):
    groups, halves, rings = plan["groups"], plan["halves"], plan["rings"]
    chunks = groups * halves
    fine_chunk, flow_chunk = plan["fine_chunk"], plan["flow_chunk"]
    fine_z, flow_z = plan["fine_z"], plan["flow_z"]
    fine_margin, mark_margin, flow_margin = 2 * ROWS, ROWS, ROWS
    fine_rows, flow_rows = chunks * fine_chunk, chunks * flow_chunk
    pairs = level_ref.shape[1] // 2
    majors = pairs * halves
    group = lax.axis_index("grp")
    half = lax.axis_index("gx")
    ring = lax.axis_index("gy")
    after = lax.rem(ring + 1, rings)
    before = lax.rem(ring + rings - 1, rings)
    mine = group * halves + half
    last = chunks - 1

    barrier = pltpu.get_barrier_semaphore()

    def greet(target_group, target_half, target_ring):
        pl.semaphore_signal(
            barrier,
            inc=1,
            device_id=(target_group, target_half, target_ring),
            device_id_type=MESH,
        )

    for chunk in range(chunks):
        tg, th = chunk // halves, chunk % halves

        @pl.when(mine != chunk)
        def _(tg=tg, th=th):
            greet(tg, th, ring)

        @pl.when(mine == 0)
        def _(tg=tg, th=th):
            greet(tg, th, before)

        @pl.when(mine == last)
        def _(tg=tg, th=th):
            greet(tg, th, after)

    @pl.when(group == groups - 1)
    def _():
        for pair in range(pairs):
            both = [level_ref[:, 2 * pair], level_ref[:, 2 * pair + 1]]
            level_turned[pair] = jnp.concatenate(both, axis=0).T

    columns = [flow_ref[:, column] for column in range(flow_ref.shape[1])]
    flow_turned[...] = jnp.concatenate(columns * halves, axis=0).T
    tiles_z, tiles_y = band_ref.shape
    wide_shape = (tiles_y, fine_rows)
    widen = (
        lanes_of(wide_shape) // (fine_rows // tiles_y)
        == lax.broadcasted_iota(jnp.int32, wide_shape, 0)
    ).astype(jnp.float32)
    wide_band = jnp.dot(
        band_ref[...].astype(jnp.float32), widen, preferred_element_type=jnp.float32
    )
    spare = LANES - tiles_z - phase_ref.shape[0]
    marks_turned[...] = jnp.concatenate(
        [
            wide_band,
            phase_ref[...].astype(jnp.float32),
            jnp.zeros((spare, fine_rows), jnp.float32),
        ],
        axis=0,
    ).T

    pl.semaphore_wait(barrier, chunks + 1)

    sent = []

    def push(source, target, chunk, ring_to, take, condition=None):
        tg, th = chunk // halves, chunk % halves
        slot = len(sent)
        remote = pltpu.make_async_remote_copy(
            src_ref=source,
            dst_ref=target,
            send_sem=send_sems.at[slot],
            recv_sem=take_sems.at[take],
            device_id=(tg, th, ring_to),
            device_id_type=MESH,
        )
        near = ring_to is ring
        far = mine != chunk if near else None
        if condition is not None:
            far = condition if far is None else jnp.logical_and(condition, far)
        if near:
            here = mine == chunk
            if condition is not None:
                here = jnp.logical_and(condition, here)

            @pl.when(here)
            def _():
                pltpu.make_async_copy(source, target, take_sems.at[take]).start()

        if far is None:
            remote.start()
        else:
            pl.when(far)(remote.start)
        sent.append((far, remote))

    holder = group == groups - 1
    major_spot = pl.ds(half * pairs, pairs)
    for chunk in range(chunks):
        start, count, spot = window(chunk, chunks, fine_chunk, fine_margin)
        push(
            level_turned.at[:, pl.ds(start, count)],
            level_in.at[major_spot, pl.ds(spot, count)],
            chunk,
            ring,
            0,
            holder,
        )
    push(
        level_turned.at[:, pl.ds(fine_rows - fine_margin, fine_margin)],
        level_in.at[major_spot, pl.ds(0, fine_margin)],
        0,
        after,
        0,
        holder,
    )
    push(
        level_turned.at[:, pl.ds(0, fine_margin)],
        level_in.at[major_spot, pl.ds(fine_margin + fine_chunk, fine_margin)],
        last,
        before,
        0,
        holder,
    )
    for chunk in range(chunks):
        start, count, spot = window(chunk, chunks, flow_chunk, flow_margin)
        push(
            flow_turned.at[pl.ds(start, count)],
            flow_in.at[group, half, pl.ds(spot, count)],
            chunk,
            ring,
            1,
        )
    push(
        flow_turned.at[pl.ds(flow_rows - flow_margin, flow_margin)],
        flow_in.at[group, half, pl.ds(0, flow_margin)],
        0,
        after,
        1,
    )
    push(
        flow_turned.at[pl.ds(0, flow_margin)],
        flow_in.at[group, half, pl.ds(flow_margin + flow_chunk, flow_margin)],
        last,
        before,
        1,
    )
    for chunk in range(chunks):
        start, count, spot = window(chunk, chunks, fine_chunk, mark_margin)
        push(
            marks_turned.at[pl.ds(start, count)],
            marks_in.at[half, pl.ds(spot, count)],
            chunk,
            ring,
            2,
            group == chunk // halves,
        )
    push(
        marks_turned.at[pl.ds(fine_rows - mark_margin, mark_margin)],
        marks_in.at[half, pl.ds(0, mark_margin)],
        0,
        after,
        2,
        group == 0,
    )
    push(
        marks_turned.at[pl.ds(0, mark_margin)],
        marks_in.at[half, pl.ds(mark_margin + fine_chunk, mark_margin)],
        last,
        before,
        2,
        group == groups - 1,
    )

    body = fine_chunk + 2 * mark_margin
    offset = fine_margin - mark_margin
    edge = jnp.zeros((majors, offset, LANES), jnp.float32)
    for stage in (stage_one, stage_two):
        stage[:, pl.ds(0, offset)] = edge
        stage[:, pl.ds(offset + body, offset)] = edge

    pltpu.make_async_copy(flow_in, flow_in, take_sems.at[1]).wait()
    share = LANES // halves
    fields = []
    flow_lane = lanes_of((flow_chunk + 2 * flow_margin, LANES))
    for field in range(groups):
        merged = flow_in[field, 0]
        for part in range(1, halves):
            merged = jnp.where(flow_lane >= part * share, flow_in[field, part], merged)
        fields.append(merged)

    from_flow = lax.broadcasted_iota(jnp.int32, (LANES, majors * LANES), 0)
    to_fine = lanes_of((LANES, majors * LANES))
    fine_cell = (to_fine // LANES) * flow_z + (to_fine % fine_z) // 2
    spread_lanes = (from_flow == fine_cell).astype(jnp.float32)
    flow_window = flow_chunk + 2 * flow_margin
    spread_rows = (
        lanes_of((body, flow_window))
        == lax.broadcasted_iota(jnp.int32, (body, flow_window), 0) // 2
        + (flow_margin - mark_margin // 2)
    ).astype(jnp.float32)
    for direction in range(3):
        tall = jnp.dot(
            spread_rows, fields[direction], precision=EXACT, preferred_element_type=jnp.float32
        )
        wide = jnp.dot(tall, spread_lanes, precision=EXACT, preferred_element_type=jnp.float32)
        for major in range(majors):
            speeds[direction, major] = wide[:, major * LANES : (major + 1) * LANES]

    def flow_beside(block, direction, step):
        if direction == 0:
            return pltpu.roll(block, (-step * flow_z) % LANES, 1)
        if direction == 1:
            return along_rows(block, step)
        return along_z(block, step, flow_z)

    def flow_slope(block, direction):
        return 0.5 * (flow_beside(block, direction, 1) - flow_beside(block, direction, -1))

    moved = []
    for component in range(3):
        moving = fields[component]
        advect = fields[0] * flow_slope(moving, 0)
        advect = advect + fields[1] * flow_slope(moving, 1)
        advect = advect + fields[2] * flow_slope(moving, 2)
        source = moving - STEP_FLOW * (advect + flow_slope(fields[3], component))
        relaxed = source
        for sweep_number in range(SWEEPS):
            beside = jnp.zeros_like(relaxed)
            for direction in range(3):
                beside = beside + flow_beside(relaxed, direction, 1)
                beside = beside + flow_beside(relaxed, direction, -1)
            relaxed = (source + IMPLICIT * beside) * (1.0 / (1.0 + 6.0 * IMPLICIT))
        moved.append(relaxed[flow_margin : flow_margin + flow_chunk])

    pltpu.make_async_copy(level_in, level_in, take_sems.at[0]).wait()

    block_rows = 2 * ROWS

    def section(current, target, keep, blend):
        def one(major, carry):
            def far_major(step):
                return lax.rem(major + majors + step, majors)

            for start in range(0, body, block_rows):
                rows = pl.ds(offset + start, block_rows)
                tall = current[major, pl.ds(start, block_rows + 2 * offset)]
                middle = tall[offset : offset + block_rows]
                low_half = lanes_of(middle.shape) < fine_z
                whole = {step: current[far_major(step), rows] for step in (-2, -1, 1, 2)}
                whole[0] = middle
                swapped = {step: pltpu.roll(whole[step], fine_z, 1) for step in whole}

                def beside(direction, step):
                    if step == 0:
                        return middle
                    if direction == 1:
                        return tall[offset + step : offset + step + block_rows]
                    if direction == 2:
                        return along_z(middle, step, fine_z)
                    base = step // 2
                    if step % 2 == 0:
                        return whole[base]
                    return jnp.where(low_half, swapped[base], swapped[base + 1])

                rate = jnp.zeros_like(middle)
                for direction in range(3):
                    cells = [beside(direction, step) for step in range(-3, 4)]
                    diffs = [cells[i + 1] - cells[i] for i in range(6)]
                    speed = speeds[direction, major, pl.ds(start, block_rows)]
                    rate = rate - speed * weno_upwind(diffs, speed)
                moved_on = blend * (middle + STEP_FINE * rate)
                if keep:
                    moved_on = keep * level_in[major, rows] + moved_on
                target[major, rows] = moved_on
            return carry

        lax.fori_loop(0, majors, one, 0)

    section(level_in, stage_one, 0.0, 1.0)
    section(stage_one, stage_two, 0.75, 0.25)
    section(stage_two, stage_one, 1.0 / 3.0, 2.0 / 3.0)

    pltpu.make_async_copy(marks_in, marks_in, take_sems.at[2]).wait()
    mark_from = lax.broadcasted_iota(jnp.int32, (LANES, LANES), 0)
    mark_to = lanes_of((LANES, LANES))
    tile_z = plan["tile_z"]
    tile_count = fine_z // tile_z
    inside = pl.ds(offset, body)
    spread_band = (mark_from == (mark_to % fine_z) // tile_z).astype(jnp.float32)
    for part in range(halves):
        marks = marks_in[part]
        band = jnp.dot(marks, spread_band, preferred_element_type=jnp.float32)
        for pair in range(pairs):
            pick = jnp.logical_and(
                mark_from == tile_count + 2 * pair + mark_to // fine_z, mark_to % fine_z == 0
            ).astype(jnp.float32)
            phase = jnp.dot(marks, pick, preferred_element_type=jnp.float32)
            major = part * pairs + pair
            banded = jnp.where(band > 0.5, stage_one[major, inside], level_in[major, inside])
            shaped[major] = jnp.where(
                phase > 1.5, SPREAD, jnp.where(phase > 0.5, -SPREAD, banded)
            )

    low_half = lanes_of((body, LANES)) < fine_z

    def x_slope(ref, major):
        here = pltpu.roll(ref[major], fine_z, 1)
        up = pltpu.roll(ref[(major + 1) % majors], fine_z, 1)
        down = pltpu.roll(ref[(major + majors - 1) % majors], fine_z, 1)
        return 0.5 * (jnp.where(low_half, here, up) - jnp.where(low_half, down, here))

    for major in range(majors):
        level = shaped[major]
        slope_x = x_slope(shaped, major)
        slope_y = 0.5 * (along_rows(level, 1) - along_rows(level, -1))
        slope_z = 0.5 * (along_z(level, 1, fine_z) - along_z(level, -1, fine_z))
        inverse = lax.rsqrt(slope_x * slope_x + slope_y * slope_y + slope_z * slope_z + 1.0)
        normals[0, major] = slope_x * inverse
        normals[1, major] = slope_y * inverse
        normals[2, major] = slope_z * inverse

    core = slice(mark_margin, mark_margin + fine_chunk)
    for major in range(majors):
        normal_y, normal_z = normals[1, major], normals[2, major]
        curvature = x_slope(normals.at[0], major)
        curvature = curvature + 0.5 * (along_rows(normal_y, 1) - along_rows(normal_y, -1))
        curvature = curvature + 0.5 * (
            along_z(normal_z, 1, fine_z) - along_z(normal_z, -1, fine_z)
        )
        level = shaped[major]
        delta_peak = jnp.exp(level * level * (-1.0 / (2.0 * SPREAD * SPREAD)))
        strength = (SURFACE / (SPREAD * 2.5066282746310002)) * curvature * delta_peak
        lane_spot = slice(major * LANES, (major + 1) * LANES)
        for direction in range(3):
            force = (normals[direction, major] * strength)[core]
            packed[pl.ds(direction * fine_chunk, fine_chunk), lane_spot] = force
        fraction = (0.5 + 0.5 * jnp.tanh(level * (1.0 / SPREAD)))[core]
        packed[pl.ds(3 * fine_chunk, fine_chunk), lane_spot] = fraction

    fine_from = lax.broadcasted_iota(jnp.int32, (majors * LANES, LANES), 0)
    flow_to = lanes_of((majors * LANES, LANES))
    fold_lanes = (
        flow_to == (fine_from // LANES) * flow_z + (fine_from % fine_z) // 2
    ).astype(jnp.float32)
    folded = jnp.dot(
        packed[...], fold_lanes, precision=EXACT, preferred_element_type=jnp.float32
    )
    fold_shape = (4 * flow_chunk, 4 * fine_chunk)
    fold_rows = (
        lanes_of(fold_shape) // 2 == lax.broadcasted_iota(jnp.int32, fold_shape, 0)
    ).astype(jnp.float32)
    means = 0.125 * jnp.dot(
        fold_rows, folded, precision=EXACT, preferred_element_type=jnp.float32
    )
    for output in range(4):
        mean = means[output * flow_chunk : (output + 1) * flow_chunk]
        results[output] = moved[output] + STEP_FLOW * mean if output < 3 else mean

    landing = pl.ds(pl.multiple_of(mine * flow_chunk, flow_chunk), flow_chunk)
    for chunk in range(chunks):
        push(results.at[chunk // halves], gathered.at[landing], chunk, ring, 3)
    pltpu.make_async_copy(gathered, gathered, take_sems.at[3]).wait()
    turned = gathered[...].T
    outcome = turned[:share]
    for part in range(1, halves):
        outcome = jnp.where(half == part, turned[part * share : (part + 1) * share], outcome)
    out_ref[...] = outcome
    for condition, copy in sent:
        if condition is None:
            copy.wait_send()
        else:
            pl.when(condition)(copy.wait_send)


def on_device_bricks(plan, flow_fields, level_set, band_tiles, nozzle_phase):
    flow_z, flow_x, flow_y = flow_fields.shape[1:]
    fine_z, fine_x, fine_y = level_set.shape[1:]
    groups, halves = plan["groups"], plan["halves"]
    chunks = groups * halves
    fine_chunk, flow_chunk = fine_y // chunks, flow_y // chunks
    tiles_z = band_tiles.shape[0]
    plan = dict(
        plan,
        fine_chunk=fine_chunk,
        flow_chunk=flow_chunk,
        fine_z=fine_z,
        flow_z=flow_z,
        tile_z=fine_z // tiles_z,
    )
    majors = fine_x // 2 * halves
    body = fine_chunk + 2 * ROWS
    tall = fine_chunk + 4 * ROWS
    vmem = pl.BlockSpec(memory_space=pltpu.VMEM)

    def room(*shape):
        return pltpu.VMEM(shape, jnp.float32)

    copies = 4 * chunks + 6
    result = pl.pallas_call(
        functools.partial(brick_kernel, plan),
        out_shape=jax.ShapeDtypeStruct((flow_x * flow_z, flow_y), jnp.float32),
        in_specs=[vmem] * 4,
        out_specs=vmem,
        scratch_shapes=[
            room(flow_y, LANES),
            room(fine_x // 2, fine_y, LANES),
            room(fine_y, LANES),
            room(groups, halves, flow_chunk + 2 * ROWS, LANES),
            room(majors, tall, LANES),
            room(halves, body, LANES),
            room(3, majors, body, LANES),
            room(majors, tall, LANES),
            room(majors, tall, LANES),
            room(majors, body, LANES),
            room(3, majors, body, LANES),
            room(4 * fine_chunk, majors * LANES),
            room(4, flow_chunk, LANES),
            room(flow_y, LANES),
            pltpu.SemaphoreType.DMA((copies,)),
            pltpu.SemaphoreType.DMA((4,)),
        ],
        compiler_params=pltpu.CompilerParams(
            collective_id=0, has_side_effects=True, vmem_limit_bytes=32 * 1024 * 1024
        ),
        name="jet_step",
    )(flow_fields[0], level_set[0], band_tiles[:, 0], nozzle_phase)
    return result.reshape(flow_x, flow_z, flow_y).transpose(1, 0, 2)[None]


def solution(mesh):
    placed = (
        P("grp", None, "gx", "gy"),
        P("grp", None, "gx", "gy"),
        P(None, "gx", "gy"),
        P("gx", "gy"),
    )
    plan = {"groups": mesh.shape["grp"], "halves": mesh.shape["gx"], "rings": mesh.shape["gy"]}

    def on_device(flow_fields, level_set, band_tiles, nozzle_phase):
        flow_z, flow_x, flow_y = flow_fields.shape[1:]
        chunks = plan["groups"] * plan["halves"]
        fits = (
            plan["halves"] * flow_x * flow_z == LANES
            and 2 * level_set.shape[1] == LANES
            and flow_y == LANES
            and flow_y % (chunks * 2 * ROWS) == 0
            and band_tiles.shape[1] == 1
            and plan["rings"] > 2
        )
        if fits:
            return on_device_bricks(plan, flow_fields, level_set, band_tiles, nozzle_phase)
        return on_device_general(flow_fields, level_set, band_tiles, nozzle_phase)

    return jax.shard_map(
        on_device, mesh=mesh, in_specs=placed, out_specs=P("grp", None, "gx", "gy"), check_vma=False
    )
```

```python
import functools

import jax
import jax.numpy as jnp
from jax import lax
from jax.experimental import pallas as pl
from jax.experimental.pallas import tpu as pltpu
from jax.sharding import PartitionSpec as P

SWEEPS = 3


WENO_EPS = 1e-06
STEP_FINE = 0.3
STEP_FLOW = 0.2
SURFACE = 6.0
SPREAD = 1.5
IMPLICIT = 0.5


def extended(block, sides, width):
    for axis, dim in sides:
        count = lax.axis_size(axis)
        forward = [(i, i + 1) for i in range(count - 1)]
        forward.append((count - 1, 0))
        backward = [(target, source) for source, target in forward]
        low = lax.ppermute(
            lax.slice_in_dim(block, block.shape[dim] - width, None, axis=dim), axis, forward
        )
        high = lax.ppermute(lax.slice_in_dim(block, 0, width, axis=dim), axis, backward)
        block = jnp.concatenate([low, block, high], axis=dim)
    return block


def weno_side(diff_one, diff_two, diff_three, diff_four, diff_five):
    cand_one = diff_one / 3.0 - 7.0 * diff_two / 6.0 + 11.0 * diff_three / 6.0
    cand_two = -diff_two / 6.0 + 5.0 * diff_three / 6.0 + diff_four / 3.0
    cand_three = diff_three / 3.0 + 5.0 * diff_four / 6.0 - diff_five / 6.0
    curve_one = diff_one - 2.0 * diff_two + diff_three
    slope_one = diff_one - 4.0 * diff_two + 3.0 * diff_three
    smooth_one = 13.0 / 12.0 * curve_one * curve_one + 0.25 * slope_one * slope_one
    curve_two = diff_two - 2.0 * diff_three + diff_four
    slope_two = diff_two - diff_four
    smooth_two = 13.0 / 12.0 * curve_two * curve_two + 0.25 * slope_two * slope_two
    curve_three = diff_three - 2.0 * diff_four + diff_five
    slope_three = 3.0 * diff_three - 4.0 * diff_four + diff_five
    smooth_three = 13.0 / 12.0 * curve_three * curve_three + 0.25 * slope_three * slope_three
    weight_one = 0.1 / ((WENO_EPS + smooth_one) * (WENO_EPS + smooth_one))
    weight_two = 0.6 / ((WENO_EPS + smooth_two) * (WENO_EPS + smooth_two))
    weight_three = 0.3 / ((WENO_EPS + smooth_three) * (WENO_EPS + smooth_three))
    return (weight_one * cand_one + weight_two * cand_two + weight_three * cand_three) / (
        weight_one + weight_two + weight_three
    )


def section_rate(padded, speeds, plane_rim):
    plane_count = padded.shape[0] - 2 * plane_rim
    row_count = padded.shape[1] - 6
    col_count = padded.shape[2] - 6

    def sample(offset, direction):
        if direction == 0:
            return padded[
                3 + offset : 3 + offset + plane_count, 3 : 3 + row_count, 3 : 3 + col_count
            ]
        if direction == 1:
            return padded[
                plane_rim : plane_rim + plane_count,
                3 + offset : 3 + offset + row_count,
                3 : 3 + col_count,
            ]
        return padded[
            plane_rim : plane_rim + plane_count,
            3 : 3 + row_count,
            3 + offset : 3 + offset + col_count,
        ]

    summed = jnp.zeros((plane_count, row_count, col_count), jnp.float32)
    for direction in range(3):
        differences = [
            sample(offset + 1, direction) - sample(offset, direction) for offset in range(-3, 3)
        ]
        minus_side = weno_side(
            differences[0], differences[1], differences[2], differences[3], differences[4]
        )
        plus_side = weno_side(
            differences[5], differences[4], differences[3], differences[2], differences[1]
        )
        upwind = jnp.where(speeds[direction] >= 0.0, minus_side, plus_side)
        summed = summed - speeds[direction] * upwind
    return summed


def refine(coarse):
    plane_count, height, breadth = coarse.shape
    spread_out = jnp.broadcast_to(
        coarse[:, None, :, None, :, None], (plane_count, 2, height, 2, breadth, 2)
    )
    return spread_out.reshape(2 * plane_count, 2 * height, 2 * breadth)


def coarsen(fine_field):
    plane_count, height, breadth = fine_field.shape
    blocks = fine_field.reshape(plane_count // 2, 2, height // 2, 2, breadth // 2, 2)
    return jnp.sum(blocks, axis=(1, 3, 5)) * 0.125


def band_cells(tile_flags):
    planes, height, breadth = tile_flags.shape
    spread_out = jnp.broadcast_to(
        tile_flags[:, None, :, None, :, None], (planes, 8, height, 4, breadth, 16)
    )
    return spread_out.reshape(planes * 8, height * 4, breadth * 16)


def with_nozzle(banded, phases):
    inflow = jnp.where(phases == 2, 1.5, jnp.where(phases == 1, -1.5, banded[0]))
    return jnp.concatenate([inflow[None], banded[1:]], axis=0)


def surface_finish(normal_x, normal_y, normal_z, curvature, surface_level):
    delta_peak = jnp.exp(-surface_level * surface_level / (2.0 * SPREAD * SPREAD)) / (
        SPREAD * 2.5066282746310002
    )
    strength = SURFACE * curvature * delta_peak
    fraction = 0.5 + 0.5 * jnp.tanh(surface_level / SPREAD)
    return jnp.stack(
        [
            coarsen(normal_x * strength),
            coarsen(normal_y * strength),
            coarsen(normal_z * strength),
            coarsen(fraction),
        ]
    )


def surface_slab(padded):
    grad_x = (padded[1:-1, 2:, 1:-1] - padded[1:-1, :-2, 1:-1]) * 0.5
    grad_y = (padded[1:-1, 1:-1, 2:] - padded[1:-1, 1:-1, :-2]) * 0.5
    grad_z = (padded[2:, 1:-1, 1:-1] - padded[:-2, 1:-1, 1:-1]) * 0.5
    inverse = 1.0 / jnp.sqrt(grad_x * grad_x + grad_y * grad_y + grad_z * grad_z + 1.0)
    normal_x = grad_x * inverse
    normal_y = grad_y * inverse
    normal_z = grad_z * inverse
    curvature = (normal_x[1:-1, 2:, 1:-1] - normal_x[1:-1, :-2, 1:-1]) * 0.5
    curvature = curvature + (normal_y[1:-1, 1:-1, 2:] - normal_y[1:-1, 1:-1, :-2]) * 0.5
    curvature = curvature + (normal_z[2:, 1:-1, 1:-1] - normal_z[:-2, 1:-1, 1:-1]) * 0.5
    return surface_finish(
        normal_x[1:-1, 1:-1, 1:-1],
        normal_y[1:-1, 1:-1, 1:-1],
        normal_z[1:-1, 1:-1, 1:-1],
        curvature,
        padded[2:-2, 2:-2, 2:-2],
    )


def centered(padded, direction):
    if direction == 0:
        middle = padded[:, 1:-1, 1:-1]
        return (jnp.roll(middle, -1, 0) - jnp.roll(middle, 1, 0)) * 0.5
    if direction == 1:
        return (padded[:, 2:, 1:-1] - padded[:, :-2, 1:-1]) * 0.5
    return (padded[:, 1:-1, 2:] - padded[:, 1:-1, :-2]) * 0.5


def predictor(padded_fields, component):
    moving = lax.dynamic_index_in_dim(padded_fields, component, 0, keepdims=False)
    inner_u = padded_fields[0, :, 1:-1, 1:-1]
    inner_v = padded_fields[1, :, 1:-1, 1:-1]
    inner_w = padded_fields[2, :, 1:-1, 1:-1]
    advect = -(
        inner_w * centered(moving, 0)
        + inner_u * centered(moving, 1)
        + inner_v * centered(moving, 2)
    )
    pressure = padded_fields[3]
    gradients = jnp.stack([centered(pressure, 1), centered(pressure, 2), centered(pressure, 0)])
    pushed = lax.dynamic_index_in_dim(gradients, component, 0, keepdims=False)
    return moving[:, 1:-1, 1:-1] + STEP_FLOW * (advect - pushed)


def sweep_once(padded, source):
    middle = padded[:, 1:-1, 1:-1]
    beside_all = (
        padded[:, 2:, 1:-1] + padded[:, :-2, 1:-1] + padded[:, 1:-1, 2:] + padded[:, 1:-1, :-2]
    )
    beside_all = beside_all + jnp.roll(middle, -1, 0) + jnp.roll(middle, 1, 0)
    return (source + IMPLICIT * beside_all) / (1.0 + 6.0 * IMPLICIT)


def spread_surface(level_set, band_tiles, nozzle_phase, inner_fields, is_level, group):
    fine_all = level_set[0]
    initial = lax.psum_scatter(
        jnp.where(is_level, fine_all, jnp.zeros_like(fine_all)),
        "grp",
        scatter_dimension=0,
        tiled=True,
    )
    coarse_planes = inner_fields.shape[1] // 4
    flow_slab = lax.dynamic_slice_in_dim(inner_fields, group * coarse_planes, coarse_planes, 1)
    speeds = (refine(flow_slab[2]), refine(flow_slab[0]), refine(flow_slab[1]))

    def run_section(current, keep_weight, blend_weight):
        padded = extended(current, (("grp", 0), ("gx", 1), ("gy", 2)), 3)
        return keep_weight * initial + blend_weight * (
            current + STEP_FINE * section_rate(padded, speeds, 3)
        )

    first_section = run_section(initial, 0.0, 1.0)
    second_section = run_section(first_section, 0.75, 0.25)
    third_section = run_section(second_section, 1.0 / 3.0, 2.0 / 3.0)
    tile_planes = band_tiles.shape[0] // 4
    tiles_here = lax.dynamic_slice_in_dim(band_tiles, group * tile_planes, tile_planes, 0)
    banded = jnp.where(band_cells(tiles_here) == 1, third_section, initial)
    shaped = jnp.where(group == 0, with_nozzle(banded, nozzle_phase), banded)
    surface_pad = extended(shaped, (("grp", 0), ("gx", 1), ("gy", 2)), 2)
    quarter = surface_slab(surface_pad)
    received = lax.all_to_all(quarter, "grp", split_axis=0, concat_axis=1, tiled=True)
    return (received, received[0])


def on_device_general(flow_fields, level_set, band_tiles, nozzle_phase):
    group = lax.axis_index("grp")
    component = jnp.minimum(group, 2)
    is_level = group == 3
    gathered = lax.all_gather(flow_fields, "grp", axis=0, tiled=True)
    padded_fields = extended(gathered, (("gx", 2), ("gy", 3)), 1)
    source = predictor(padded_fields, component)
    inner_fields = padded_fields[:, :, 1:-1, 1:-1]
    received, fraction = spread_surface(
        level_set, band_tiles, nozzle_phase, inner_fields, is_level, group
    )
    pushed = received[0]
    relaxed = source
    for sweep_number in range(SWEEPS):
        padded = extended(relaxed, (("gx", 1), ("gy", 2)), 1)
        relaxed = sweep_once(padded, source)
    updated = relaxed + STEP_FLOW * pushed
    result = jnp.where(is_level, fraction, updated)
    return result[None]


MESH = pl.DeviceIdType.MESH
LANES = 128
ROWS = 8
EXACT = lax.Precision.HIGHEST


def lanes_of(shape, dim=1):
    return lax.broadcasted_iota(jnp.int32, shape, dim)


def along_z(block, offset, period):
    spot = lanes_of(block.shape) % period
    plain = pltpu.roll(block, (-offset) % LANES, 1)
    if offset > 0:
        around = pltpu.roll(block, (period - offset) % LANES, 1)
        return jnp.where(spot < period - offset, plain, around)
    around = pltpu.roll(block, (-period - offset) % LANES, 1)
    return jnp.where(spot >= -offset, plain, around)


def along_rows(block, offset):
    return pltpu.roll(block, (-offset) % block.shape[0], 0)


def weno_upwind(diffs, speed):
    forward = speed >= 0.0
    one = jnp.where(forward, diffs[0], diffs[5])
    two = jnp.where(forward, diffs[1], diffs[4])
    three = jnp.where(forward, diffs[2], diffs[3])
    four = jnp.where(forward, diffs[3], diffs[2])
    five = jnp.where(forward, diffs[4], diffs[1])
    step_a = two - one
    step_b = three - two
    step_c = four - three
    step_d = five - four

    def weight(curve, slope):
        rough = (WENO_EPS * 12.0 / 13.0) + curve * curve + (3.0 / 13.0) * (slope * slope)
        inverse = 1.0 / rough
        return inverse * inverse

    weight_one = weight(step_b - step_a, 3.0 * step_b - step_a)
    weight_two = 6.0 * weight(step_c - step_b, step_c + step_b)
    weight_three = 3.0 * weight(step_d - step_c, 3.0 * step_c - step_d)
    mixed = (
        weight_one * (5.0 * step_b - 2.0 * step_a)
        + weight_two * (step_b + 2.0 * step_c)
        + weight_three * (4.0 * step_c - step_d)
    )
    total = weight_one + weight_two + weight_three
    return three + mixed / (6.0 * total)


def window(index, count, chunk, margin):
    low = index * chunk - margin
    high = (index + 1) * chunk + margin
    start, stop = max(low, 0), min(high, count * chunk)
    return start, stop - start, start - low


def brick_kernel(
    plan,
    flow_far,
    level_far,
    band_far,
    phase_far,
    out_ref,
    flow_ref,
    level_ref,
    band_ref,
    phase_ref,
    flow_turned,
    level_turned,
    marks_turned,
    flow_in,
    level_in,
    marks_in,
    speeds,
    stage_one,
    stage_two,
    shaped,
    normals,
    packed,
    results,
    gathered,
    send_sems,
    take_sems,
    load_sems,
):
    groups, halves, rings = plan["groups"], plan["halves"], plan["rings"]
    chunks = groups * halves
    fine_chunk, flow_chunk = plan["fine_chunk"], plan["flow_chunk"]
    fine_z, flow_z = plan["fine_z"], plan["flow_z"]
    fine_margin, mark_margin, flow_margin = 2 * ROWS, ROWS, ROWS
    fine_rows, flow_rows = chunks * fine_chunk, chunks * flow_chunk
    pairs = level_ref.shape[1] // 2
    majors = pairs * halves
    group = lax.axis_index("grp")
    half = lax.axis_index("gx")
    ring = lax.axis_index("gy")
    after = lax.rem(ring + 1, rings)
    before = lax.rem(ring + rings - 1, rings)
    mine = group * halves + half
    last = chunks - 1

    holder = group == groups - 1
    load_level = pltpu.make_async_copy(level_far, level_ref, load_sems.at[0])
    load_flow = pltpu.make_async_copy(flow_far, flow_ref, load_sems.at[1])
    load_band = pltpu.make_async_copy(band_far, band_ref, load_sems.at[2])
    load_phase = pltpu.make_async_copy(phase_far, phase_ref, load_sems.at[3])
    pl.when(holder)(load_level.start)
    load_flow.start()
    load_band.start()
    load_phase.start()

    barrier = pltpu.get_barrier_semaphore()

    def greet(target_group, target_half, target_ring):
        pl.semaphore_signal(
            barrier,
            inc=1,
            device_id=(target_group, target_half, target_ring),
            device_id_type=MESH,
        )

    for chunk in range(chunks):
        tg, th = chunk // halves, chunk % halves

        @pl.when(mine != chunk)
        def _(tg=tg, th=th):
            greet(tg, th, ring)

        @pl.when(mine == 0)
        def _(tg=tg, th=th):
            greet(tg, th, before)

        @pl.when(mine == last)
        def _(tg=tg, th=th):
            greet(tg, th, after)

    @pl.when(holder)
    def _():
        load_level.wait()
        for pair in range(pairs):
            both = [level_ref[:, 2 * pair], level_ref[:, 2 * pair + 1]]
            level_turned[pair] = jnp.concatenate(both, axis=0).T

    load_flow.wait()
    columns = [flow_ref[:, column] for column in range(flow_ref.shape[1])]
    flow_turned[...] = jnp.concatenate(columns * halves, axis=0).T
    load_band.wait()
    load_phase.wait()
    tiles_z, tiles_y = band_ref.shape
    wide_shape = (tiles_y, fine_rows)
    widen = (
        lanes_of(wide_shape) // (fine_rows // tiles_y)
        == lax.broadcasted_iota(jnp.int32, wide_shape, 0)
    ).astype(jnp.float32)
    wide_band = jnp.dot(
        band_ref[...].astype(jnp.float32), widen, preferred_element_type=jnp.float32
    )
    spare = LANES - tiles_z - phase_ref.shape[0]
    marks_turned[...] = jnp.concatenate(
        [
            wide_band,
            phase_ref[...].astype(jnp.float32),
            jnp.zeros((spare, fine_rows), jnp.float32),
        ],
        axis=0,
    ).T

    pl.semaphore_wait(barrier, chunks + 1)

    sent = []

    def push(source, target, chunk, ring_to, take, condition=None):
        tg, th = chunk // halves, chunk % halves
        slot = len(sent)
        remote = pltpu.make_async_remote_copy(
            src_ref=source,
            dst_ref=target,
            send_sem=send_sems.at[slot],
            recv_sem=take_sems.at[take],
            device_id=(tg, th, ring_to),
            device_id_type=MESH,
        )
        near = ring_to is ring
        far = mine != chunk if near else None
        if condition is not None:
            far = condition if far is None else jnp.logical_and(condition, far)
        if near:
            here = mine == chunk
            if condition is not None:
                here = jnp.logical_and(condition, here)

            @pl.when(here)
            def _():
                pltpu.make_async_copy(source, target, take_sems.at[take]).start()

        if far is None:
            remote.start()
        else:
            pl.when(far)(remote.start)
        sent.append((far, remote))

    major_spot = pl.ds(half * pairs, pairs)
    for chunk in range(chunks):
        start, count, spot = window(chunk, chunks, fine_chunk, fine_margin)
        push(
            level_turned.at[:, pl.ds(start, count)],
            level_in.at[major_spot, pl.ds(spot, count)],
            chunk,
            ring,
            0,
            holder,
        )
    push(
        level_turned.at[:, pl.ds(fine_rows - fine_margin, fine_margin)],
        level_in.at[major_spot, pl.ds(0, fine_margin)],
        0,
        after,
        0,
        holder,
    )
    push(
        level_turned.at[:, pl.ds(0, fine_margin)],
        level_in.at[major_spot, pl.ds(fine_margin + fine_chunk, fine_margin)],
        last,
        before,
        0,
        holder,
    )
    for chunk in range(chunks):
        start, count, spot = window(chunk, chunks, flow_chunk, flow_margin)
        push(
            flow_turned.at[pl.ds(start, count)],
            flow_in.at[group, half, pl.ds(spot, count)],
            chunk,
            ring,
            1,
        )
    push(
        flow_turned.at[pl.ds(flow_rows - flow_margin, flow_margin)],
        flow_in.at[group, half, pl.ds(0, flow_margin)],
        0,
        after,
        1,
    )
    push(
        flow_turned.at[pl.ds(0, flow_margin)],
        flow_in.at[group, half, pl.ds(flow_margin + flow_chunk, flow_margin)],
        last,
        before,
        1,
    )
    for chunk in range(chunks):
        start, count, spot = window(chunk, chunks, fine_chunk, mark_margin)
        push(
            marks_turned.at[pl.ds(start, count)],
            marks_in.at[half, pl.ds(spot, count)],
            chunk,
            ring,
            2,
            group == chunk // halves,
        )
    push(
        marks_turned.at[pl.ds(fine_rows - mark_margin, mark_margin)],
        marks_in.at[half, pl.ds(0, mark_margin)],
        0,
        after,
        2,
        group == 0,
    )
    push(
        marks_turned.at[pl.ds(0, mark_margin)],
        marks_in.at[half, pl.ds(mark_margin + fine_chunk, mark_margin)],
        last,
        before,
        2,
        group == groups - 1,
    )

    body = fine_chunk + 2 * mark_margin
    offset = fine_margin - mark_margin
    edge = jnp.zeros((majors, offset, LANES), jnp.float32)
    for stage in (stage_one, stage_two):
        stage[:, pl.ds(0, offset)] = edge
        stage[:, pl.ds(offset + body, offset)] = edge

    pltpu.make_async_copy(flow_in, flow_in, take_sems.at[1]).wait()
    share = LANES // halves
    fields = []
    flow_lane = lanes_of((flow_chunk + 2 * flow_margin, LANES))
    for field in range(groups):
        merged = flow_in[field, 0]
        for part in range(1, halves):
            merged = jnp.where(flow_lane >= part * share, flow_in[field, part], merged)
        fields.append(merged)

    from_flow = lax.broadcasted_iota(jnp.int32, (LANES, majors * LANES), 0)
    to_fine = lanes_of((LANES, majors * LANES))
    fine_cell = (to_fine // LANES) * flow_z + (to_fine % fine_z) // 2
    spread_lanes = (from_flow == fine_cell).astype(jnp.float32)
    flow_window = flow_chunk + 2 * flow_margin
    spread_rows = (
        lanes_of((body, flow_window))
        == lax.broadcasted_iota(jnp.int32, (body, flow_window), 0) // 2
        + (flow_margin - mark_margin // 2)
    ).astype(jnp.float32)
    for direction in range(3):
        tall = jnp.dot(
            spread_rows, fields[direction], precision=EXACT, preferred_element_type=jnp.float32
        )
        wide = jnp.dot(tall, spread_lanes, precision=EXACT, preferred_element_type=jnp.float32)
        for major in range(majors):
            speeds[direction, major] = wide[:, major * LANES : (major + 1) * LANES]

    def flow_beside(block, direction, step):
        if direction == 0:
            return pltpu.roll(block, (-step * flow_z) % LANES, 1)
        if direction == 1:
            return along_rows(block, step)
        return along_z(block, step, flow_z)

    def flow_slope(block, direction):
        return 0.5 * (flow_beside(block, direction, 1) - flow_beside(block, direction, -1))

    moved = []
    for component in range(3):
        moving = fields[component]
        advect = fields[0] * flow_slope(moving, 0)
        advect = advect + fields[1] * flow_slope(moving, 1)
        advect = advect + fields[2] * flow_slope(moving, 2)
        source = moving - STEP_FLOW * (advect + flow_slope(fields[3], component))
        relaxed = source
        for sweep_number in range(SWEEPS):
            beside = jnp.zeros_like(relaxed)
            for direction in range(3):
                beside = beside + flow_beside(relaxed, direction, 1)
                beside = beside + flow_beside(relaxed, direction, -1)
            relaxed = (source + IMPLICIT * beside) * (1.0 / (1.0 + 6.0 * IMPLICIT))
        moved.append(relaxed[flow_margin : flow_margin + flow_chunk])

    pltpu.make_async_copy(level_in, level_in, take_sems.at[0]).wait()

    block_rows = 2 * ROWS

    def section(current, target, keep, blend):
        def one(major, carry):
            def far_major(step):
                return lax.rem(major + majors + step, majors)

            for start in range(0, body, block_rows):
                rows = pl.ds(offset + start, block_rows)
                tall = current[major, pl.ds(start, block_rows + 2 * offset)]
                middle = tall[offset : offset + block_rows]
                low_half = lanes_of(middle.shape) < fine_z
                whole = {step: current[far_major(step), rows] for step in (-2, -1, 1, 2)}
                whole[0] = middle
                swapped = {step: pltpu.roll(whole[step], fine_z, 1) for step in whole}

                def beside(direction, step):
                    if step == 0:
                        return middle
                    if direction == 1:
                        return tall[offset + step : offset + step + block_rows]
                    if direction == 2:
                        return along_z(middle, step, fine_z)
                    base = step // 2
                    if step % 2 == 0:
                        return whole[base]
                    return jnp.where(low_half, swapped[base], swapped[base + 1])

                rate = jnp.zeros_like(middle)
                for direction in range(3):
                    cells = [beside(direction, step) for step in range(-3, 4)]
                    diffs = [cells[i + 1] - cells[i] for i in range(6)]
                    speed = speeds[direction, major, pl.ds(start, block_rows)]
                    rate = rate - speed * weno_upwind(diffs, speed)
                moved_on = blend * (middle + STEP_FINE * rate)
                if keep:
                    moved_on = keep * level_in[major, rows] + moved_on
                target[major, rows] = moved_on
            return carry

        lax.fori_loop(0, majors, one, 0)

    section(level_in, stage_one, 0.0, 1.0)
    section(stage_one, stage_two, 0.75, 0.25)
    section(stage_two, stage_one, 1.0 / 3.0, 2.0 / 3.0)

    pltpu.make_async_copy(marks_in, marks_in, take_sems.at[2]).wait()
    mark_from = lax.broadcasted_iota(jnp.int32, (LANES, LANES), 0)
    mark_to = lanes_of((LANES, LANES))
    tile_z = plan["tile_z"]
    tile_count = fine_z // tile_z
    inside = pl.ds(offset, body)
    spread_band = (mark_from == (mark_to % fine_z) // tile_z).astype(jnp.float32)
    for part in range(halves):
        marks = marks_in[part]
        band = jnp.dot(marks, spread_band, preferred_element_type=jnp.float32)
        for pair in range(pairs):
            pick = jnp.logical_and(
                mark_from == tile_count + 2 * pair + mark_to // fine_z, mark_to % fine_z == 0
            ).astype(jnp.float32)
            phase = jnp.dot(marks, pick, preferred_element_type=jnp.float32)
            major = part * pairs + pair
            banded = jnp.where(band > 0.5, stage_one[major, inside], level_in[major, inside])
            shaped[major] = jnp.where(
                phase > 1.5, SPREAD, jnp.where(phase > 0.5, -SPREAD, banded)
            )

    low_half = lanes_of((body, LANES)) < fine_z

    def x_slope(ref, major):
        here = pltpu.roll(ref[major], fine_z, 1)
        up = pltpu.roll(ref[(major + 1) % majors], fine_z, 1)
        down = pltpu.roll(ref[(major + majors - 1) % majors], fine_z, 1)
        return 0.5 * (jnp.where(low_half, here, up) - jnp.where(low_half, down, here))

    for major in range(majors):
        level = shaped[major]
        slope_x = x_slope(shaped, major)
        slope_y = 0.5 * (along_rows(level, 1) - along_rows(level, -1))
        slope_z = 0.5 * (along_z(level, 1, fine_z) - along_z(level, -1, fine_z))
        inverse = lax.rsqrt(slope_x * slope_x + slope_y * slope_y + slope_z * slope_z + 1.0)
        normals[0, major] = slope_x * inverse
        normals[1, major] = slope_y * inverse
        normals[2, major] = slope_z * inverse

    core = slice(mark_margin, mark_margin + fine_chunk)
    for major in range(majors):
        normal_y, normal_z = normals[1, major], normals[2, major]
        curvature = x_slope(normals.at[0], major)
        curvature = curvature + 0.5 * (along_rows(normal_y, 1) - along_rows(normal_y, -1))
        curvature = curvature + 0.5 * (
            along_z(normal_z, 1, fine_z) - along_z(normal_z, -1, fine_z)
        )
        level = shaped[major]
        delta_peak = jnp.exp(level * level * (-1.0 / (2.0 * SPREAD * SPREAD)))
        strength = (SURFACE / (SPREAD * 2.5066282746310002)) * curvature * delta_peak
        lane_spot = slice(major * LANES, (major + 1) * LANES)
        for direction in range(3):
            force = (normals[direction, major] * strength)[core]
            packed[pl.ds(direction * fine_chunk, fine_chunk), lane_spot] = force
        fraction = (0.5 + 0.5 * jnp.tanh(level * (1.0 / SPREAD)))[core]
        packed[pl.ds(3 * fine_chunk, fine_chunk), lane_spot] = fraction

    fine_from = lax.broadcasted_iota(jnp.int32, (majors * LANES, LANES), 0)
    flow_to = lanes_of((majors * LANES, LANES))
    fold_lanes = (
        flow_to == (fine_from // LANES) * flow_z + (fine_from % fine_z) // 2
    ).astype(jnp.float32)
    folded = jnp.dot(
        packed[...], fold_lanes, precision=EXACT, preferred_element_type=jnp.float32
    )
    fold_shape = (4 * flow_chunk, 4 * fine_chunk)
    fold_rows = (
        lanes_of(fold_shape) // 2 == lax.broadcasted_iota(jnp.int32, fold_shape, 0)
    ).astype(jnp.float32)
    means = 0.125 * jnp.dot(
        fold_rows, folded, precision=EXACT, preferred_element_type=jnp.float32
    )
    for output in range(4):
        mean = means[output * flow_chunk : (output + 1) * flow_chunk]
        results[output] = moved[output] + STEP_FLOW * mean if output < 3 else mean

    landing = pl.ds(pl.multiple_of(mine * flow_chunk, flow_chunk), flow_chunk)
    for chunk in range(chunks):
        push(results.at[chunk // halves], gathered.at[landing], chunk, ring, 3)
    pltpu.make_async_copy(gathered, gathered, take_sems.at[3]).wait()
    turned = gathered[...].T
    outcome = turned[:share]
    for part in range(1, halves):
        outcome = jnp.where(half == part, turned[part * share : (part + 1) * share], outcome)
    out_ref[...] = outcome
    for condition, copy in sent:
        if condition is None:
            copy.wait_send()
        else:
            pl.when(condition)(copy.wait_send)


def on_device_bricks(plan, flow_fields, level_set, band_tiles, nozzle_phase):
    flow_z, flow_x, flow_y = flow_fields.shape[1:]
    fine_z, fine_x, fine_y = level_set.shape[1:]
    groups, halves = plan["groups"], plan["halves"]
    chunks = groups * halves
    fine_chunk, flow_chunk = fine_y // chunks, flow_y // chunks
    tiles_z = band_tiles.shape[0]
    plan = dict(
        plan,
        fine_chunk=fine_chunk,
        flow_chunk=flow_chunk,
        fine_z=fine_z,
        flow_z=flow_z,
        tile_z=fine_z // tiles_z,
    )
    majors = fine_x // 2 * halves
    body = fine_chunk + 2 * ROWS
    tall = fine_chunk + 4 * ROWS
    vmem = pl.BlockSpec(memory_space=pltpu.VMEM)

    def room(*shape):
        return pltpu.VMEM(shape, jnp.float32)

    copies = 4 * chunks + 6
    result = pl.pallas_call(
        functools.partial(brick_kernel, plan),
        out_shape=jax.ShapeDtypeStruct((flow_x * flow_z, flow_y), jnp.float32),
        in_specs=[pl.BlockSpec(memory_space=pltpu.HBM)] * 4,
        out_specs=vmem,
        scratch_shapes=[
            room(flow_z, flow_x, flow_y),
            room(fine_z, fine_x, fine_y),
            pltpu.VMEM((band_tiles.shape[0], band_tiles.shape[2]), band_tiles.dtype),
            pltpu.VMEM(nozzle_phase.shape, nozzle_phase.dtype),
            room(flow_y, LANES),
            room(fine_x // 2, fine_y, LANES),
            room(fine_y, LANES),
            room(groups, halves, flow_chunk + 2 * ROWS, LANES),
            room(majors, tall, LANES),
            room(halves, body, LANES),
            room(3, majors, body, LANES),
            room(majors, tall, LANES),
            room(majors, tall, LANES),
            room(majors, body, LANES),
            room(3, majors, body, LANES),
            room(4 * fine_chunk, majors * LANES),
            room(4, flow_chunk, LANES),
            room(flow_y, LANES),
            pltpu.SemaphoreType.DMA((copies,)),
            pltpu.SemaphoreType.DMA((4,)),
            pltpu.SemaphoreType.DMA((4,)),
        ],
        compiler_params=pltpu.CompilerParams(
            collective_id=0, has_side_effects=True, vmem_limit_bytes=60 * 1024 * 1024
        ),
        name="jet_step",
    )(flow_fields[0], level_set[0], band_tiles[:, 0], nozzle_phase)
    return result.reshape(flow_x, flow_z, flow_y).transpose(1, 0, 2)[None]


def solution(mesh):
    placed = (
        P("grp", None, "gx", "gy"),
        P("grp", None, "gx", "gy"),
        P(None, "gx", "gy"),
        P("gx", "gy"),
    )
    plan = {"groups": mesh.shape["grp"], "halves": mesh.shape["gx"], "rings": mesh.shape["gy"]}

    def on_device(flow_fields, level_set, band_tiles, nozzle_phase):
        flow_z, flow_x, flow_y = flow_fields.shape[1:]
        chunks = plan["groups"] * plan["halves"]
        fits = (
            plan["halves"] * flow_x * flow_z == LANES
            and 2 * level_set.shape[1] == LANES
            and flow_y == LANES
            and flow_y % (chunks * 2 * ROWS) == 0
            and band_tiles.shape[1] == 1
            and plan["rings"] > 2
        )
        if fits:
            return on_device_bricks(plan, flow_fields, level_set, band_tiles, nozzle_phase)
        return on_device_general(flow_fields, level_set, band_tiles, nozzle_phase)

    return jax.shard_map(
        on_device, mesh=mesh, in_specs=placed, out_specs=P("grp", None, "gx", "gy"), check_vma=False
    )
```

```python
import functools

import jax
import jax.numpy as jnp
from jax import lax
from jax.experimental import pallas as pl
from jax.experimental.pallas import tpu as pltpu
from jax.sharding import PartitionSpec as P

SWEEPS = 3


WENO_EPS = 1e-06
STEP_FINE = 0.3
STEP_FLOW = 0.2
SURFACE = 6.0
SPREAD = 1.5
IMPLICIT = 0.5


def extended(block, sides, width):
    for axis, dim in sides:
        count = lax.axis_size(axis)
        forward = [(i, i + 1) for i in range(count - 1)]
        forward.append((count - 1, 0))
        backward = [(target, source) for source, target in forward]
        low = lax.ppermute(
            lax.slice_in_dim(block, block.shape[dim] - width, None, axis=dim), axis, forward
        )
        high = lax.ppermute(lax.slice_in_dim(block, 0, width, axis=dim), axis, backward)
        block = jnp.concatenate([low, block, high], axis=dim)
    return block


def weno_side(diff_one, diff_two, diff_three, diff_four, diff_five):
    cand_one = diff_one / 3.0 - 7.0 * diff_two / 6.0 + 11.0 * diff_three / 6.0
    cand_two = -diff_two / 6.0 + 5.0 * diff_three / 6.0 + diff_four / 3.0
    cand_three = diff_three / 3.0 + 5.0 * diff_four / 6.0 - diff_five / 6.0
    curve_one = diff_one - 2.0 * diff_two + diff_three
    slope_one = diff_one - 4.0 * diff_two + 3.0 * diff_three
    smooth_one = 13.0 / 12.0 * curve_one * curve_one + 0.25 * slope_one * slope_one
    curve_two = diff_two - 2.0 * diff_three + diff_four
    slope_two = diff_two - diff_four
    smooth_two = 13.0 / 12.0 * curve_two * curve_two + 0.25 * slope_two * slope_two
    curve_three = diff_three - 2.0 * diff_four + diff_five
    slope_three = 3.0 * diff_three - 4.0 * diff_four + diff_five
    smooth_three = 13.0 / 12.0 * curve_three * curve_three + 0.25 * slope_three * slope_three
    weight_one = 0.1 / ((WENO_EPS + smooth_one) * (WENO_EPS + smooth_one))
    weight_two = 0.6 / ((WENO_EPS + smooth_two) * (WENO_EPS + smooth_two))
    weight_three = 0.3 / ((WENO_EPS + smooth_three) * (WENO_EPS + smooth_three))
    return (weight_one * cand_one + weight_two * cand_two + weight_three * cand_three) / (
        weight_one + weight_two + weight_three
    )


def section_rate(padded, speeds, plane_rim):
    plane_count = padded.shape[0] - 2 * plane_rim
    row_count = padded.shape[1] - 6
    col_count = padded.shape[2] - 6

    def sample(offset, direction):
        if direction == 0:
            return padded[
                3 + offset : 3 + offset + plane_count, 3 : 3 + row_count, 3 : 3 + col_count
            ]
        if direction == 1:
            return padded[
                plane_rim : plane_rim + plane_count,
                3 + offset : 3 + offset + row_count,
                3 : 3 + col_count,
            ]
        return padded[
            plane_rim : plane_rim + plane_count,
            3 : 3 + row_count,
            3 + offset : 3 + offset + col_count,
        ]

    summed = jnp.zeros((plane_count, row_count, col_count), jnp.float32)
    for direction in range(3):
        differences = [
            sample(offset + 1, direction) - sample(offset, direction) for offset in range(-3, 3)
        ]
        minus_side = weno_side(
            differences[0], differences[1], differences[2], differences[3], differences[4]
        )
        plus_side = weno_side(
            differences[5], differences[4], differences[3], differences[2], differences[1]
        )
        upwind = jnp.where(speeds[direction] >= 0.0, minus_side, plus_side)
        summed = summed - speeds[direction] * upwind
    return summed


def refine(coarse):
    plane_count, height, breadth = coarse.shape
    spread_out = jnp.broadcast_to(
        coarse[:, None, :, None, :, None], (plane_count, 2, height, 2, breadth, 2)
    )
    return spread_out.reshape(2 * plane_count, 2 * height, 2 * breadth)


def coarsen(fine_field):
    plane_count, height, breadth = fine_field.shape
    blocks = fine_field.reshape(plane_count // 2, 2, height // 2, 2, breadth // 2, 2)
    return jnp.sum(blocks, axis=(1, 3, 5)) * 0.125


def band_cells(tile_flags):
    planes, height, breadth = tile_flags.shape
    spread_out = jnp.broadcast_to(
        tile_flags[:, None, :, None, :, None], (planes, 8, height, 4, breadth, 16)
    )
    return spread_out.reshape(planes * 8, height * 4, breadth * 16)


def with_nozzle(banded, phases):
    inflow = jnp.where(phases == 2, 1.5, jnp.where(phases == 1, -1.5, banded[0]))
    return jnp.concatenate([inflow[None], banded[1:]], axis=0)


def surface_finish(normal_x, normal_y, normal_z, curvature, surface_level):
    delta_peak = jnp.exp(-surface_level * surface_level / (2.0 * SPREAD * SPREAD)) / (
        SPREAD * 2.5066282746310002
    )
    strength = SURFACE * curvature * delta_peak
    fraction = 0.5 + 0.5 * jnp.tanh(surface_level / SPREAD)
    return jnp.stack(
        [
            coarsen(normal_x * strength),
            coarsen(normal_y * strength),
            coarsen(normal_z * strength),
            coarsen(fraction),
        ]
    )


def surface_slab(padded):
    grad_x = (padded[1:-1, 2:, 1:-1] - padded[1:-1, :-2, 1:-1]) * 0.5
    grad_y = (padded[1:-1, 1:-1, 2:] - padded[1:-1, 1:-1, :-2]) * 0.5
    grad_z = (padded[2:, 1:-1, 1:-1] - padded[:-2, 1:-1, 1:-1]) * 0.5
    inverse = 1.0 / jnp.sqrt(grad_x * grad_x + grad_y * grad_y + grad_z * grad_z + 1.0)
    normal_x = grad_x * inverse
    normal_y = grad_y * inverse
    normal_z = grad_z * inverse
    curvature = (normal_x[1:-1, 2:, 1:-1] - normal_x[1:-1, :-2, 1:-1]) * 0.5
    curvature = curvature + (normal_y[1:-1, 1:-1, 2:] - normal_y[1:-1, 1:-1, :-2]) * 0.5
    curvature = curvature + (normal_z[2:, 1:-1, 1:-1] - normal_z[:-2, 1:-1, 1:-1]) * 0.5
    return surface_finish(
        normal_x[1:-1, 1:-1, 1:-1],
        normal_y[1:-1, 1:-1, 1:-1],
        normal_z[1:-1, 1:-1, 1:-1],
        curvature,
        padded[2:-2, 2:-2, 2:-2],
    )


def centered(padded, direction):
    if direction == 0:
        middle = padded[:, 1:-1, 1:-1]
        return (jnp.roll(middle, -1, 0) - jnp.roll(middle, 1, 0)) * 0.5
    if direction == 1:
        return (padded[:, 2:, 1:-1] - padded[:, :-2, 1:-1]) * 0.5
    return (padded[:, 1:-1, 2:] - padded[:, 1:-1, :-2]) * 0.5


def predictor(padded_fields, component):
    moving = lax.dynamic_index_in_dim(padded_fields, component, 0, keepdims=False)
    inner_u = padded_fields[0, :, 1:-1, 1:-1]
    inner_v = padded_fields[1, :, 1:-1, 1:-1]
    inner_w = padded_fields[2, :, 1:-1, 1:-1]
    advect = -(
        inner_w * centered(moving, 0)
        + inner_u * centered(moving, 1)
        + inner_v * centered(moving, 2)
    )
    pressure = padded_fields[3]
    gradients = jnp.stack([centered(pressure, 1), centered(pressure, 2), centered(pressure, 0)])
    pushed = lax.dynamic_index_in_dim(gradients, component, 0, keepdims=False)
    return moving[:, 1:-1, 1:-1] + STEP_FLOW * (advect - pushed)


def sweep_once(padded, source):
    middle = padded[:, 1:-1, 1:-1]
    beside_all = (
        padded[:, 2:, 1:-1] + padded[:, :-2, 1:-1] + padded[:, 1:-1, 2:] + padded[:, 1:-1, :-2]
    )
    beside_all = beside_all + jnp.roll(middle, -1, 0) + jnp.roll(middle, 1, 0)
    return (source + IMPLICIT * beside_all) / (1.0 + 6.0 * IMPLICIT)


def spread_surface(level_set, band_tiles, nozzle_phase, inner_fields, is_level, group):
    fine_all = level_set[0]
    initial = lax.psum_scatter(
        jnp.where(is_level, fine_all, jnp.zeros_like(fine_all)),
        "grp",
        scatter_dimension=0,
        tiled=True,
    )
    coarse_planes = inner_fields.shape[1] // 4
    flow_slab = lax.dynamic_slice_in_dim(inner_fields, group * coarse_planes, coarse_planes, 1)
    speeds = (refine(flow_slab[2]), refine(flow_slab[0]), refine(flow_slab[1]))

    def run_section(current, keep_weight, blend_weight):
        padded = extended(current, (("grp", 0), ("gx", 1), ("gy", 2)), 3)
        return keep_weight * initial + blend_weight * (
            current + STEP_FINE * section_rate(padded, speeds, 3)
        )

    first_section = run_section(initial, 0.0, 1.0)
    second_section = run_section(first_section, 0.75, 0.25)
    third_section = run_section(second_section, 1.0 / 3.0, 2.0 / 3.0)
    tile_planes = band_tiles.shape[0] // 4
    tiles_here = lax.dynamic_slice_in_dim(band_tiles, group * tile_planes, tile_planes, 0)
    banded = jnp.where(band_cells(tiles_here) == 1, third_section, initial)
    shaped = jnp.where(group == 0, with_nozzle(banded, nozzle_phase), banded)
    surface_pad = extended(shaped, (("grp", 0), ("gx", 1), ("gy", 2)), 2)
    quarter = surface_slab(surface_pad)
    received = lax.all_to_all(quarter, "grp", split_axis=0, concat_axis=1, tiled=True)
    return (received, received[0])


def on_device_general(flow_fields, level_set, band_tiles, nozzle_phase):
    group = lax.axis_index("grp")
    component = jnp.minimum(group, 2)
    is_level = group == 3
    gathered = lax.all_gather(flow_fields, "grp", axis=0, tiled=True)
    padded_fields = extended(gathered, (("gx", 2), ("gy", 3)), 1)
    source = predictor(padded_fields, component)
    inner_fields = padded_fields[:, :, 1:-1, 1:-1]
    received, fraction = spread_surface(
        level_set, band_tiles, nozzle_phase, inner_fields, is_level, group
    )
    pushed = received[0]
    relaxed = source
    for sweep_number in range(SWEEPS):
        padded = extended(relaxed, (("gx", 1), ("gy", 2)), 1)
        relaxed = sweep_once(padded, source)
    updated = relaxed + STEP_FLOW * pushed
    result = jnp.where(is_level, fraction, updated)
    return result[None]


MESH = pl.DeviceIdType.MESH
LANES = 128
ROWS = 8
EXACT = lax.Precision.HIGHEST


def lanes_of(shape, dim=1):
    return lax.broadcasted_iota(jnp.int32, shape, dim)


def along_z(block, offset, period):
    spot = lanes_of(block.shape) % period
    plain = pltpu.roll(block, (-offset) % LANES, 1)
    if offset > 0:
        around = pltpu.roll(block, (period - offset) % LANES, 1)
        return jnp.where(spot < period - offset, plain, around)
    around = pltpu.roll(block, (-period - offset) % LANES, 1)
    return jnp.where(spot >= -offset, plain, around)


def along_rows(block, offset):
    return pltpu.roll(block, (-offset) % block.shape[0], 0)


def inverse_of(block):
    rough = pl.reciprocal(block, approx=True)
    return rough * (2.0 - block * rough)


def weno_flux(bends, near, speed, forward, pace):
    step_a = jnp.where(forward, bends[0], bends[4])
    step_b = jnp.where(forward, bends[1], bends[3])
    step_c = bends[2]
    step_d = jnp.where(forward, bends[3], bends[1])
    three = jnp.where(forward, near[0], near[1])

    def weight(curve, slope):
        inverse = inverse_of(
            (WENO_EPS * 12.0 / 13.0) + curve * curve + (3.0 / 13.0) * (slope * slope)
        )
        return inverse * inverse

    triple_c = 3.0 * step_c
    weight_one = weight(step_b - step_a, 3.0 * step_b - step_a)
    weight_two = 6.0 * weight(step_c - step_b, step_c + step_b)
    weight_three = 3.0 * weight(step_d - step_c, triple_c - step_d)
    mixed = (
        weight_one * (5.0 * step_b - 2.0 * step_a)
        + weight_two * (step_b + 2.0 * step_c)
        + weight_three * (step_c + triple_c - step_d)
    )
    total = weight_one + weight_two + weight_three
    return speed * three + (pace * mixed) * inverse_of(total)


def window(index, count, chunk, margin):
    low = index * chunk - margin
    high = (index + 1) * chunk + margin
    start, stop = max(low, 0), min(high, count * chunk)
    return start, stop - start, start - low


def brick_kernel(
    plan,
    flow_far,
    level_far,
    band_far,
    phase_far,
    out_ref,
    flow_ref,
    level_ref,
    band_ref,
    phase_ref,
    flow_turned,
    level_turned,
    marks_turned,
    flow_in,
    level_in,
    marks_in,
    speeds,
    stage_one,
    stage_two,
    shaped,
    normals,
    packed,
    results,
    gathered,
    send_sems,
    take_sems,
    load_sems,
):
    groups, halves, rings = plan["groups"], plan["halves"], plan["rings"]
    chunks = groups * halves
    fine_chunk, flow_chunk = plan["fine_chunk"], plan["flow_chunk"]
    fine_z, flow_z = plan["fine_z"], plan["flow_z"]
    fine_margin, mark_margin, flow_margin = 2 * ROWS, ROWS, ROWS
    fine_rows, flow_rows = chunks * fine_chunk, chunks * flow_chunk
    pairs = level_ref.shape[1] // 2
    majors = pairs * halves
    group = lax.axis_index("grp")
    half = lax.axis_index("gx")
    ring = lax.axis_index("gy")
    after = lax.rem(ring + 1, rings)
    before = lax.rem(ring + rings - 1, rings)
    mine = group * halves + half
    last = chunks - 1

    holder = group == groups - 1
    load_level = pltpu.make_async_copy(level_far, level_ref, load_sems.at[0])
    load_flow = pltpu.make_async_copy(flow_far, flow_ref, load_sems.at[1])
    load_band = pltpu.make_async_copy(band_far, band_ref, load_sems.at[2])
    load_phase = pltpu.make_async_copy(phase_far, phase_ref, load_sems.at[3])
    pl.when(holder)(load_level.start)
    load_flow.start()
    load_band.start()
    load_phase.start()

    barrier = pltpu.get_barrier_semaphore()

    def greet(target_group, target_half, target_ring):
        pl.semaphore_signal(
            barrier,
            inc=1,
            device_id=(target_group, target_half, target_ring),
            device_id_type=MESH,
        )

    for chunk in range(chunks):
        tg, th = chunk // halves, chunk % halves

        @pl.when(mine != chunk)
        def _(tg=tg, th=th):
            greet(tg, th, ring)

        @pl.when(mine == 0)
        def _(tg=tg, th=th):
            greet(tg, th, before)

        @pl.when(mine == last)
        def _(tg=tg, th=th):
            greet(tg, th, after)

    @pl.when(holder)
    def _():
        load_level.wait()
        for pair in range(pairs):
            both = [level_ref[:, 2 * pair], level_ref[:, 2 * pair + 1]]
            level_turned[pair] = jnp.concatenate(both, axis=0).T

    load_flow.wait()
    columns = [flow_ref[:, column] for column in range(flow_ref.shape[1])]
    flow_turned[...] = jnp.concatenate(columns * halves, axis=0).T
    load_band.wait()
    load_phase.wait()
    tiles_z, tiles_y = band_ref.shape
    wide_shape = (tiles_y, fine_rows)
    widen = (
        lanes_of(wide_shape) // (fine_rows // tiles_y)
        == lax.broadcasted_iota(jnp.int32, wide_shape, 0)
    ).astype(jnp.float32)
    wide_band = jnp.dot(
        band_ref[...].astype(jnp.float32), widen, preferred_element_type=jnp.float32
    )
    spare = LANES - tiles_z - phase_ref.shape[0]
    marks_turned[...] = jnp.concatenate(
        [
            wide_band,
            phase_ref[...].astype(jnp.float32),
            jnp.zeros((spare, fine_rows), jnp.float32),
        ],
        axis=0,
    ).T

    pl.semaphore_wait(barrier, chunks + 1)

    sent = []

    def push(source, target, chunk, ring_to, take, condition=None):
        tg, th = chunk // halves, chunk % halves
        slot = len(sent)
        remote = pltpu.make_async_remote_copy(
            src_ref=source,
            dst_ref=target,
            send_sem=send_sems.at[slot],
            recv_sem=take_sems.at[take],
            device_id=(tg, th, ring_to),
            device_id_type=MESH,
        )
        near = ring_to is ring
        far = mine != chunk if near else None
        if condition is not None:
            far = condition if far is None else jnp.logical_and(condition, far)
        if near:
            here = mine == chunk
            if condition is not None:
                here = jnp.logical_and(condition, here)

            @pl.when(here)
            def _():
                pltpu.make_async_copy(source, target, take_sems.at[take]).start()

        if far is None:
            remote.start()
        else:
            pl.when(far)(remote.start)
        sent.append((far, remote))

    major_spot = pl.ds(half * pairs, pairs)
    for chunk in range(chunks):
        start, count, spot = window(chunk, chunks, fine_chunk, fine_margin)
        push(
            level_turned.at[:, pl.ds(start, count)],
            level_in.at[major_spot, pl.ds(spot, count)],
            chunk,
            ring,
            0,
            holder,
        )
    push(
        level_turned.at[:, pl.ds(fine_rows - fine_margin, fine_margin)],
        level_in.at[major_spot, pl.ds(0, fine_margin)],
        0,
        after,
        0,
        holder,
    )
    push(
        level_turned.at[:, pl.ds(0, fine_margin)],
        level_in.at[major_spot, pl.ds(fine_margin + fine_chunk, fine_margin)],
        last,
        before,
        0,
        holder,
    )
    for chunk in range(chunks):
        start, count, spot = window(chunk, chunks, flow_chunk, flow_margin)
        push(
            flow_turned.at[pl.ds(start, count)],
            flow_in.at[group, half, pl.ds(spot, count)],
            chunk,
            ring,
            1,
        )
    push(
        flow_turned.at[pl.ds(flow_rows - flow_margin, flow_margin)],
        flow_in.at[group, half, pl.ds(0, flow_margin)],
        0,
        after,
        1,
    )
    push(
        flow_turned.at[pl.ds(0, flow_margin)],
        flow_in.at[group, half, pl.ds(flow_margin + flow_chunk, flow_margin)],
        last,
        before,
        1,
    )
    for chunk in range(chunks):
        start, count, spot = window(chunk, chunks, fine_chunk, mark_margin)
        push(
            marks_turned.at[pl.ds(start, count)],
            marks_in.at[half, pl.ds(spot, count)],
            chunk,
            ring,
            2,
            group == chunk // halves,
        )
    push(
        marks_turned.at[pl.ds(fine_rows - mark_margin, mark_margin)],
        marks_in.at[half, pl.ds(0, mark_margin)],
        0,
        after,
        2,
        group == 0,
    )
    push(
        marks_turned.at[pl.ds(0, mark_margin)],
        marks_in.at[half, pl.ds(mark_margin + fine_chunk, mark_margin)],
        last,
        before,
        2,
        group == groups - 1,
    )

    body = fine_chunk + 2 * mark_margin
    offset = fine_margin - mark_margin
    edge = jnp.zeros((majors, offset, LANES), jnp.float32)
    for stage in (stage_one, stage_two):
        stage[:, pl.ds(0, offset)] = edge
        stage[:, pl.ds(offset + body, offset)] = edge

    pltpu.make_async_copy(flow_in, flow_in, take_sems.at[1]).wait()
    share = LANES // halves
    fields = []
    flow_lane = lanes_of((flow_chunk + 2 * flow_margin, LANES))
    for field in range(groups):
        merged = flow_in[field, 0]
        for part in range(1, halves):
            merged = jnp.where(flow_lane >= part * share, flow_in[field, part], merged)
        fields.append(merged)

    from_flow = lax.broadcasted_iota(jnp.int32, (LANES, majors * LANES), 0)
    to_fine = lanes_of((LANES, majors * LANES))
    fine_cell = (to_fine // LANES) * flow_z + (to_fine % fine_z) // 2
    spread_lanes = (from_flow == fine_cell).astype(jnp.float32)
    flow_window = flow_chunk + 2 * flow_margin
    spread_rows = (
        lanes_of((body, flow_window))
        == lax.broadcasted_iota(jnp.int32, (body, flow_window), 0) // 2
        + (flow_margin - mark_margin // 2)
    ).astype(jnp.float32)
    for direction in range(3):
        tall = jnp.dot(
            spread_rows, fields[direction], precision=EXACT, preferred_element_type=jnp.float32
        )
        wide = jnp.dot(tall, spread_lanes, precision=EXACT, preferred_element_type=jnp.float32)
        for major in range(majors):
            speeds[direction, major] = wide[:, major * LANES : (major + 1) * LANES]

    def flow_beside(block, direction, step):
        if direction == 0:
            return pltpu.roll(block, (-step * flow_z) % LANES, 1)
        if direction == 1:
            return along_rows(block, step)
        return along_z(block, step, flow_z)

    def flow_slope(block, direction):
        return 0.5 * (flow_beside(block, direction, 1) - flow_beside(block, direction, -1))

    moved = []
    for component in range(3):
        moving = fields[component]
        advect = fields[0] * flow_slope(moving, 0)
        advect = advect + fields[1] * flow_slope(moving, 1)
        advect = advect + fields[2] * flow_slope(moving, 2)
        source = moving - STEP_FLOW * (advect + flow_slope(fields[3], component))
        relaxed = source
        for sweep_number in range(SWEEPS):
            beside = jnp.zeros_like(relaxed)
            for direction in range(3):
                beside = beside + flow_beside(relaxed, direction, 1)
                beside = beside + flow_beside(relaxed, direction, -1)
            relaxed = (source + IMPLICIT * beside) * (1.0 / (1.0 + 6.0 * IMPLICIT))
        moved.append(relaxed[flow_margin : flow_margin + flow_chunk])

    pltpu.make_async_copy(level_in, level_in, take_sems.at[0]).wait()

    block_rows = 2 * ROWS

    def section(current, target, keep, blend):
        def one(major, carry):
            def far_major(step):
                return lax.rem(major + majors + step, majors)

            for start in range(0, body, block_rows):
                rows = pl.ds(offset + start, block_rows)
                tall = current[major, pl.ds(start, block_rows + 2 * offset)]
                middle = tall[offset : offset + block_rows]
                low_half = lanes_of(middle.shape) < fine_z
                whole = {step: current[far_major(step), rows] for step in (-2, -1, 1, 2)}
                whole[0] = middle
                swapped = {step: pltpu.roll(whole[step], fine_z, 1) for step in whole}

                def beside(direction, step):
                    if step == 0:
                        return middle
                    if direction == 1:
                        return tall[offset + step : offset + step + block_rows]
                    if direction == 2:
                        return along_z(middle, step, fine_z)
                    base = step // 2
                    if step % 2 == 0:
                        return whole[base]
                    return jnp.where(low_half, swapped[base], swapped[base + 1])

                rate = jnp.zeros_like(middle)
                for direction in range(3):
                    if direction == 2:
                        first = along_z(middle, 1, fine_z) - middle
                        behind = along_z(first, -1, fine_z)
                        bend = first - behind
                        bends = [
                            along_z(bend, step, fine_z) if step else bend
                            for step in (-2, -1, 0, 1, 2)
                        ]
                        near = (behind, first)
                    else:
                        cells = [beside(direction, step) for step in range(-3, 4)]
                        diffs = [cells[i + 1] - cells[i] for i in range(6)]
                        bends = [diffs[i + 1] - diffs[i] for i in range(5)]
                        near = (diffs[2], diffs[3])
                    speed = speeds[direction, major, pl.ds(start, block_rows)]
                    forward = speed >= 0.0
                    pace = jnp.abs(speed) * (1.0 / 6.0)
                    rate = rate - weno_flux(bends, near, speed, forward, pace)
                moved_on = blend * (middle + STEP_FINE * rate)
                if keep:
                    moved_on = keep * level_in[major, rows] + moved_on
                target[major, rows] = moved_on
            return carry

        lax.fori_loop(0, majors, one, 0)

    section(level_in, stage_one, 0.0, 1.0)
    section(stage_one, stage_two, 0.75, 0.25)
    section(stage_two, stage_one, 1.0 / 3.0, 2.0 / 3.0)

    pltpu.make_async_copy(marks_in, marks_in, take_sems.at[2]).wait()
    mark_from = lax.broadcasted_iota(jnp.int32, (LANES, LANES), 0)
    mark_to = lanes_of((LANES, LANES))
    tile_z = plan["tile_z"]
    tile_count = fine_z // tile_z
    inside = pl.ds(offset, body)
    spread_band = (mark_from == (mark_to % fine_z) // tile_z).astype(jnp.float32)
    for part in range(halves):
        marks = marks_in[part]
        band = jnp.dot(marks, spread_band, preferred_element_type=jnp.float32)
        for pair in range(pairs):
            pick = jnp.logical_and(
                mark_from == tile_count + 2 * pair + mark_to // fine_z, mark_to % fine_z == 0
            ).astype(jnp.float32)
            phase = jnp.dot(marks, pick, preferred_element_type=jnp.float32)
            major = part * pairs + pair
            banded = jnp.where(band > 0.5, stage_one[major, inside], level_in[major, inside])
            shaped[major] = jnp.where(
                phase > 1.5, SPREAD, jnp.where(phase > 0.5, -SPREAD, banded)
            )

    low_half = lanes_of((body, LANES)) < fine_z

    def x_slope(ref, major):
        here = pltpu.roll(ref[major], fine_z, 1)
        up = pltpu.roll(ref[(major + 1) % majors], fine_z, 1)
        down = pltpu.roll(ref[(major + majors - 1) % majors], fine_z, 1)
        return 0.5 * (jnp.where(low_half, here, up) - jnp.where(low_half, down, here))

    for major in range(majors):
        level = shaped[major]
        slope_x = x_slope(shaped, major)
        slope_y = 0.5 * (along_rows(level, 1) - along_rows(level, -1))
        slope_z = 0.5 * (along_z(level, 1, fine_z) - along_z(level, -1, fine_z))
        inverse = lax.rsqrt(slope_x * slope_x + slope_y * slope_y + slope_z * slope_z + 1.0)
        normals[0, major] = slope_x * inverse
        normals[1, major] = slope_y * inverse
        normals[2, major] = slope_z * inverse

    core = slice(mark_margin, mark_margin + fine_chunk)
    for major in range(majors):
        normal_y, normal_z = normals[1, major], normals[2, major]
        curvature = x_slope(normals.at[0], major)
        curvature = curvature + 0.5 * (along_rows(normal_y, 1) - along_rows(normal_y, -1))
        curvature = curvature + 0.5 * (
            along_z(normal_z, 1, fine_z) - along_z(normal_z, -1, fine_z)
        )
        level = shaped[major]
        delta_peak = jnp.exp(level * level * (-1.0 / (2.0 * SPREAD * SPREAD)))
        strength = (SURFACE / (SPREAD * 2.5066282746310002)) * curvature * delta_peak
        lane_spot = slice(major * LANES, (major + 1) * LANES)
        for direction in range(3):
            force = (normals[direction, major] * strength)[core]
            packed[pl.ds(direction * fine_chunk, fine_chunk), lane_spot] = force
        fraction = (0.5 + 0.5 * jnp.tanh(level * (1.0 / SPREAD)))[core]
        packed[pl.ds(3 * fine_chunk, fine_chunk), lane_spot] = fraction

    fine_from = lax.broadcasted_iota(jnp.int32, (majors * LANES, LANES), 0)
    flow_to = lanes_of((majors * LANES, LANES))
    fold_lanes = (
        flow_to == (fine_from // LANES) * flow_z + (fine_from % fine_z) // 2
    ).astype(jnp.float32)
    folded = jnp.dot(
        packed[...], fold_lanes, precision=EXACT, preferred_element_type=jnp.float32
    )
    fold_shape = (4 * flow_chunk, 4 * fine_chunk)
    fold_rows = (
        lanes_of(fold_shape) // 2 == lax.broadcasted_iota(jnp.int32, fold_shape, 0)
    ).astype(jnp.float32)
    means = 0.125 * jnp.dot(
        fold_rows, folded, precision=EXACT, preferred_element_type=jnp.float32
    )
    for output in range(4):
        mean = means[output * flow_chunk : (output + 1) * flow_chunk]
        results[output] = moved[output] + STEP_FLOW * mean if output < 3 else mean

    landing = pl.ds(pl.multiple_of(mine * flow_chunk, flow_chunk), flow_chunk)
    for chunk in range(chunks):
        push(results.at[chunk // halves], gathered.at[landing], chunk, ring, 3)
    pltpu.make_async_copy(gathered, gathered, take_sems.at[3]).wait()
    turned = gathered[...].T
    outcome = turned[:share]
    for part in range(1, halves):
        outcome = jnp.where(half == part, turned[part * share : (part + 1) * share], outcome)
    out_ref[...] = outcome
    for condition, copy in sent:
        if condition is None:
            copy.wait_send()
        else:
            pl.when(condition)(copy.wait_send)


def on_device_bricks(plan, flow_fields, level_set, band_tiles, nozzle_phase):
    flow_z, flow_x, flow_y = flow_fields.shape[1:]
    fine_z, fine_x, fine_y = level_set.shape[1:]
    groups, halves = plan["groups"], plan["halves"]
    chunks = groups * halves
    fine_chunk, flow_chunk = fine_y // chunks, flow_y // chunks
    tiles_z = band_tiles.shape[0]
    plan = dict(
        plan,
        fine_chunk=fine_chunk,
        flow_chunk=flow_chunk,
        fine_z=fine_z,
        flow_z=flow_z,
        tile_z=fine_z // tiles_z,
    )
    majors = fine_x // 2 * halves
    body = fine_chunk + 2 * ROWS
    tall = fine_chunk + 4 * ROWS
    vmem = pl.BlockSpec(memory_space=pltpu.VMEM)

    def room(*shape):
        return pltpu.VMEM(shape, jnp.float32)

    copies = 4 * chunks + 6
    result = pl.pallas_call(
        functools.partial(brick_kernel, plan),
        out_shape=jax.ShapeDtypeStruct((flow_x * flow_z, flow_y), jnp.float32),
        in_specs=[pl.BlockSpec(memory_space=pltpu.HBM)] * 4,
        out_specs=vmem,
        scratch_shapes=[
            room(flow_z, flow_x, flow_y),
            room(fine_z, fine_x, fine_y),
            pltpu.VMEM((band_tiles.shape[0], band_tiles.shape[2]), band_tiles.dtype),
            pltpu.VMEM(nozzle_phase.shape, nozzle_phase.dtype),
            room(flow_y, LANES),
            room(fine_x // 2, fine_y, LANES),
            room(fine_y, LANES),
            room(groups, halves, flow_chunk + 2 * ROWS, LANES),
            room(majors, tall, LANES),
            room(halves, body, LANES),
            room(3, majors, body, LANES),
            room(majors, tall, LANES),
            room(majors, tall, LANES),
            room(majors, body, LANES),
            room(3, majors, body, LANES),
            room(4 * fine_chunk, majors * LANES),
            room(4, flow_chunk, LANES),
            room(flow_y, LANES),
            pltpu.SemaphoreType.DMA((copies,)),
            pltpu.SemaphoreType.DMA((4,)),
            pltpu.SemaphoreType.DMA((4,)),
        ],
        compiler_params=pltpu.CompilerParams(
            collective_id=0, has_side_effects=True, vmem_limit_bytes=60 * 1024 * 1024
        ),
        name="jet_step",
    )(flow_fields[0], level_set[0], band_tiles[:, 0], nozzle_phase)
    return result.reshape(flow_x, flow_z, flow_y).transpose(1, 0, 2)[None]


def solution(mesh):
    placed = (
        P("grp", None, "gx", "gy"),
        P("grp", None, "gx", "gy"),
        P(None, "gx", "gy"),
        P("gx", "gy"),
    )
    plan = {"groups": mesh.shape["grp"], "halves": mesh.shape["gx"], "rings": mesh.shape["gy"]}

    def on_device(flow_fields, level_set, band_tiles, nozzle_phase):
        flow_z, flow_x, flow_y = flow_fields.shape[1:]
        chunks = plan["groups"] * plan["halves"]
        fits = (
            plan["halves"] * flow_x * flow_z == LANES
            and 2 * level_set.shape[1] == LANES
            and flow_y == LANES
            and flow_y % (chunks * 2 * ROWS) == 0
            and band_tiles.shape[1] == 1
            and plan["rings"] > 2
        )
        if fits:
            return on_device_bricks(plan, flow_fields, level_set, band_tiles, nozzle_phase)
        return on_device_general(flow_fields, level_set, band_tiles, nozzle_phase)

    return jax.shard_map(
        on_device, mesh=mesh, in_specs=placed, out_specs=P("grp", None, "gx", "gy"), check_vma=False
    )
```

```python
import functools

import jax
import jax.numpy as jnp
from jax import lax
from jax.experimental import pallas as pl
from jax.experimental.pallas import tpu as pltpu
from jax.sharding import PartitionSpec as P

SWEEPS = 3


WENO_EPS = 1e-06
STEP_FINE = 0.3
STEP_FLOW = 0.2
SURFACE = 6.0
SPREAD = 1.5
IMPLICIT = 0.5


def extended(block, sides, width):
    for axis, dim in sides:
        count = lax.axis_size(axis)
        forward = [(i, i + 1) for i in range(count - 1)]
        forward.append((count - 1, 0))
        backward = [(target, source) for source, target in forward]
        low = lax.ppermute(
            lax.slice_in_dim(block, block.shape[dim] - width, None, axis=dim), axis, forward
        )
        high = lax.ppermute(lax.slice_in_dim(block, 0, width, axis=dim), axis, backward)
        block = jnp.concatenate([low, block, high], axis=dim)
    return block


def weno_side(diff_one, diff_two, diff_three, diff_four, diff_five):
    cand_one = diff_one / 3.0 - 7.0 * diff_two / 6.0 + 11.0 * diff_three / 6.0
    cand_two = -diff_two / 6.0 + 5.0 * diff_three / 6.0 + diff_four / 3.0
    cand_three = diff_three / 3.0 + 5.0 * diff_four / 6.0 - diff_five / 6.0
    curve_one = diff_one - 2.0 * diff_two + diff_three
    slope_one = diff_one - 4.0 * diff_two + 3.0 * diff_three
    smooth_one = 13.0 / 12.0 * curve_one * curve_one + 0.25 * slope_one * slope_one
    curve_two = diff_two - 2.0 * diff_three + diff_four
    slope_two = diff_two - diff_four
    smooth_two = 13.0 / 12.0 * curve_two * curve_two + 0.25 * slope_two * slope_two
    curve_three = diff_three - 2.0 * diff_four + diff_five
    slope_three = 3.0 * diff_three - 4.0 * diff_four + diff_five
    smooth_three = 13.0 / 12.0 * curve_three * curve_three + 0.25 * slope_three * slope_three
    weight_one = 0.1 / ((WENO_EPS + smooth_one) * (WENO_EPS + smooth_one))
    weight_two = 0.6 / ((WENO_EPS + smooth_two) * (WENO_EPS + smooth_two))
    weight_three = 0.3 / ((WENO_EPS + smooth_three) * (WENO_EPS + smooth_three))
    return (weight_one * cand_one + weight_two * cand_two + weight_three * cand_three) / (
        weight_one + weight_two + weight_three
    )


def section_rate(padded, speeds, plane_rim):
    plane_count = padded.shape[0] - 2 * plane_rim
    row_count = padded.shape[1] - 6
    col_count = padded.shape[2] - 6

    def sample(offset, direction):
        if direction == 0:
            return padded[
                3 + offset : 3 + offset + plane_count, 3 : 3 + row_count, 3 : 3 + col_count
            ]
        if direction == 1:
            return padded[
                plane_rim : plane_rim + plane_count,
                3 + offset : 3 + offset + row_count,
                3 : 3 + col_count,
            ]
        return padded[
            plane_rim : plane_rim + plane_count,
            3 : 3 + row_count,
            3 + offset : 3 + offset + col_count,
        ]

    summed = jnp.zeros((plane_count, row_count, col_count), jnp.float32)
    for direction in range(3):
        differences = [
            sample(offset + 1, direction) - sample(offset, direction) for offset in range(-3, 3)
        ]
        minus_side = weno_side(
            differences[0], differences[1], differences[2], differences[3], differences[4]
        )
        plus_side = weno_side(
            differences[5], differences[4], differences[3], differences[2], differences[1]
        )
        upwind = jnp.where(speeds[direction] >= 0.0, minus_side, plus_side)
        summed = summed - speeds[direction] * upwind
    return summed


def refine(coarse):
    plane_count, height, breadth = coarse.shape
    spread_out = jnp.broadcast_to(
        coarse[:, None, :, None, :, None], (plane_count, 2, height, 2, breadth, 2)
    )
    return spread_out.reshape(2 * plane_count, 2 * height, 2 * breadth)


def coarsen(fine_field):
    plane_count, height, breadth = fine_field.shape
    blocks = fine_field.reshape(plane_count // 2, 2, height // 2, 2, breadth // 2, 2)
    return jnp.sum(blocks, axis=(1, 3, 5)) * 0.125


def band_cells(tile_flags):
    planes, height, breadth = tile_flags.shape
    spread_out = jnp.broadcast_to(
        tile_flags[:, None, :, None, :, None], (planes, 8, height, 4, breadth, 16)
    )
    return spread_out.reshape(planes * 8, height * 4, breadth * 16)


def with_nozzle(banded, phases):
    inflow = jnp.where(phases == 2, 1.5, jnp.where(phases == 1, -1.5, banded[0]))
    return jnp.concatenate([inflow[None], banded[1:]], axis=0)


def surface_finish(normal_x, normal_y, normal_z, curvature, surface_level):
    delta_peak = jnp.exp(-surface_level * surface_level / (2.0 * SPREAD * SPREAD)) / (
        SPREAD * 2.5066282746310002
    )
    strength = SURFACE * curvature * delta_peak
    fraction = 0.5 + 0.5 * jnp.tanh(surface_level / SPREAD)
    return jnp.stack(
        [
            coarsen(normal_x * strength),
            coarsen(normal_y * strength),
            coarsen(normal_z * strength),
            coarsen(fraction),
        ]
    )


def surface_slab(padded):
    grad_x = (padded[1:-1, 2:, 1:-1] - padded[1:-1, :-2, 1:-1]) * 0.5
    grad_y = (padded[1:-1, 1:-1, 2:] - padded[1:-1, 1:-1, :-2]) * 0.5
    grad_z = (padded[2:, 1:-1, 1:-1] - padded[:-2, 1:-1, 1:-1]) * 0.5
    inverse = 1.0 / jnp.sqrt(grad_x * grad_x + grad_y * grad_y + grad_z * grad_z + 1.0)
    normal_x = grad_x * inverse
    normal_y = grad_y * inverse
    normal_z = grad_z * inverse
    curvature = (normal_x[1:-1, 2:, 1:-1] - normal_x[1:-1, :-2, 1:-1]) * 0.5
    curvature = curvature + (normal_y[1:-1, 1:-1, 2:] - normal_y[1:-1, 1:-1, :-2]) * 0.5
    curvature = curvature + (normal_z[2:, 1:-1, 1:-1] - normal_z[:-2, 1:-1, 1:-1]) * 0.5
    return surface_finish(
        normal_x[1:-1, 1:-1, 1:-1],
        normal_y[1:-1, 1:-1, 1:-1],
        normal_z[1:-1, 1:-1, 1:-1],
        curvature,
        padded[2:-2, 2:-2, 2:-2],
    )


def centered(padded, direction):
    if direction == 0:
        middle = padded[:, 1:-1, 1:-1]
        return (jnp.roll(middle, -1, 0) - jnp.roll(middle, 1, 0)) * 0.5
    if direction == 1:
        return (padded[:, 2:, 1:-1] - padded[:, :-2, 1:-1]) * 0.5
    return (padded[:, 1:-1, 2:] - padded[:, 1:-1, :-2]) * 0.5


def predictor(padded_fields, component):
    moving = lax.dynamic_index_in_dim(padded_fields, component, 0, keepdims=False)
    inner_u = padded_fields[0, :, 1:-1, 1:-1]
    inner_v = padded_fields[1, :, 1:-1, 1:-1]
    inner_w = padded_fields[2, :, 1:-1, 1:-1]
    advect = -(
        inner_w * centered(moving, 0)
        + inner_u * centered(moving, 1)
        + inner_v * centered(moving, 2)
    )
    pressure = padded_fields[3]
    gradients = jnp.stack([centered(pressure, 1), centered(pressure, 2), centered(pressure, 0)])
    pushed = lax.dynamic_index_in_dim(gradients, component, 0, keepdims=False)
    return moving[:, 1:-1, 1:-1] + STEP_FLOW * (advect - pushed)


def sweep_once(padded, source):
    middle = padded[:, 1:-1, 1:-1]
    beside_all = (
        padded[:, 2:, 1:-1] + padded[:, :-2, 1:-1] + padded[:, 1:-1, 2:] + padded[:, 1:-1, :-2]
    )
    beside_all = beside_all + jnp.roll(middle, -1, 0) + jnp.roll(middle, 1, 0)
    return (source + IMPLICIT * beside_all) / (1.0 + 6.0 * IMPLICIT)


def spread_surface(level_set, band_tiles, nozzle_phase, inner_fields, is_level, group):
    fine_all = level_set[0]
    initial = lax.psum_scatter(
        jnp.where(is_level, fine_all, jnp.zeros_like(fine_all)),
        "grp",
        scatter_dimension=0,
        tiled=True,
    )
    coarse_planes = inner_fields.shape[1] // 4
    flow_slab = lax.dynamic_slice_in_dim(inner_fields, group * coarse_planes, coarse_planes, 1)
    speeds = (refine(flow_slab[2]), refine(flow_slab[0]), refine(flow_slab[1]))

    def run_section(current, keep_weight, blend_weight):
        padded = extended(current, (("grp", 0), ("gx", 1), ("gy", 2)), 3)
        return keep_weight * initial + blend_weight * (
            current + STEP_FINE * section_rate(padded, speeds, 3)
        )

    first_section = run_section(initial, 0.0, 1.0)
    second_section = run_section(first_section, 0.75, 0.25)
    third_section = run_section(second_section, 1.0 / 3.0, 2.0 / 3.0)
    tile_planes = band_tiles.shape[0] // 4
    tiles_here = lax.dynamic_slice_in_dim(band_tiles, group * tile_planes, tile_planes, 0)
    banded = jnp.where(band_cells(tiles_here) == 1, third_section, initial)
    shaped = jnp.where(group == 0, with_nozzle(banded, nozzle_phase), banded)
    surface_pad = extended(shaped, (("grp", 0), ("gx", 1), ("gy", 2)), 2)
    quarter = surface_slab(surface_pad)
    received = lax.all_to_all(quarter, "grp", split_axis=0, concat_axis=1, tiled=True)
    return (received, received[0])


def on_device_general(flow_fields, level_set, band_tiles, nozzle_phase):
    group = lax.axis_index("grp")
    component = jnp.minimum(group, 2)
    is_level = group == 3
    gathered = lax.all_gather(flow_fields, "grp", axis=0, tiled=True)
    padded_fields = extended(gathered, (("gx", 2), ("gy", 3)), 1)
    source = predictor(padded_fields, component)
    inner_fields = padded_fields[:, :, 1:-1, 1:-1]
    received, fraction = spread_surface(
        level_set, band_tiles, nozzle_phase, inner_fields, is_level, group
    )
    pushed = received[0]
    relaxed = source
    for sweep_number in range(SWEEPS):
        padded = extended(relaxed, (("gx", 1), ("gy", 2)), 1)
        relaxed = sweep_once(padded, source)
    updated = relaxed + STEP_FLOW * pushed
    result = jnp.where(is_level, fraction, updated)
    return result[None]


MESH = pl.DeviceIdType.MESH
LANES = 128
ROWS = 8
EXACT = lax.Precision.HIGHEST


def lanes_of(shape, dim=1):
    return lax.broadcasted_iota(jnp.int32, shape, dim)


def along_z(block, offset, period):
    spot = lanes_of(block.shape) % period
    plain = pltpu.roll(block, (-offset) % LANES, 1)
    if offset > 0:
        around = pltpu.roll(block, (period - offset) % LANES, 1)
        return jnp.where(spot < period - offset, plain, around)
    around = pltpu.roll(block, (-period - offset) % LANES, 1)
    return jnp.where(spot >= -offset, plain, around)


def along_rows(block, offset):
    return pltpu.roll(block, (-offset) % block.shape[0], 0)


def inverse_of(block):
    rough = pl.reciprocal(block, approx=True)
    return rough * (2.0 - block * rough)


def weno_flux(bends, near, speed, forward, pace):
    step_a = jnp.where(forward, bends[0], bends[4])
    step_b = jnp.where(forward, bends[1], bends[3])
    step_c = bends[2]
    step_d = jnp.where(forward, bends[3], bends[1])
    three = jnp.where(forward, near[0], near[1])

    def weight(curve, slope):
        inverse = inverse_of(
            (WENO_EPS * 12.0 / 13.0) + curve * curve + (3.0 / 13.0) * (slope * slope)
        )
        return inverse * inverse

    triple_c = 3.0 * step_c
    weight_one = weight(step_b - step_a, 3.0 * step_b - step_a)
    weight_two = 6.0 * weight(step_c - step_b, step_c + step_b)
    weight_three = 3.0 * weight(step_d - step_c, triple_c - step_d)
    mixed = (
        weight_one * (5.0 * step_b - 2.0 * step_a)
        + weight_two * (step_b + 2.0 * step_c)
        + weight_three * (step_c + triple_c - step_d)
    )
    total = weight_one + weight_two + weight_three
    return speed * three + (pace * mixed) * inverse_of(total)


def window(index, count, chunk, margin):
    low = index * chunk - margin
    high = (index + 1) * chunk + margin
    start, stop = max(low, 0), min(high, count * chunk)
    return start, stop - start, start - low


def brick_kernel(
    plan,
    flow_far,
    level_far,
    band_far,
    phase_far,
    out_ref,
    flow_ref,
    level_ref,
    band_ref,
    phase_ref,
    flow_turned,
    level_turned,
    marks_turned,
    flow_in,
    level_in,
    marks_in,
    speeds,
    stage_one,
    stage_two,
    shaped,
    normals,
    packed,
    results,
    gathered,
    send_sems,
    take_sems,
    load_sems,
):
    groups, halves, rings = plan["groups"], plan["halves"], plan["rings"]
    chunks = groups * halves
    fine_chunk, flow_chunk = plan["fine_chunk"], plan["flow_chunk"]
    fine_z, flow_z = plan["fine_z"], plan["flow_z"]
    fine_margin, mark_margin, flow_margin = 2 * ROWS, ROWS, ROWS
    fine_rows, flow_rows = chunks * fine_chunk, chunks * flow_chunk
    pairs = level_ref.shape[1] // 2
    majors = pairs * halves
    group = lax.axis_index("grp")
    half = lax.axis_index("gx")
    ring = lax.axis_index("gy")
    after = lax.rem(ring + 1, rings)
    before = lax.rem(ring + rings - 1, rings)
    mine = group * halves + half
    last = chunks - 1

    holder = group == groups - 1
    load_level = pltpu.make_async_copy(level_far, level_ref, load_sems.at[0])
    load_flow = pltpu.make_async_copy(flow_far, flow_ref, load_sems.at[1])
    load_band = pltpu.make_async_copy(band_far, band_ref, load_sems.at[2])
    load_phase = pltpu.make_async_copy(phase_far, phase_ref, load_sems.at[3])
    pl.when(holder)(load_level.start)
    load_flow.start()
    load_band.start()
    load_phase.start()

    barrier = pltpu.get_barrier_semaphore()

    def greet(target_group, target_half, target_ring):
        pl.semaphore_signal(
            barrier,
            inc=1,
            device_id=(target_group, target_half, target_ring),
            device_id_type=MESH,
        )

    for chunk in range(chunks):
        tg, th = chunk // halves, chunk % halves

        @pl.when(mine != chunk)
        def _(tg=tg, th=th):
            greet(tg, th, ring)

        @pl.when(mine == 0)
        def _(tg=tg, th=th):
            greet(tg, th, before)

        @pl.when(mine == last)
        def _(tg=tg, th=th):
            greet(tg, th, after)

    @pl.when(holder)
    def _():
        load_level.wait()
        for pair in range(pairs):
            both = [level_ref[:, 2 * pair], level_ref[:, 2 * pair + 1]]
            level_turned[pair] = jnp.concatenate(both, axis=0).T

    load_flow.wait()
    columns = [flow_ref[:, column] for column in range(flow_ref.shape[1])]
    flow_turned[...] = jnp.concatenate(columns * halves, axis=0).T
    load_band.wait()
    load_phase.wait()
    tiles_z, tiles_y = band_ref.shape
    wide_shape = (tiles_y, fine_rows)
    widen = (
        lanes_of(wide_shape) // (fine_rows // tiles_y)
        == lax.broadcasted_iota(jnp.int32, wide_shape, 0)
    ).astype(jnp.float32)
    wide_band = jnp.dot(
        band_ref[...].astype(jnp.float32), widen, preferred_element_type=jnp.float32
    )
    spare = LANES - tiles_z - phase_ref.shape[0]
    marks_turned[...] = jnp.concatenate(
        [
            wide_band,
            phase_ref[...].astype(jnp.float32),
            jnp.zeros((spare, fine_rows), jnp.float32),
        ],
        axis=0,
    ).T

    pl.semaphore_wait(barrier, chunks + 1)

    sent = []

    def push(source, target, chunk, ring_to, take, condition=None):
        tg, th = chunk // halves, chunk % halves
        slot = len(sent)
        remote = pltpu.make_async_remote_copy(
            src_ref=source,
            dst_ref=target,
            send_sem=send_sems.at[slot],
            recv_sem=take_sems.at[take],
            device_id=(tg, th, ring_to),
            device_id_type=MESH,
        )
        near = ring_to is ring
        far = mine != chunk if near else None
        if condition is not None:
            far = condition if far is None else jnp.logical_and(condition, far)
        if near:
            here = mine == chunk
            if condition is not None:
                here = jnp.logical_and(condition, here)

            @pl.when(here)
            def _():
                pltpu.make_async_copy(source, target, take_sems.at[take]).start()

        if far is None:
            remote.start()
        else:
            pl.when(far)(remote.start)
        sent.append((far, remote))

    major_spot = pl.ds(half * pairs, pairs)
    for chunk in range(chunks):
        start, count, spot = window(chunk, chunks, fine_chunk, fine_margin)
        push(
            level_turned.at[:, pl.ds(start, count)],
            level_in.at[major_spot, pl.ds(spot, count)],
            chunk,
            ring,
            0,
            holder,
        )
    push(
        level_turned.at[:, pl.ds(fine_rows - fine_margin, fine_margin)],
        level_in.at[major_spot, pl.ds(0, fine_margin)],
        0,
        after,
        0,
        holder,
    )
    push(
        level_turned.at[:, pl.ds(0, fine_margin)],
        level_in.at[major_spot, pl.ds(fine_margin + fine_chunk, fine_margin)],
        last,
        before,
        0,
        holder,
    )
    for chunk in range(chunks):
        start, count, spot = window(chunk, chunks, flow_chunk, flow_margin)
        push(
            flow_turned.at[pl.ds(start, count)],
            flow_in.at[group, half, pl.ds(spot, count)],
            chunk,
            ring,
            1,
        )
    push(
        flow_turned.at[pl.ds(flow_rows - flow_margin, flow_margin)],
        flow_in.at[group, half, pl.ds(0, flow_margin)],
        0,
        after,
        1,
    )
    push(
        flow_turned.at[pl.ds(0, flow_margin)],
        flow_in.at[group, half, pl.ds(flow_margin + flow_chunk, flow_margin)],
        last,
        before,
        1,
    )
    for chunk in range(chunks):
        start, count, spot = window(chunk, chunks, fine_chunk, mark_margin)
        push(
            marks_turned.at[pl.ds(start, count)],
            marks_in.at[half, pl.ds(spot, count)],
            chunk,
            ring,
            2,
            group == chunk // halves,
        )
    push(
        marks_turned.at[pl.ds(fine_rows - mark_margin, mark_margin)],
        marks_in.at[half, pl.ds(0, mark_margin)],
        0,
        after,
        2,
        group == 0,
    )
    push(
        marks_turned.at[pl.ds(0, mark_margin)],
        marks_in.at[half, pl.ds(mark_margin + fine_chunk, mark_margin)],
        last,
        before,
        2,
        group == groups - 1,
    )

    body = fine_chunk + 2 * mark_margin
    offset = fine_margin - mark_margin
    edge = jnp.zeros((majors, offset, LANES), jnp.float32)
    for stage in (stage_one, stage_two):
        stage[:, pl.ds(0, offset)] = edge
        stage[:, pl.ds(offset + body, offset)] = edge

    pltpu.make_async_copy(flow_in, flow_in, take_sems.at[1]).wait()
    share = LANES // halves
    fields = []
    flow_lane = lanes_of((flow_chunk + 2 * flow_margin, LANES))
    for field in range(groups):
        merged = flow_in[field, 0]
        for part in range(1, halves):
            merged = jnp.where(flow_lane >= part * share, flow_in[field, part], merged)
        fields.append(merged)

    from_flow = lax.broadcasted_iota(jnp.int32, (LANES, majors * LANES), 0)
    to_fine = lanes_of((LANES, majors * LANES))
    fine_cell = (to_fine // LANES) * flow_z + (to_fine % fine_z) // 2
    spread_lanes = (from_flow == fine_cell).astype(jnp.float32)
    flow_window = flow_chunk + 2 * flow_margin
    spread_rows = (
        lanes_of((body, flow_window))
        == lax.broadcasted_iota(jnp.int32, (body, flow_window), 0) // 2
        + (flow_margin - mark_margin // 2)
    ).astype(jnp.float32)
    for direction in range(3):
        tall = jnp.dot(
            spread_rows, fields[direction], precision=EXACT, preferred_element_type=jnp.float32
        )
        wide = jnp.dot(tall, spread_lanes, precision=EXACT, preferred_element_type=jnp.float32)
        for major in range(majors):
            speeds[direction, major] = wide[:, major * LANES : (major + 1) * LANES]

    def flow_beside(block, direction, step):
        if direction == 0:
            return pltpu.roll(block, (-step * flow_z) % LANES, 1)
        if direction == 1:
            return along_rows(block, step)
        return along_z(block, step, flow_z)

    def flow_slope(block, direction):
        return 0.5 * (flow_beside(block, direction, 1) - flow_beside(block, direction, -1))

    moved = []
    for component in range(3):
        moving = fields[component]
        advect = fields[0] * flow_slope(moving, 0)
        advect = advect + fields[1] * flow_slope(moving, 1)
        advect = advect + fields[2] * flow_slope(moving, 2)
        source = moving - STEP_FLOW * (advect + flow_slope(fields[3], component))
        relaxed = source
        for sweep_number in range(SWEEPS):
            beside = jnp.zeros_like(relaxed)
            for direction in range(3):
                beside = beside + flow_beside(relaxed, direction, 1)
                beside = beside + flow_beside(relaxed, direction, -1)
            relaxed = (source + IMPLICIT * beside) * (1.0 / (1.0 + 6.0 * IMPLICIT))
        moved.append(relaxed[flow_margin : flow_margin + flow_chunk])

    pltpu.make_async_copy(level_in, level_in, take_sems.at[0]).wait()

    block_rows = 2 * ROWS

    def section(current, target, keep, blend):
        for start in range(0, body, block_rows):
            rows = pl.ds(offset + start, block_rows)
            span = pl.ds(start, block_rows + 2 * offset)
            here = pl.ds(start, block_rows)
            talls = [current[major, span] for major in range(majors)]
            whole = [tall[offset : offset + block_rows] for tall in talls]
            swapped = [pltpu.roll(block, fine_z, 1) for block in whole]
            low_half = lanes_of(whole[0].shape) < fine_z
            crossed = [
                jnp.where(low_half, swapped[major], swapped[(major + 1) % majors])
                for major in range(majors)
            ]
            rises = [crossed[major] - whole[major] for major in range(majors)]
            falls = [whole[(major + 1) % majors] - crossed[major] for major in range(majors)]
            humps = [falls[major] - rises[major] for major in range(majors)]
            dips = [rises[(major + 1) % majors] - falls[major] for major in range(majors)]
            for major in range(majors):
                middle = whole[major]
                rate = jnp.zeros_like(middle)
                for direction in range(3):
                    if direction == 0:
                        left, far = (major - 1) % majors, (major - 2) % majors
                        bends = [
                            dips[far],
                            humps[left],
                            dips[left],
                            humps[major],
                            dips[major],
                        ]
                        near = (falls[left], rises[major])
                    elif direction == 1:
                        tall = talls[major]
                        cells = [
                            tall[offset + step : offset + step + block_rows]
                            for step in range(-3, 4)
                        ]
                        diffs = [cells[i + 1] - cells[i] for i in range(6)]
                        bends = [diffs[i + 1] - diffs[i] for i in range(5)]
                        near = (diffs[2], diffs[3])
                    else:
                        first = along_z(middle, 1, fine_z) - middle
                        behind = along_z(first, -1, fine_z)
                        bend = first - behind
                        bends = [
                            along_z(bend, step, fine_z) if step else bend
                            for step in (-2, -1, 0, 1, 2)
                        ]
                        near = (behind, first)
                    speed = speeds[direction, major, here]
                    forward = speed >= 0.0
                    pace = jnp.abs(speed) * (1.0 / 6.0)
                    rate = rate - weno_flux(bends, near, speed, forward, pace)
                moved_on = blend * (middle + STEP_FINE * rate)
                if keep:
                    moved_on = keep * level_in[major, rows] + moved_on
                target[major, rows] = moved_on

    section(level_in, stage_one, 0.0, 1.0)
    section(stage_one, stage_two, 0.75, 0.25)
    section(stage_two, stage_one, 1.0 / 3.0, 2.0 / 3.0)

    pltpu.make_async_copy(marks_in, marks_in, take_sems.at[2]).wait()
    mark_from = lax.broadcasted_iota(jnp.int32, (LANES, LANES), 0)
    mark_to = lanes_of((LANES, LANES))
    tile_z = plan["tile_z"]
    tile_count = fine_z // tile_z
    inside = pl.ds(offset, body)
    spread_band = (mark_from == (mark_to % fine_z) // tile_z).astype(jnp.float32)
    for part in range(halves):
        marks = marks_in[part]
        band = jnp.dot(marks, spread_band, preferred_element_type=jnp.float32)
        for pair in range(pairs):
            pick = jnp.logical_and(
                mark_from == tile_count + 2 * pair + mark_to // fine_z, mark_to % fine_z == 0
            ).astype(jnp.float32)
            phase = jnp.dot(marks, pick, preferred_element_type=jnp.float32)
            major = part * pairs + pair
            banded = jnp.where(band > 0.5, stage_one[major, inside], level_in[major, inside])
            shaped[major] = jnp.where(
                phase > 1.5, SPREAD, jnp.where(phase > 0.5, -SPREAD, banded)
            )

    low_half = lanes_of((body, LANES)) < fine_z

    def x_slope(ref, major):
        here = pltpu.roll(ref[major], fine_z, 1)
        up = pltpu.roll(ref[(major + 1) % majors], fine_z, 1)
        down = pltpu.roll(ref[(major + majors - 1) % majors], fine_z, 1)
        return 0.5 * (jnp.where(low_half, here, up) - jnp.where(low_half, down, here))

    for major in range(majors):
        level = shaped[major]
        slope_x = x_slope(shaped, major)
        slope_y = 0.5 * (along_rows(level, 1) - along_rows(level, -1))
        slope_z = 0.5 * (along_z(level, 1, fine_z) - along_z(level, -1, fine_z))
        inverse = lax.rsqrt(slope_x * slope_x + slope_y * slope_y + slope_z * slope_z + 1.0)
        normals[0, major] = slope_x * inverse
        normals[1, major] = slope_y * inverse
        normals[2, major] = slope_z * inverse

    core = slice(mark_margin, mark_margin + fine_chunk)
    for major in range(majors):
        normal_y, normal_z = normals[1, major], normals[2, major]
        curvature = x_slope(normals.at[0], major)
        curvature = curvature + 0.5 * (along_rows(normal_y, 1) - along_rows(normal_y, -1))
        curvature = curvature + 0.5 * (
            along_z(normal_z, 1, fine_z) - along_z(normal_z, -1, fine_z)
        )
        level = shaped[major]
        delta_peak = jnp.exp(level * level * (-1.0 / (2.0 * SPREAD * SPREAD)))
        strength = (SURFACE / (SPREAD * 2.5066282746310002)) * curvature * delta_peak
        lane_spot = slice(major * LANES, (major + 1) * LANES)
        for direction in range(3):
            force = (normals[direction, major] * strength)[core]
            packed[pl.ds(direction * fine_chunk, fine_chunk), lane_spot] = force
        fraction = (0.5 + 0.5 * jnp.tanh(level * (1.0 / SPREAD)))[core]
        packed[pl.ds(3 * fine_chunk, fine_chunk), lane_spot] = fraction

    fine_from = lax.broadcasted_iota(jnp.int32, (majors * LANES, LANES), 0)
    flow_to = lanes_of((majors * LANES, LANES))
    fold_lanes = (
        flow_to == (fine_from // LANES) * flow_z + (fine_from % fine_z) // 2
    ).astype(jnp.float32)
    folded = jnp.dot(
        packed[...], fold_lanes, precision=EXACT, preferred_element_type=jnp.float32
    )
    fold_shape = (4 * flow_chunk, 4 * fine_chunk)
    fold_rows = (
        lanes_of(fold_shape) // 2 == lax.broadcasted_iota(jnp.int32, fold_shape, 0)
    ).astype(jnp.float32)
    means = 0.125 * jnp.dot(
        fold_rows, folded, precision=EXACT, preferred_element_type=jnp.float32
    )
    for output in range(4):
        mean = means[output * flow_chunk : (output + 1) * flow_chunk]
        results[output] = moved[output] + STEP_FLOW * mean if output < 3 else mean

    landing = pl.ds(pl.multiple_of(mine * flow_chunk, flow_chunk), flow_chunk)
    for chunk in range(chunks):
        push(results.at[chunk // halves], gathered.at[landing], chunk, ring, 3)
    pltpu.make_async_copy(gathered, gathered, take_sems.at[3]).wait()
    turned = gathered[...].T
    outcome = turned[:share]
    for part in range(1, halves):
        outcome = jnp.where(half == part, turned[part * share : (part + 1) * share], outcome)
    depth = share // out_ref.shape[1]
    for column in range(out_ref.shape[1]):
        out_ref[:, column] = outcome[column * depth : (column + 1) * depth]
    for condition, copy in sent:
        if condition is None:
            copy.wait_send()
        else:
            pl.when(condition)(copy.wait_send)


def on_device_bricks(plan, flow_fields, level_set, band_tiles, nozzle_phase):
    flow_z, flow_x, flow_y = flow_fields.shape[1:]
    fine_z, fine_x, fine_y = level_set.shape[1:]
    groups, halves = plan["groups"], plan["halves"]
    chunks = groups * halves
    fine_chunk, flow_chunk = fine_y // chunks, flow_y // chunks
    tiles_z = band_tiles.shape[0]
    plan = dict(
        plan,
        fine_chunk=fine_chunk,
        flow_chunk=flow_chunk,
        fine_z=fine_z,
        flow_z=flow_z,
        tile_z=fine_z // tiles_z,
    )
    majors = fine_x // 2 * halves
    body = fine_chunk + 2 * ROWS
    tall = fine_chunk + 4 * ROWS
    vmem = pl.BlockSpec(memory_space=pltpu.VMEM)

    def room(*shape):
        return pltpu.VMEM(shape, jnp.float32)

    copies = 4 * chunks + 6
    result = pl.pallas_call(
        functools.partial(brick_kernel, plan),
        out_shape=jax.ShapeDtypeStruct((flow_z, flow_x, flow_y), jnp.float32),
        in_specs=[pl.BlockSpec(memory_space=pltpu.HBM)] * 4,
        out_specs=vmem,
        scratch_shapes=[
            room(flow_z, flow_x, flow_y),
            room(fine_z, fine_x, fine_y),
            pltpu.VMEM((band_tiles.shape[0], band_tiles.shape[2]), band_tiles.dtype),
            pltpu.VMEM(nozzle_phase.shape, nozzle_phase.dtype),
            room(flow_y, LANES),
            room(fine_x // 2, fine_y, LANES),
            room(fine_y, LANES),
            room(groups, halves, flow_chunk + 2 * ROWS, LANES),
            room(majors, tall, LANES),
            room(halves, body, LANES),
            room(3, majors, body, LANES),
            room(majors, tall, LANES),
            room(majors, tall, LANES),
            room(majors, body, LANES),
            room(3, majors, body, LANES),
            room(4 * fine_chunk, majors * LANES),
            room(4, flow_chunk, LANES),
            room(flow_y, LANES),
            pltpu.SemaphoreType.DMA((copies,)),
            pltpu.SemaphoreType.DMA((4,)),
            pltpu.SemaphoreType.DMA((4,)),
        ],
        compiler_params=pltpu.CompilerParams(
            collective_id=0, has_side_effects=True, vmem_limit_bytes=60 * 1024 * 1024
        ),
        name="jet_step",
    )(flow_fields[0], level_set[0], band_tiles[:, 0], nozzle_phase)
    return result[None]


def solution(mesh):
    placed = (
        P("grp", None, "gx", "gy"),
        P("grp", None, "gx", "gy"),
        P(None, "gx", "gy"),
        P("gx", "gy"),
    )
    plan = {"groups": mesh.shape["grp"], "halves": mesh.shape["gx"], "rings": mesh.shape["gy"]}

    def on_device(flow_fields, level_set, band_tiles, nozzle_phase):
        flow_z, flow_x, flow_y = flow_fields.shape[1:]
        chunks = plan["groups"] * plan["halves"]
        fits = (
            plan["halves"] * flow_x * flow_z == LANES
            and 2 * level_set.shape[1] == LANES
            and flow_y == LANES
            and flow_y % (chunks * 2 * ROWS) == 0
            and band_tiles.shape[1] == 1
            and plan["rings"] > 2
        )
        if fits:
            return on_device_bricks(plan, flow_fields, level_set, band_tiles, nozzle_phase)
        return on_device_general(flow_fields, level_set, band_tiles, nozzle_phase)

    return jax.shard_map(
        on_device, mesh=mesh, in_specs=placed, out_specs=P("grp", None, "gx", "gy"), check_vma=False
    )
```

```python
import functools

import jax
import jax.numpy as jnp
from jax import lax
from jax.experimental import pallas as pl
from jax.experimental.pallas import tpu as pltpu
from jax.sharding import PartitionSpec as P

SWEEPS = 3


WENO_EPS = 1e-06
STEP_FINE = 0.3
STEP_FLOW = 0.2
SURFACE = 6.0
SPREAD = 1.5
IMPLICIT = 0.5


def extended(block, sides, width):
    for axis, dim in sides:
        count = lax.axis_size(axis)
        forward = [(i, i + 1) for i in range(count - 1)]
        forward.append((count - 1, 0))
        backward = [(target, source) for source, target in forward]
        low = lax.ppermute(
            lax.slice_in_dim(block, block.shape[dim] - width, None, axis=dim), axis, forward
        )
        high = lax.ppermute(lax.slice_in_dim(block, 0, width, axis=dim), axis, backward)
        block = jnp.concatenate([low, block, high], axis=dim)
    return block


def weno_side(diff_one, diff_two, diff_three, diff_four, diff_five):
    cand_one = diff_one / 3.0 - 7.0 * diff_two / 6.0 + 11.0 * diff_three / 6.0
    cand_two = -diff_two / 6.0 + 5.0 * diff_three / 6.0 + diff_four / 3.0
    cand_three = diff_three / 3.0 + 5.0 * diff_four / 6.0 - diff_five / 6.0
    curve_one = diff_one - 2.0 * diff_two + diff_three
    slope_one = diff_one - 4.0 * diff_two + 3.0 * diff_three
    smooth_one = 13.0 / 12.0 * curve_one * curve_one + 0.25 * slope_one * slope_one
    curve_two = diff_two - 2.0 * diff_three + diff_four
    slope_two = diff_two - diff_four
    smooth_two = 13.0 / 12.0 * curve_two * curve_two + 0.25 * slope_two * slope_two
    curve_three = diff_three - 2.0 * diff_four + diff_five
    slope_three = 3.0 * diff_three - 4.0 * diff_four + diff_five
    smooth_three = 13.0 / 12.0 * curve_three * curve_three + 0.25 * slope_three * slope_three
    weight_one = 0.1 / ((WENO_EPS + smooth_one) * (WENO_EPS + smooth_one))
    weight_two = 0.6 / ((WENO_EPS + smooth_two) * (WENO_EPS + smooth_two))
    weight_three = 0.3 / ((WENO_EPS + smooth_three) * (WENO_EPS + smooth_three))
    return (weight_one * cand_one + weight_two * cand_two + weight_three * cand_three) / (
        weight_one + weight_two + weight_three
    )


def section_rate(padded, speeds, plane_rim):
    plane_count = padded.shape[0] - 2 * plane_rim
    row_count = padded.shape[1] - 6
    col_count = padded.shape[2] - 6

    def sample(offset, direction):
        if direction == 0:
            return padded[
                3 + offset : 3 + offset + plane_count, 3 : 3 + row_count, 3 : 3 + col_count
            ]
        if direction == 1:
            return padded[
                plane_rim : plane_rim + plane_count,
                3 + offset : 3 + offset + row_count,
                3 : 3 + col_count,
            ]
        return padded[
            plane_rim : plane_rim + plane_count,
            3 : 3 + row_count,
            3 + offset : 3 + offset + col_count,
        ]

    summed = jnp.zeros((plane_count, row_count, col_count), jnp.float32)
    for direction in range(3):
        differences = [
            sample(offset + 1, direction) - sample(offset, direction) for offset in range(-3, 3)
        ]
        minus_side = weno_side(
            differences[0], differences[1], differences[2], differences[3], differences[4]
        )
        plus_side = weno_side(
            differences[5], differences[4], differences[3], differences[2], differences[1]
        )
        upwind = jnp.where(speeds[direction] >= 0.0, minus_side, plus_side)
        summed = summed - speeds[direction] * upwind
    return summed


def refine(coarse):
    plane_count, height, breadth = coarse.shape
    spread_out = jnp.broadcast_to(
        coarse[:, None, :, None, :, None], (plane_count, 2, height, 2, breadth, 2)
    )
    return spread_out.reshape(2 * plane_count, 2 * height, 2 * breadth)


def coarsen(fine_field):
    plane_count, height, breadth = fine_field.shape
    blocks = fine_field.reshape(plane_count // 2, 2, height // 2, 2, breadth // 2, 2)
    return jnp.sum(blocks, axis=(1, 3, 5)) * 0.125


def band_cells(tile_flags):
    planes, height, breadth = tile_flags.shape
    spread_out = jnp.broadcast_to(
        tile_flags[:, None, :, None, :, None], (planes, 8, height, 4, breadth, 16)
    )
    return spread_out.reshape(planes * 8, height * 4, breadth * 16)


def with_nozzle(banded, phases):
    inflow = jnp.where(phases == 2, 1.5, jnp.where(phases == 1, -1.5, banded[0]))
    return jnp.concatenate([inflow[None], banded[1:]], axis=0)


def surface_finish(normal_x, normal_y, normal_z, curvature, surface_level):
    delta_peak = jnp.exp(-surface_level * surface_level / (2.0 * SPREAD * SPREAD)) / (
        SPREAD * 2.5066282746310002
    )
    strength = SURFACE * curvature * delta_peak
    fraction = 0.5 + 0.5 * jnp.tanh(surface_level / SPREAD)
    return jnp.stack(
        [
            coarsen(normal_x * strength),
            coarsen(normal_y * strength),
            coarsen(normal_z * strength),
            coarsen(fraction),
        ]
    )


def surface_slab(padded):
    grad_x = (padded[1:-1, 2:, 1:-1] - padded[1:-1, :-2, 1:-1]) * 0.5
    grad_y = (padded[1:-1, 1:-1, 2:] - padded[1:-1, 1:-1, :-2]) * 0.5
    grad_z = (padded[2:, 1:-1, 1:-1] - padded[:-2, 1:-1, 1:-1]) * 0.5
    inverse = 1.0 / jnp.sqrt(grad_x * grad_x + grad_y * grad_y + grad_z * grad_z + 1.0)
    normal_x = grad_x * inverse
    normal_y = grad_y * inverse
    normal_z = grad_z * inverse
    curvature = (normal_x[1:-1, 2:, 1:-1] - normal_x[1:-1, :-2, 1:-1]) * 0.5
    curvature = curvature + (normal_y[1:-1, 1:-1, 2:] - normal_y[1:-1, 1:-1, :-2]) * 0.5
    curvature = curvature + (normal_z[2:, 1:-1, 1:-1] - normal_z[:-2, 1:-1, 1:-1]) * 0.5
    return surface_finish(
        normal_x[1:-1, 1:-1, 1:-1],
        normal_y[1:-1, 1:-1, 1:-1],
        normal_z[1:-1, 1:-1, 1:-1],
        curvature,
        padded[2:-2, 2:-2, 2:-2],
    )


def centered(padded, direction):
    if direction == 0:
        middle = padded[:, 1:-1, 1:-1]
        return (jnp.roll(middle, -1, 0) - jnp.roll(middle, 1, 0)) * 0.5
    if direction == 1:
        return (padded[:, 2:, 1:-1] - padded[:, :-2, 1:-1]) * 0.5
    return (padded[:, 1:-1, 2:] - padded[:, 1:-1, :-2]) * 0.5


def predictor(padded_fields, component):
    moving = lax.dynamic_index_in_dim(padded_fields, component, 0, keepdims=False)
    inner_u = padded_fields[0, :, 1:-1, 1:-1]
    inner_v = padded_fields[1, :, 1:-1, 1:-1]
    inner_w = padded_fields[2, :, 1:-1, 1:-1]
    advect = -(
        inner_w * centered(moving, 0)
        + inner_u * centered(moving, 1)
        + inner_v * centered(moving, 2)
    )
    pressure = padded_fields[3]
    gradients = jnp.stack([centered(pressure, 1), centered(pressure, 2), centered(pressure, 0)])
    pushed = lax.dynamic_index_in_dim(gradients, component, 0, keepdims=False)
    return moving[:, 1:-1, 1:-1] + STEP_FLOW * (advect - pushed)


def sweep_once(padded, source):
    middle = padded[:, 1:-1, 1:-1]
    beside_all = (
        padded[:, 2:, 1:-1] + padded[:, :-2, 1:-1] + padded[:, 1:-1, 2:] + padded[:, 1:-1, :-2]
    )
    beside_all = beside_all + jnp.roll(middle, -1, 0) + jnp.roll(middle, 1, 0)
    return (source + IMPLICIT * beside_all) / (1.0 + 6.0 * IMPLICIT)


def spread_surface(level_set, band_tiles, nozzle_phase, inner_fields, is_level, group):
    fine_all = level_set[0]
    initial = lax.psum_scatter(
        jnp.where(is_level, fine_all, jnp.zeros_like(fine_all)),
        "grp",
        scatter_dimension=0,
        tiled=True,
    )
    coarse_planes = inner_fields.shape[1] // 4
    flow_slab = lax.dynamic_slice_in_dim(inner_fields, group * coarse_planes, coarse_planes, 1)
    speeds = (refine(flow_slab[2]), refine(flow_slab[0]), refine(flow_slab[1]))

    def run_section(current, keep_weight, blend_weight):
        padded = extended(current, (("grp", 0), ("gx", 1), ("gy", 2)), 3)
        return keep_weight * initial + blend_weight * (
            current + STEP_FINE * section_rate(padded, speeds, 3)
        )

    first_section = run_section(initial, 0.0, 1.0)
    second_section = run_section(first_section, 0.75, 0.25)
    third_section = run_section(second_section, 1.0 / 3.0, 2.0 / 3.0)
    tile_planes = band_tiles.shape[0] // 4
    tiles_here = lax.dynamic_slice_in_dim(band_tiles, group * tile_planes, tile_planes, 0)
    banded = jnp.where(band_cells(tiles_here) == 1, third_section, initial)
    shaped = jnp.where(group == 0, with_nozzle(banded, nozzle_phase), banded)
    surface_pad = extended(shaped, (("grp", 0), ("gx", 1), ("gy", 2)), 2)
    quarter = surface_slab(surface_pad)
    received = lax.all_to_all(quarter, "grp", split_axis=0, concat_axis=1, tiled=True)
    return (received, received[0])


def on_device_general(flow_fields, level_set, band_tiles, nozzle_phase):
    group = lax.axis_index("grp")
    component = jnp.minimum(group, 2)
    is_level = group == 3
    gathered = lax.all_gather(flow_fields, "grp", axis=0, tiled=True)
    padded_fields = extended(gathered, (("gx", 2), ("gy", 3)), 1)
    source = predictor(padded_fields, component)
    inner_fields = padded_fields[:, :, 1:-1, 1:-1]
    received, fraction = spread_surface(
        level_set, band_tiles, nozzle_phase, inner_fields, is_level, group
    )
    pushed = received[0]
    relaxed = source
    for sweep_number in range(SWEEPS):
        padded = extended(relaxed, (("gx", 1), ("gy", 2)), 1)
        relaxed = sweep_once(padded, source)
    updated = relaxed + STEP_FLOW * pushed
    result = jnp.where(is_level, fraction, updated)
    return result[None]


MESH = pl.DeviceIdType.MESH
LANES = 128
ROWS = 8
EXACT = lax.Precision.HIGHEST


def lanes_of(shape, dim=1):
    return lax.broadcasted_iota(jnp.int32, shape, dim)


def along_z(block, offset, period):
    spot = lanes_of(block.shape) % period
    plain = pltpu.roll(block, (-offset) % LANES, 1)
    if offset > 0:
        around = pltpu.roll(block, (period - offset) % LANES, 1)
        return jnp.where(spot < period - offset, plain, around)
    around = pltpu.roll(block, (-period - offset) % LANES, 1)
    return jnp.where(spot >= -offset, plain, around)


def along_rows(block, offset):
    return pltpu.roll(block, (-offset) % block.shape[0], 0)


def inverse_of(block):
    rough = pl.reciprocal(block, approx=True)
    return rough * (2.0 - block * rough)


def weno_flux(bends, near, speed, forward, pace):
    step_a = jnp.where(forward, bends[0], bends[4])
    step_b = jnp.where(forward, bends[1], bends[3])
    step_c = bends[2]
    step_d = jnp.where(forward, bends[3], bends[1])
    three = jnp.where(forward, near[0], near[1])

    def weight(curve, slope):
        inverse = inverse_of(
            (WENO_EPS * 12.0 / 13.0) + curve * curve + (3.0 / 13.0) * (slope * slope)
        )
        return inverse * inverse

    triple_c = 3.0 * step_c
    weight_one = weight(step_b - step_a, 3.0 * step_b - step_a)
    weight_two = 6.0 * weight(step_c - step_b, step_c + step_b)
    weight_three = 3.0 * weight(step_d - step_c, triple_c - step_d)
    mixed = (
        weight_one * (5.0 * step_b - 2.0 * step_a)
        + weight_two * (step_b + 2.0 * step_c)
        + weight_three * (step_c + triple_c - step_d)
    )
    total = weight_one + weight_two + weight_three
    return speed * three + (pace * mixed) * inverse_of(total)


def brick_kernel(
    plan,
    flow_far,
    level_far,
    band_far,
    phase_far,
    out_ref,
    flow_ref,
    level_ref,
    band_ref,
    phase_ref,
    flow_turned,
    level_turned,
    marks_turned,
    flow_in,
    stages,
    marks_in,
    speeds,
    fields,
    pushes,
    shaped,
    normals,
    folded,
    results,
    gathered,
    send_sems,
    take_sems,
    load_sems,
):
    groups, halves, rings = plan["groups"], plan["halves"], plan["rings"]
    chunks = groups * halves
    fine_chunk, flow_chunk = plan["fine_chunk"], plan["flow_chunk"]
    fine_z, flow_z = plan["fine_z"], plan["flow_z"]
    fine_margin, mark_margin, flow_margin = 2 * ROWS, ROWS, ROWS
    fine_rows, flow_rows = chunks * fine_chunk, chunks * flow_chunk
    pairs = level_ref.shape[1] // 2
    majors = pairs * halves
    group = lax.axis_index("grp")
    half = lax.axis_index("gx")
    ring = lax.axis_index("gy")
    after = lax.rem(ring + 1, rings)
    before = lax.rem(ring + rings - 1, rings)
    mine = group * halves + half
    last = chunks - 1

    holder = group == groups - 1
    load_level = pltpu.make_async_copy(level_far, level_ref, load_sems.at[0])
    load_flow = pltpu.make_async_copy(flow_far, flow_ref, load_sems.at[1])
    load_band = pltpu.make_async_copy(band_far, band_ref, load_sems.at[2])
    load_phase = pltpu.make_async_copy(phase_far, phase_ref, load_sems.at[3])
    pl.when(holder)(load_level.start)
    load_flow.start()
    load_band.start()
    load_phase.start()

    barrier = pltpu.get_barrier_semaphore()

    def greet(target_group, target_half, target_ring):
        pl.semaphore_signal(
            barrier,
            inc=1,
            device_id=(target_group, target_half, target_ring),
            device_id_type=MESH,
        )

    def greet_all(chunk, carry):
        tg, th = chunk // halves, lax.rem(chunk, halves)

        @pl.when(mine != chunk)
        def _():
            greet(tg, th, ring)

        @pl.when(mine == 0)
        def _():
            greet(tg, th, before)

        @pl.when(mine == last)
        def _():
            greet(tg, th, after)

        return carry

    lax.fori_loop(0, chunks, greet_all, 0)

    @pl.when(holder)
    def _():
        load_level.wait()
        for pair in range(pairs):
            both = [level_ref[:, 2 * pair], level_ref[:, 2 * pair + 1]]
            level_turned[pair] = jnp.concatenate(both, axis=0).T

    load_flow.wait()
    columns = [flow_ref[:, column] for column in range(flow_ref.shape[1])]
    flow_turned[...] = jnp.concatenate(columns * halves, axis=0).T
    load_band.wait()
    load_phase.wait()
    tiles_z, tiles_y = band_ref.shape
    wide_shape = (tiles_y, fine_rows)
    widen = (
        lanes_of(wide_shape) // (fine_rows // tiles_y)
        == lax.broadcasted_iota(jnp.int32, wide_shape, 0)
    ).astype(jnp.float32)
    wide_band = jnp.dot(
        band_ref[...].astype(jnp.float32), widen, preferred_element_type=jnp.float32
    )
    spare = LANES - tiles_z - phase_ref.shape[0]
    marks_turned[...] = jnp.concatenate(
        [
            wide_band,
            phase_ref[...].astype(jnp.float32),
            jnp.zeros((spare, fine_rows), jnp.float32),
        ],
        axis=0,
    ).T

    pl.semaphore_wait(barrier, chunks + 1)

    def move(kind, slot, source, target, chunk, ring_to, condition, finish):
        tg, th = chunk // halves, lax.rem(chunk, halves)
        near = ring_to is ring
        far = jnp.logical_and(condition, mine != chunk) if near else condition
        remote = pltpu.make_async_remote_copy(
            src_ref=source,
            dst_ref=target,
            send_sem=send_sems.at[kind * (chunks + 2) + slot],
            recv_sem=take_sems.at[kind],
            device_id=(tg, th, ring_to),
            device_id_type=MESH,
        )
        pl.when(far)(remote.wait_send if finish else remote.start)
        if near and not finish:

            @pl.when(jnp.logical_and(condition, mine == chunk))
            def _():
                pltpu.make_async_copy(source, target, take_sems.at[kind]).start()

    def spread(kind, source, target, chunk_rows, margin, condition, finish):
        total = chunks * chunk_rows
        wide = chunk_rows + 2 * margin
        first, final = jnp.int32(0), jnp.int32(last)
        side = wide - margin
        move(
            kind,
            0,
            source(pl.ds(0, side)),
            target(pl.ds(margin, side)),
            first,
            ring,
            condition(first),
            finish,
        )

        def inner(chunk, carry):
            start = pl.multiple_of(chunk * chunk_rows - margin, ROWS)
            move(
                kind,
                chunk,
                source(pl.ds(start, wide)),
                target(pl.ds(0, wide)),
                chunk,
                ring,
                condition(chunk),
                finish,
            )
            return carry

        lax.fori_loop(1, last, inner, 0)
        move(
            kind,
            last,
            source(pl.ds(total - side, side)),
            target(pl.ds(0, side)),
            final,
            ring,
            condition(final),
            finish,
        )
        move(
            kind,
            chunks,
            source(pl.ds(total - margin, margin)),
            target(pl.ds(0, margin)),
            first,
            after,
            condition(first),
            finish,
        )
        move(
            kind,
            chunks + 1,
            source(pl.ds(0, margin)),
            target(pl.ds(margin + chunk_rows, margin)),
            final,
            before,
            condition(final),
            finish,
        )

    major_spot = pl.ds(half * pairs, pairs)

    def spread_level(finish):
        spread(
            0,
            lambda rows: level_turned.at[:, rows],
            lambda rows: stages.at[0, major_spot, rows],
            fine_chunk,
            fine_margin,
            lambda chunk: holder,
            finish,
        )

    def spread_flow(finish):
        spread(
            1,
            lambda rows: flow_turned.at[rows],
            lambda rows: flow_in.at[group, half, rows],
            flow_chunk,
            flow_margin,
            lambda chunk: group >= 0,
            finish,
        )

    def spread_marks(finish):
        spread(
            2,
            lambda rows: marks_turned.at[rows],
            lambda rows: marks_in.at[half, rows],
            fine_chunk,
            mark_margin,
            lambda chunk: group == chunk // halves,
            finish,
        )

    landing = pl.ds(pl.multiple_of(mine * flow_chunk, flow_chunk), flow_chunk)

    def spread_results(finish):
        def one(chunk, carry):
            move(
                3,
                chunk,
                results.at[chunk // halves],
                gathered.at[landing],
                chunk,
                ring,
                group >= 0,
                finish,
            )
            return carry

        lax.fori_loop(0, chunks, one, 0)

    pl.when(holder)(lambda: spread_level(False))
    spread_flow(False)
    spread_marks(False)

    body = fine_chunk + 2 * mark_margin
    offset = fine_margin - mark_margin
    edge = jnp.zeros((majors, offset, LANES), jnp.float32)
    for stage in (1, 2):
        stages[stage, :, pl.ds(0, offset)] = edge
        stages[stage, :, pl.ds(offset + body, offset)] = edge

    pltpu.make_async_copy(flow_in, flow_in, take_sems.at[1]).wait()
    share = LANES // halves
    flow_lane = lanes_of((flow_chunk + 2 * flow_margin, LANES))
    for field in range(groups):
        merged = flow_in[field, 0]
        for part in range(1, halves):
            merged = jnp.where(flow_lane >= part * share, flow_in[field, part], merged)
        fields[field] = merged

    from_flow = lax.broadcasted_iota(jnp.int32, (LANES, majors * LANES), 0)
    to_fine = lanes_of((LANES, majors * LANES))
    fine_cell = (to_fine // LANES) * flow_z + (to_fine % fine_z) // 2
    spread_lanes = (from_flow == fine_cell).astype(jnp.float32)
    flow_window = flow_chunk + 2 * flow_margin
    spread_rows = (
        lanes_of((body, flow_window))
        == lax.broadcasted_iota(jnp.int32, (body, flow_window), 0) // 2
        + (flow_margin - mark_margin // 2)
    ).astype(jnp.float32)

    def spread_speed(direction, carry):
        tall = jnp.dot(
            spread_rows, fields[direction], precision=EXACT, preferred_element_type=jnp.float32
        )
        wide = jnp.dot(tall, spread_lanes, precision=EXACT, preferred_element_type=jnp.float32)
        for major in range(majors):
            speeds[direction, major] = wide[:, major * LANES : (major + 1) * LANES]
        return carry

    lax.fori_loop(0, 3, spread_speed, 0)

    def flow_beside(block, direction, step):
        if direction == 0:
            return pltpu.roll(block, (-step * flow_z) % LANES, 1)
        if direction == 1:
            return along_rows(block, step)
        return along_z(block, step, flow_z)

    def flow_slope(block, direction):
        return 0.5 * (flow_beside(block, direction, 1) - flow_beside(block, direction, -1))

    for direction in range(3):
        pushes[direction] = flow_slope(fields[3], direction)

    def relax(component, carry):
        moving = fields[component]
        advect = fields[0] * flow_slope(moving, 0)
        advect = advect + fields[1] * flow_slope(moving, 1)
        advect = advect + fields[2] * flow_slope(moving, 2)
        source = moving - STEP_FLOW * (advect + pushes[component])

        def sweep(number, relaxed):
            beside = jnp.zeros_like(relaxed)
            for direction in range(3):
                beside = beside + flow_beside(relaxed, direction, 1)
                beside = beside + flow_beside(relaxed, direction, -1)
            return (source + IMPLICIT * beside) * (1.0 / (1.0 + 6.0 * IMPLICIT))

        relaxed = lax.fori_loop(0, SWEEPS, sweep, source)
        results[component] = relaxed[flow_margin : flow_margin + flow_chunk]
        return carry

    lax.fori_loop(0, 3, relax, 0)

    pltpu.make_async_copy(stages.at[0], stages.at[0], take_sems.at[0]).wait()

    block_rows = 2 * ROWS

    def section(number, carry):
        later = (number > 0).astype(jnp.float32)
        latest = (number > 1).astype(jnp.float32)
        keep = later * 0.75 - latest * (0.75 - 1.0 / 3.0)
        blend = 1.0 - keep

        def one(major, inner_carry):
            def far_major(step):
                return lax.rem(major + majors + step, majors)

            for start in range(0, body, block_rows):
                rows = pl.ds(offset + start, block_rows)
                tall = stages[number, major, pl.ds(start, block_rows + 2 * offset)]
                middle = tall[offset : offset + block_rows]
                low_half = lanes_of(middle.shape) < fine_z
                whole = {step: stages[number, far_major(step), rows] for step in (-2, -1, 1, 2)}
                whole[0] = middle
                swapped = {step: pltpu.roll(whole[step], fine_z, 1) for step in whole}

                def beside(direction, step):
                    if step == 0:
                        return middle
                    if direction == 1:
                        return tall[offset + step : offset + step + block_rows]
                    if direction == 2:
                        return along_z(middle, step, fine_z)
                    base = step // 2
                    if step % 2 == 0:
                        return whole[base]
                    return jnp.where(low_half, swapped[base], swapped[base + 1])

                rate = jnp.zeros_like(middle)
                for direction in range(3):
                    if direction == 2:
                        first = along_z(middle, 1, fine_z) - middle
                        behind = along_z(first, -1, fine_z)
                        bend = first - behind
                        bends = [
                            along_z(bend, step, fine_z) if step else bend
                            for step in (-2, -1, 0, 1, 2)
                        ]
                        near = (behind, first)
                    else:
                        cells = [beside(direction, step) for step in range(-3, 4)]
                        diffs = [cells[i + 1] - cells[i] for i in range(6)]
                        bends = [diffs[i + 1] - diffs[i] for i in range(5)]
                        near = (diffs[2], diffs[3])
                    speed = speeds[direction, major, pl.ds(start, block_rows)]
                    forward = speed >= 0.0
                    pace = jnp.abs(speed) * (1.0 / 6.0)
                    rate = rate - weno_flux(bends, near, speed, forward, pace)
                moved_on = blend * (middle + STEP_FINE * rate)
                stages[number + 1, major, rows] = keep * stages[0, major, rows] + moved_on
            return inner_carry

        lax.fori_loop(0, majors, one, 0)
        return carry

    lax.fori_loop(0, 3, section, 0)

    pltpu.make_async_copy(marks_in, marks_in, take_sems.at[2]).wait()
    mark_from = lax.broadcasted_iota(jnp.int32, (LANES, LANES), 0)
    mark_to = lanes_of((LANES, LANES))
    tile_z = plan["tile_z"]
    tile_count = fine_z // tile_z
    inside = pl.ds(offset, body)
    spread_band = (mark_from == (mark_to % fine_z) // tile_z).astype(jnp.float32)
    for part in range(halves):
        marks = marks_in[part]
        band = jnp.dot(marks, spread_band, preferred_element_type=jnp.float32)
        for pair in range(pairs):
            pick = jnp.logical_and(
                mark_from == tile_count + 2 * pair + mark_to // fine_z, mark_to % fine_z == 0
            ).astype(jnp.float32)
            phase = jnp.dot(marks, pick, preferred_element_type=jnp.float32)
            major = part * pairs + pair
            banded = jnp.where(band > 0.5, stages[3, major, inside], stages[0, major, inside])
            shaped[major] = jnp.where(
                phase > 1.5, SPREAD, jnp.where(phase > 0.5, -SPREAD, banded)
            )

    low_half = lanes_of((body, LANES)) < fine_z

    def x_slope(ref, major):
        here = pltpu.roll(ref[major], fine_z, 1)
        up = pltpu.roll(ref[lax.rem(major + 1, majors)], fine_z, 1)
        down = pltpu.roll(ref[lax.rem(major + majors - 1, majors)], fine_z, 1)
        return 0.5 * (jnp.where(low_half, here, up) - jnp.where(low_half, down, here))

    def steepness(major, carry):
        level = shaped[major]
        slope_x = x_slope(shaped, major)
        slope_y = 0.5 * (along_rows(level, 1) - along_rows(level, -1))
        slope_z = 0.5 * (along_z(level, 1, fine_z) - along_z(level, -1, fine_z))
        inverse = lax.rsqrt(slope_x * slope_x + slope_y * slope_y + slope_z * slope_z + 1.0)
        normals[0, major] = slope_x * inverse
        normals[1, major] = slope_y * inverse
        normals[2, major] = slope_z * inverse
        return carry

    lax.fori_loop(0, majors, steepness, 0)

    core = slice(mark_margin, mark_margin + fine_chunk)
    fine_from = lax.broadcasted_iota(jnp.int32, (LANES, LANES), 0) % fine_z // 2
    flow_to = lanes_of((LANES, LANES))
    folded[...] = jnp.zeros_like(folded)

    def tension(major, carry):
        normal_y, normal_z = normals[1, major], normals[2, major]
        curvature = x_slope(normals.at[0], major)
        curvature = curvature + 0.5 * (along_rows(normal_y, 1) - along_rows(normal_y, -1))
        curvature = curvature + 0.5 * (
            along_z(normal_z, 1, fine_z) - along_z(normal_z, -1, fine_z)
        )
        level = shaped[major]
        delta_peak = jnp.exp(level * level * (-1.0 / (2.0 * SPREAD * SPREAD)))
        strength = (SURFACE / (SPREAD * 2.5066282746310002)) * curvature * delta_peak
        terms = [(normals[direction, major] * strength)[core] for direction in range(3)]
        terms.append((0.5 + 0.5 * jnp.tanh(level * (1.0 / SPREAD)))[core])
        fold = (flow_to == major * flow_z + fine_from).astype(jnp.float32)
        folded[...] += jnp.dot(
            jnp.concatenate(terms, axis=0),
            fold,
            precision=EXACT,
            preferred_element_type=jnp.float32,
        )
        return carry

    lax.fori_loop(0, majors, tension, 0)

    fold_shape = (4 * flow_chunk, 4 * fine_chunk)
    fold_rows = (
        lanes_of(fold_shape) // 2 == lax.broadcasted_iota(jnp.int32, fold_shape, 0)
    ).astype(jnp.float32)
    means = 0.125 * jnp.dot(
        fold_rows, folded[...], precision=EXACT, preferred_element_type=jnp.float32
    )
    for output in range(4):
        mean = means[output * flow_chunk : (output + 1) * flow_chunk]
        results[output] = results[output] + STEP_FLOW * mean if output < 3 else mean

    spread_results(False)
    pltpu.make_async_copy(gathered, gathered, take_sems.at[3]).wait()
    turned = gathered[...].T
    outcome = turned[:share]
    for part in range(1, halves):
        outcome = jnp.where(half == part, turned[part * share : (part + 1) * share], outcome)
    out_ref[...] = outcome
    pl.when(holder)(lambda: spread_level(True))
    spread_flow(True)
    spread_marks(True)
    spread_results(True)


def on_device_bricks(plan, flow_fields, level_set, band_tiles, nozzle_phase):
    flow_z, flow_x, flow_y = flow_fields.shape[1:]
    fine_z, fine_x, fine_y = level_set.shape[1:]
    groups, halves = plan["groups"], plan["halves"]
    chunks = groups * halves
    fine_chunk, flow_chunk = fine_y // chunks, flow_y // chunks
    tiles_z = band_tiles.shape[0]
    plan = dict(
        plan,
        fine_chunk=fine_chunk,
        flow_chunk=flow_chunk,
        fine_z=fine_z,
        flow_z=flow_z,
        tile_z=fine_z // tiles_z,
    )
    majors = fine_x // 2 * halves
    body = fine_chunk + 2 * ROWS
    tall = fine_chunk + 4 * ROWS
    vmem = pl.BlockSpec(memory_space=pltpu.VMEM)

    def room(*shape):
        return pltpu.VMEM(shape, jnp.float32)

    copies = 4 * (chunks + 2)
    result = pl.pallas_call(
        functools.partial(brick_kernel, plan),
        out_shape=jax.ShapeDtypeStruct((flow_x * flow_z, flow_y), jnp.float32),
        in_specs=[pl.BlockSpec(memory_space=pltpu.HBM)] * 4,
        out_specs=vmem,
        scratch_shapes=[
            room(flow_z, flow_x, flow_y),
            room(fine_z, fine_x, fine_y),
            pltpu.VMEM((band_tiles.shape[0], band_tiles.shape[2]), band_tiles.dtype),
            pltpu.VMEM(nozzle_phase.shape, nozzle_phase.dtype),
            room(flow_y, LANES),
            room(fine_x // 2, fine_y, LANES),
            room(fine_y, LANES),
            room(groups, halves, flow_chunk + 2 * ROWS, LANES),
            room(4, majors, tall, LANES),
            room(halves, body, LANES),
            room(3, majors, body, LANES),
            room(groups, flow_chunk + 2 * ROWS, LANES),
            room(3, flow_chunk + 2 * ROWS, LANES),
            room(majors, body, LANES),
            room(3, majors, body, LANES),
            room(4 * fine_chunk, LANES),
            room(4, flow_chunk, LANES),
            room(flow_y, LANES),
            pltpu.SemaphoreType.DMA((copies,)),
            pltpu.SemaphoreType.DMA((4,)),
            pltpu.SemaphoreType.DMA((4,)),
        ],
        compiler_params=pltpu.CompilerParams(
            collective_id=0, has_side_effects=True, vmem_limit_bytes=60 * 1024 * 1024
        ),
        name="jet_step",
    )(flow_fields[0], level_set[0], band_tiles[:, 0], nozzle_phase)
    return result.reshape(flow_x, flow_z, flow_y).transpose(1, 0, 2)[None]


def solution(mesh):
    placed = (
        P("grp", None, "gx", "gy"),
        P("grp", None, "gx", "gy"),
        P(None, "gx", "gy"),
        P("gx", "gy"),
    )
    plan = {"groups": mesh.shape["grp"], "halves": mesh.shape["gx"], "rings": mesh.shape["gy"]}

    def on_device(flow_fields, level_set, band_tiles, nozzle_phase):
        flow_z, flow_x, flow_y = flow_fields.shape[1:]
        chunks = plan["groups"] * plan["halves"]
        fits = (
            plan["halves"] * flow_x * flow_z == LANES
            and 2 * level_set.shape[1] == LANES
            and flow_y == LANES
            and flow_y % (chunks * 2 * ROWS) == 0
            and band_tiles.shape[1] == 1
            and plan["rings"] > 2
        )
        if fits:
            return on_device_bricks(plan, flow_fields, level_set, band_tiles, nozzle_phase)
        return on_device_general(flow_fields, level_set, band_tiles, nozzle_phase)

    return jax.shard_map(
        on_device, mesh=mesh, in_specs=placed, out_specs=P("grp", None, "gx", "gy"), check_vma=False
    )
```

```python
import functools

import jax
import jax.numpy as jnp
from jax import lax
from jax.experimental import pallas as pl
from jax.experimental.pallas import tpu as pltpu
from jax.sharding import PartitionSpec as P

SWEEPS = 3


WENO_EPS = 1e-06
STEP_FINE = 0.3
STEP_FLOW = 0.2
SURFACE = 6.0
SPREAD = 1.5
IMPLICIT = 0.5


def extended(block, sides, width):
    for axis, dim in sides:
        count = lax.axis_size(axis)
        forward = [(i, i + 1) for i in range(count - 1)]
        forward.append((count - 1, 0))
        backward = [(target, source) for source, target in forward]
        low = lax.ppermute(
            lax.slice_in_dim(block, block.shape[dim] - width, None, axis=dim), axis, forward
        )
        high = lax.ppermute(lax.slice_in_dim(block, 0, width, axis=dim), axis, backward)
        block = jnp.concatenate([low, block, high], axis=dim)
    return block


def weno_side(diff_one, diff_two, diff_three, diff_four, diff_five):
    cand_one = diff_one / 3.0 - 7.0 * diff_two / 6.0 + 11.0 * diff_three / 6.0
    cand_two = -diff_two / 6.0 + 5.0 * diff_three / 6.0 + diff_four / 3.0
    cand_three = diff_three / 3.0 + 5.0 * diff_four / 6.0 - diff_five / 6.0
    curve_one = diff_one - 2.0 * diff_two + diff_three
    slope_one = diff_one - 4.0 * diff_two + 3.0 * diff_three
    smooth_one = 13.0 / 12.0 * curve_one * curve_one + 0.25 * slope_one * slope_one
    curve_two = diff_two - 2.0 * diff_three + diff_four
    slope_two = diff_two - diff_four
    smooth_two = 13.0 / 12.0 * curve_two * curve_two + 0.25 * slope_two * slope_two
    curve_three = diff_three - 2.0 * diff_four + diff_five
    slope_three = 3.0 * diff_three - 4.0 * diff_four + diff_five
    smooth_three = 13.0 / 12.0 * curve_three * curve_three + 0.25 * slope_three * slope_three
    weight_one = 0.1 / ((WENO_EPS + smooth_one) * (WENO_EPS + smooth_one))
    weight_two = 0.6 / ((WENO_EPS + smooth_two) * (WENO_EPS + smooth_two))
    weight_three = 0.3 / ((WENO_EPS + smooth_three) * (WENO_EPS + smooth_three))
    return (weight_one * cand_one + weight_two * cand_two + weight_three * cand_three) / (
        weight_one + weight_two + weight_three
    )


def section_rate(padded, speeds, plane_rim):
    plane_count = padded.shape[0] - 2 * plane_rim
    row_count = padded.shape[1] - 6
    col_count = padded.shape[2] - 6

    def sample(offset, direction):
        if direction == 0:
            return padded[
                3 + offset : 3 + offset + plane_count, 3 : 3 + row_count, 3 : 3 + col_count
            ]
        if direction == 1:
            return padded[
                plane_rim : plane_rim + plane_count,
                3 + offset : 3 + offset + row_count,
                3 : 3 + col_count,
            ]
        return padded[
            plane_rim : plane_rim + plane_count,
            3 : 3 + row_count,
            3 + offset : 3 + offset + col_count,
        ]

    summed = jnp.zeros((plane_count, row_count, col_count), jnp.float32)
    for direction in range(3):
        differences = [
            sample(offset + 1, direction) - sample(offset, direction) for offset in range(-3, 3)
        ]
        minus_side = weno_side(
            differences[0], differences[1], differences[2], differences[3], differences[4]
        )
        plus_side = weno_side(
            differences[5], differences[4], differences[3], differences[2], differences[1]
        )
        upwind = jnp.where(speeds[direction] >= 0.0, minus_side, plus_side)
        summed = summed - speeds[direction] * upwind
    return summed


def refine(coarse):
    plane_count, height, breadth = coarse.shape
    spread_out = jnp.broadcast_to(
        coarse[:, None, :, None, :, None], (plane_count, 2, height, 2, breadth, 2)
    )
    return spread_out.reshape(2 * plane_count, 2 * height, 2 * breadth)


def coarsen(fine_field):
    plane_count, height, breadth = fine_field.shape
    blocks = fine_field.reshape(plane_count // 2, 2, height // 2, 2, breadth // 2, 2)
    return jnp.sum(blocks, axis=(1, 3, 5)) * 0.125


def band_cells(tile_flags):
    planes, height, breadth = tile_flags.shape
    spread_out = jnp.broadcast_to(
        tile_flags[:, None, :, None, :, None], (planes, 8, height, 4, breadth, 16)
    )
    return spread_out.reshape(planes * 8, height * 4, breadth * 16)


def with_nozzle(banded, phases):
    inflow = jnp.where(phases == 2, 1.5, jnp.where(phases == 1, -1.5, banded[0]))
    return jnp.concatenate([inflow[None], banded[1:]], axis=0)


def surface_finish(normal_x, normal_y, normal_z, curvature, surface_level):
    delta_peak = jnp.exp(-surface_level * surface_level / (2.0 * SPREAD * SPREAD)) / (
        SPREAD * 2.5066282746310002
    )
    strength = SURFACE * curvature * delta_peak
    fraction = 0.5 + 0.5 * jnp.tanh(surface_level / SPREAD)
    return jnp.stack(
        [
            coarsen(normal_x * strength),
            coarsen(normal_y * strength),
            coarsen(normal_z * strength),
            coarsen(fraction),
        ]
    )


def surface_slab(padded):
    grad_x = (padded[1:-1, 2:, 1:-1] - padded[1:-1, :-2, 1:-1]) * 0.5
    grad_y = (padded[1:-1, 1:-1, 2:] - padded[1:-1, 1:-1, :-2]) * 0.5
    grad_z = (padded[2:, 1:-1, 1:-1] - padded[:-2, 1:-1, 1:-1]) * 0.5
    inverse = 1.0 / jnp.sqrt(grad_x * grad_x + grad_y * grad_y + grad_z * grad_z + 1.0)
    normal_x = grad_x * inverse
    normal_y = grad_y * inverse
    normal_z = grad_z * inverse
    curvature = (normal_x[1:-1, 2:, 1:-1] - normal_x[1:-1, :-2, 1:-1]) * 0.5
    curvature = curvature + (normal_y[1:-1, 1:-1, 2:] - normal_y[1:-1, 1:-1, :-2]) * 0.5
    curvature = curvature + (normal_z[2:, 1:-1, 1:-1] - normal_z[:-2, 1:-1, 1:-1]) * 0.5
    return surface_finish(
        normal_x[1:-1, 1:-1, 1:-1],
        normal_y[1:-1, 1:-1, 1:-1],
        normal_z[1:-1, 1:-1, 1:-1],
        curvature,
        padded[2:-2, 2:-2, 2:-2],
    )


def centered(padded, direction):
    if direction == 0:
        middle = padded[:, 1:-1, 1:-1]
        return (jnp.roll(middle, -1, 0) - jnp.roll(middle, 1, 0)) * 0.5
    if direction == 1:
        return (padded[:, 2:, 1:-1] - padded[:, :-2, 1:-1]) * 0.5
    return (padded[:, 1:-1, 2:] - padded[:, 1:-1, :-2]) * 0.5


def predictor(padded_fields, component):
    moving = lax.dynamic_index_in_dim(padded_fields, component, 0, keepdims=False)
    inner_u = padded_fields[0, :, 1:-1, 1:-1]
    inner_v = padded_fields[1, :, 1:-1, 1:-1]
    inner_w = padded_fields[2, :, 1:-1, 1:-1]
    advect = -(
        inner_w * centered(moving, 0)
        + inner_u * centered(moving, 1)
        + inner_v * centered(moving, 2)
    )
    pressure = padded_fields[3]
    gradients = jnp.stack([centered(pressure, 1), centered(pressure, 2), centered(pressure, 0)])
    pushed = lax.dynamic_index_in_dim(gradients, component, 0, keepdims=False)
    return moving[:, 1:-1, 1:-1] + STEP_FLOW * (advect - pushed)


def sweep_once(padded, source):
    middle = padded[:, 1:-1, 1:-1]
    beside_all = (
        padded[:, 2:, 1:-1] + padded[:, :-2, 1:-1] + padded[:, 1:-1, 2:] + padded[:, 1:-1, :-2]
    )
    beside_all = beside_all + jnp.roll(middle, -1, 0) + jnp.roll(middle, 1, 0)
    return (source + IMPLICIT * beside_all) / (1.0 + 6.0 * IMPLICIT)


def spread_surface(level_set, band_tiles, nozzle_phase, inner_fields, is_level, group):
    fine_all = level_set[0]
    initial = lax.psum_scatter(
        jnp.where(is_level, fine_all, jnp.zeros_like(fine_all)),
        "grp",
        scatter_dimension=0,
        tiled=True,
    )
    coarse_planes = inner_fields.shape[1] // 4
    flow_slab = lax.dynamic_slice_in_dim(inner_fields, group * coarse_planes, coarse_planes, 1)
    speeds = (refine(flow_slab[2]), refine(flow_slab[0]), refine(flow_slab[1]))

    def run_section(current, keep_weight, blend_weight):
        padded = extended(current, (("grp", 0), ("gx", 1), ("gy", 2)), 3)
        return keep_weight * initial + blend_weight * (
            current + STEP_FINE * section_rate(padded, speeds, 3)
        )

    first_section = run_section(initial, 0.0, 1.0)
    second_section = run_section(first_section, 0.75, 0.25)
    third_section = run_section(second_section, 1.0 / 3.0, 2.0 / 3.0)
    tile_planes = band_tiles.shape[0] // 4
    tiles_here = lax.dynamic_slice_in_dim(band_tiles, group * tile_planes, tile_planes, 0)
    banded = jnp.where(band_cells(tiles_here) == 1, third_section, initial)
    shaped = jnp.where(group == 0, with_nozzle(banded, nozzle_phase), banded)
    surface_pad = extended(shaped, (("grp", 0), ("gx", 1), ("gy", 2)), 2)
    quarter = surface_slab(surface_pad)
    received = lax.all_to_all(quarter, "grp", split_axis=0, concat_axis=1, tiled=True)
    return (received, received[0])


def on_device_general(flow_fields, level_set, band_tiles, nozzle_phase):
    group = lax.axis_index("grp")
    component = jnp.minimum(group, 2)
    is_level = group == 3
    gathered = lax.all_gather(flow_fields, "grp", axis=0, tiled=True)
    padded_fields = extended(gathered, (("gx", 2), ("gy", 3)), 1)
    source = predictor(padded_fields, component)
    inner_fields = padded_fields[:, :, 1:-1, 1:-1]
    received, fraction = spread_surface(
        level_set, band_tiles, nozzle_phase, inner_fields, is_level, group
    )
    pushed = received[0]
    relaxed = source
    for sweep_number in range(SWEEPS):
        padded = extended(relaxed, (("gx", 1), ("gy", 2)), 1)
        relaxed = sweep_once(padded, source)
    updated = relaxed + STEP_FLOW * pushed
    result = jnp.where(is_level, fraction, updated)
    return result[None]


MESH = pl.DeviceIdType.MESH
LANES = 128
ROWS = 8
EXACT = lax.Precision.HIGHEST


def lanes_of(shape, dim=1):
    return lax.broadcasted_iota(jnp.int32, shape, dim)


def along_z(block, offset, period):
    spot = lanes_of(block.shape) % period
    plain = pltpu.roll(block, (-offset) % LANES, 1)
    if offset > 0:
        around = pltpu.roll(block, (period - offset) % LANES, 1)
        return jnp.where(spot < period - offset, plain, around)
    around = pltpu.roll(block, (-period - offset) % LANES, 1)
    return jnp.where(spot >= -offset, plain, around)


def along_rows(block, offset):
    return pltpu.roll(block, (-offset) % block.shape[0], 0)


def halves_of(block):
    top = block.astype(jnp.bfloat16)
    rest = (block - top.astype(jnp.float32)).astype(jnp.bfloat16)
    return top, rest


def plain_dot(left, right):
    return jnp.dot(left, right, preferred_element_type=jnp.float32)


def inverse_of(block):
    rough = pl.reciprocal(block, approx=True)
    return rough * (2.0 - block * rough)


def weno_flux(bends, near, speed, forward, pace):
    step_a = jnp.where(forward, bends[0], bends[4])
    step_b = jnp.where(forward, bends[1], bends[3])
    step_c = bends[2]
    step_d = jnp.where(forward, bends[3], bends[1])
    three = jnp.where(forward, near[0], near[1])

    def weight(curve, slope):
        inverse = inverse_of(
            (WENO_EPS * 12.0 / 13.0) + curve * curve + (3.0 / 13.0) * (slope * slope)
        )
        return inverse * inverse

    triple_c = 3.0 * step_c
    weight_one = weight(step_b - step_a, 3.0 * step_b - step_a)
    weight_two = 6.0 * weight(step_c - step_b, step_c + step_b)
    weight_three = 3.0 * weight(step_d - step_c, triple_c - step_d)
    mixed = (
        weight_one * (5.0 * step_b - 2.0 * step_a)
        + weight_two * (step_b + 2.0 * step_c)
        + weight_three * (step_c + triple_c - step_d)
    )
    total = weight_one + weight_two + weight_three
    return speed * three + (pace * mixed) * inverse_of(total)


def window(index, count, chunk, margin):
    low = index * chunk - margin
    high = (index + 1) * chunk + margin
    start, stop = max(low, 0), min(high, count * chunk)
    return start, stop - start, start - low


def brick_kernel(
    plan,
    flow_far,
    level_far,
    band_far,
    phase_far,
    out_ref,
    flow_ref,
    level_ref,
    band_ref,
    phase_ref,
    flow_turned,
    level_turned,
    marks_turned,
    flow_in,
    level_in,
    marks_in,
    speeds,
    stage_one,
    stage_two,
    shaped,
    normals,
    packed,
    results,
    gathered,
    send_sems,
    take_sems,
    load_sems,
):
    groups, halves, rings = plan["groups"], plan["halves"], plan["rings"]
    chunks = groups * halves
    fine_chunk, flow_chunk = plan["fine_chunk"], plan["flow_chunk"]
    fine_z, flow_z = plan["fine_z"], plan["flow_z"]
    fine_margin, mark_margin, flow_margin = 2 * ROWS, ROWS, ROWS
    fine_rows, flow_rows = chunks * fine_chunk, chunks * flow_chunk
    pairs = level_ref.shape[1] // 2
    majors = pairs * halves
    group = lax.axis_index("grp")
    half = lax.axis_index("gx")
    ring = lax.axis_index("gy")
    after = lax.rem(ring + 1, rings)
    before = lax.rem(ring + rings - 1, rings)
    mine = group * halves + half
    last = chunks - 1

    holder = group == groups - 1
    load_level = pltpu.make_async_copy(level_far, level_ref, load_sems.at[0])
    load_flow = pltpu.make_async_copy(flow_far, flow_ref, load_sems.at[1])
    load_band = pltpu.make_async_copy(band_far, band_ref, load_sems.at[2])
    load_phase = pltpu.make_async_copy(phase_far, phase_ref, load_sems.at[3])
    pl.when(holder)(load_level.start)
    load_flow.start()
    load_band.start()
    load_phase.start()

    barrier = pltpu.get_barrier_semaphore()

    def greet(target_group, target_half, target_ring):
        pl.semaphore_signal(
            barrier,
            inc=1,
            device_id=(target_group, target_half, target_ring),
            device_id_type=MESH,
        )

    for chunk in range(chunks):
        tg, th = chunk // halves, chunk % halves

        @pl.when(mine != chunk)
        def _(tg=tg, th=th):
            greet(tg, th, ring)

        @pl.when(mine == 0)
        def _(tg=tg, th=th):
            greet(tg, th, before)

        @pl.when(mine == last)
        def _(tg=tg, th=th):
            greet(tg, th, after)

    @pl.when(holder)
    def _():
        load_level.wait()
        for pair in range(pairs):
            both = [level_ref[:, 2 * pair], level_ref[:, 2 * pair + 1]]
            level_turned[pair] = jnp.concatenate(both, axis=0).T

    load_flow.wait()
    columns = [flow_ref[:, column] for column in range(flow_ref.shape[1])]
    flow_turned[...] = jnp.concatenate(columns * halves, axis=0).T
    load_band.wait()
    load_phase.wait()
    tiles_z, tiles_y = band_ref.shape
    wide_shape = (tiles_y, fine_rows)
    widen = (
        lanes_of(wide_shape) // (fine_rows // tiles_y)
        == lax.broadcasted_iota(jnp.int32, wide_shape, 0)
    ).astype(jnp.float32)
    wide_band = jnp.dot(
        band_ref[...].astype(jnp.float32), widen, preferred_element_type=jnp.float32
    )
    spare = LANES - tiles_z - phase_ref.shape[0]
    marks_turned[...] = jnp.concatenate(
        [
            wide_band,
            phase_ref[...].astype(jnp.float32),
            jnp.zeros((spare, fine_rows), jnp.float32),
        ],
        axis=0,
    ).T

    pl.semaphore_wait(barrier, chunks + 1)

    sent = []

    def push(source, target, chunk, ring_to, take, condition=None):
        tg, th = chunk // halves, chunk % halves
        slot = len(sent)
        remote = pltpu.make_async_remote_copy(
            src_ref=source,
            dst_ref=target,
            send_sem=send_sems.at[slot],
            recv_sem=take_sems.at[take],
            device_id=(tg, th, ring_to),
            device_id_type=MESH,
        )
        near = ring_to is ring
        far = mine != chunk if near else None
        if condition is not None:
            far = condition if far is None else jnp.logical_and(condition, far)
        if near:
            here = mine == chunk
            if condition is not None:
                here = jnp.logical_and(condition, here)

            @pl.when(here)
            def _():
                pltpu.make_async_copy(source, target, take_sems.at[take]).start()

        if far is None:
            remote.start()
        else:
            pl.when(far)(remote.start)
        sent.append((far, remote))

    major_spot = pl.ds(half * pairs, pairs)
    for chunk in range(chunks):
        start, count, spot = window(chunk, chunks, fine_chunk, fine_margin)
        push(
            level_turned.at[:, pl.ds(start, count)],
            level_in.at[major_spot, pl.ds(spot, count)],
            chunk,
            ring,
            0,
            holder,
        )
    push(
        level_turned.at[:, pl.ds(fine_rows - fine_margin, fine_margin)],
        level_in.at[major_spot, pl.ds(0, fine_margin)],
        0,
        after,
        0,
        holder,
    )
    push(
        level_turned.at[:, pl.ds(0, fine_margin)],
        level_in.at[major_spot, pl.ds(fine_margin + fine_chunk, fine_margin)],
        last,
        before,
        0,
        holder,
    )
    for chunk in range(chunks):
        start, count, spot = window(chunk, chunks, flow_chunk, flow_margin)
        push(
            flow_turned.at[pl.ds(start, count)],
            flow_in.at[group, half, pl.ds(spot, count)],
            chunk,
            ring,
            1,
        )
    push(
        flow_turned.at[pl.ds(flow_rows - flow_margin, flow_margin)],
        flow_in.at[group, half, pl.ds(0, flow_margin)],
        0,
        after,
        1,
    )
    push(
        flow_turned.at[pl.ds(0, flow_margin)],
        flow_in.at[group, half, pl.ds(flow_margin + flow_chunk, flow_margin)],
        last,
        before,
        1,
    )
    for chunk in range(chunks):
        start, count, spot = window(chunk, chunks, fine_chunk, mark_margin)
        push(
            marks_turned.at[pl.ds(start, count)],
            marks_in.at[half, pl.ds(spot, count)],
            chunk,
            ring,
            2,
            group == chunk // halves,
        )
    push(
        marks_turned.at[pl.ds(fine_rows - mark_margin, mark_margin)],
        marks_in.at[half, pl.ds(0, mark_margin)],
        0,
        after,
        2,
        group == 0,
    )
    push(
        marks_turned.at[pl.ds(0, mark_margin)],
        marks_in.at[half, pl.ds(mark_margin + fine_chunk, mark_margin)],
        last,
        before,
        2,
        group == groups - 1,
    )

    body = fine_chunk + 2 * mark_margin
    offset = fine_margin - mark_margin
    edge = jnp.zeros((majors, offset, LANES), jnp.float32)
    for stage in (stage_one, stage_two):
        stage[:, pl.ds(0, offset)] = edge
        stage[:, pl.ds(offset + body, offset)] = edge

    pltpu.make_async_copy(flow_in, flow_in, take_sems.at[1]).wait()
    share = LANES // halves
    fields = []
    flow_lane = lanes_of((flow_chunk + 2 * flow_margin, LANES))
    for field in range(groups):
        merged = flow_in[field, 0]
        for part in range(1, halves):
            merged = jnp.where(flow_lane >= part * share, flow_in[field, part], merged)
        fields.append(merged)

    from_flow = lax.broadcasted_iota(jnp.int32, (LANES, majors * LANES), 0)
    to_fine = lanes_of((LANES, majors * LANES))
    fine_cell = (to_fine // LANES) * flow_z + (to_fine % fine_z) // 2
    spread_lanes = (from_flow == fine_cell).astype(jnp.bfloat16)
    flow_window = flow_chunk + 2 * flow_margin
    spread_shape = (3 * body, 3 * flow_window)
    spread_to = lax.broadcasted_iota(jnp.int32, spread_shape, 0)
    spread_rows = (
        lanes_of(spread_shape)
        == spread_to // body * flow_window
        + spread_to % body // 2
        + (flow_margin - mark_margin // 2)
    ).astype(jnp.bfloat16)
    wide = jnp.zeros((3 * body, majors * LANES), jnp.float32)
    for piece in halves_of(jnp.concatenate(fields[:3], axis=0)):
        tall = plain_dot(spread_rows, piece).astype(jnp.bfloat16)
        wide = wide + plain_dot(tall, spread_lanes)
    for direction in range(3):
        for major in range(majors):
            speeds[direction, major] = wide[
                direction * body : (direction + 1) * body, major * LANES : (major + 1) * LANES
            ]

    def flow_beside(block, direction, step):
        if direction == 0:
            return pltpu.roll(block, (-step * flow_z) % LANES, 1)
        if direction == 1:
            return along_rows(block, step)
        return along_z(block, step, flow_z)

    def flow_slope(block, direction):
        return 0.5 * (flow_beside(block, direction, 1) - flow_beside(block, direction, -1))

    moved = []
    for component in range(3):
        moving = fields[component]
        advect = fields[0] * flow_slope(moving, 0)
        advect = advect + fields[1] * flow_slope(moving, 1)
        advect = advect + fields[2] * flow_slope(moving, 2)
        source = moving - STEP_FLOW * (advect + flow_slope(fields[3], component))
        relaxed = source
        for sweep_number in range(SWEEPS):
            beside = jnp.zeros_like(relaxed)
            for direction in range(3):
                beside = beside + flow_beside(relaxed, direction, 1)
                beside = beside + flow_beside(relaxed, direction, -1)
            relaxed = (source + IMPLICIT * beside) * (1.0 / (1.0 + 6.0 * IMPLICIT))
        moved.append(relaxed[flow_margin : flow_margin + flow_chunk])

    pltpu.make_async_copy(level_in, level_in, take_sems.at[0]).wait()

    block_rows = 2 * ROWS

    def section(current, target, keep, blend):
        def one(major, carry):
            def far_major(step):
                return lax.rem(major + majors + step, majors)

            for start in range(0, body, block_rows):
                rows = pl.ds(offset + start, block_rows)
                tall = current[major, pl.ds(start, block_rows + 2 * offset)]
                middle = tall[offset : offset + block_rows]
                low_half = lanes_of(middle.shape) < fine_z
                whole = {step: current[far_major(step), rows] for step in (-2, -1, 1, 2)}
                whole[0] = middle
                swapped = {step: pltpu.roll(whole[step], fine_z, 1) for step in whole}

                def beside(direction, step):
                    if step == 0:
                        return middle
                    if direction == 1:
                        return tall[offset + step : offset + step + block_rows]
                    if direction == 2:
                        return along_z(middle, step, fine_z)
                    base = step // 2
                    if step % 2 == 0:
                        return whole[base]
                    return jnp.where(low_half, swapped[base], swapped[base + 1])

                rate = jnp.zeros_like(middle)
                for direction in range(3):
                    cells = [beside(direction, step) for step in range(-3, 4)]
                    diffs = [cells[i + 1] - cells[i] for i in range(6)]
                    bends = [diffs[i + 1] - diffs[i] for i in range(5)]
                    near = (diffs[2], diffs[3])
                    speed = speeds[direction, major, pl.ds(start, block_rows)]
                    forward = speed >= 0.0
                    pace = jnp.abs(speed) * (1.0 / 6.0)
                    rate = rate - weno_flux(bends, near, speed, forward, pace)
                moved_on = blend * (middle + STEP_FINE * rate)
                if keep:
                    moved_on = keep * level_in[major, rows] + moved_on
                target[major, rows] = moved_on
            return carry

        lax.fori_loop(0, majors, one, 0)

    section(level_in, stage_one, 0.0, 1.0)
    section(stage_one, stage_two, 0.75, 0.25)
    section(stage_two, stage_one, 1.0 / 3.0, 2.0 / 3.0)

    pltpu.make_async_copy(marks_in, marks_in, take_sems.at[2]).wait()
    mark_from = lax.broadcasted_iota(jnp.int32, (LANES, LANES), 0)
    mark_to = lanes_of((LANES, LANES))
    tile_z = plan["tile_z"]
    tile_count = fine_z // tile_z
    inside = pl.ds(offset, body)
    spread_band = (mark_from == (mark_to % fine_z) // tile_z).astype(jnp.float32)
    for part in range(halves):
        marks = marks_in[part]
        band = jnp.dot(marks, spread_band, preferred_element_type=jnp.float32)
        for pair in range(pairs):
            pick = jnp.logical_and(
                mark_from == tile_count + 2 * pair + mark_to // fine_z, mark_to % fine_z == 0
            ).astype(jnp.float32)
            phase = jnp.dot(marks, pick, preferred_element_type=jnp.float32)
            major = part * pairs + pair
            banded = jnp.where(band > 0.5, stage_one[major, inside], level_in[major, inside])
            shaped[major] = jnp.where(
                phase > 1.5, SPREAD, jnp.where(phase > 0.5, -SPREAD, banded)
            )

    low_half = lanes_of((body, LANES)) < fine_z

    def x_slope(ref, major):
        here = pltpu.roll(ref[major], fine_z, 1)
        up = pltpu.roll(ref[(major + 1) % majors], fine_z, 1)
        down = pltpu.roll(ref[(major + majors - 1) % majors], fine_z, 1)
        return 0.5 * (jnp.where(low_half, here, up) - jnp.where(low_half, down, here))

    for major in range(majors):
        level = shaped[major]
        slope_x = x_slope(shaped, major)
        slope_y = 0.5 * (along_rows(level, 1) - along_rows(level, -1))
        slope_z = 0.5 * (along_z(level, 1, fine_z) - along_z(level, -1, fine_z))
        inverse = lax.rsqrt(slope_x * slope_x + slope_y * slope_y + slope_z * slope_z + 1.0)
        normals[0, major] = slope_x * inverse
        normals[1, major] = slope_y * inverse
        normals[2, major] = slope_z * inverse

    core = slice(mark_margin, mark_margin + fine_chunk)
    for major in range(majors):
        normal_y, normal_z = normals[1, major], normals[2, major]
        curvature = x_slope(normals.at[0], major)
        curvature = curvature + 0.5 * (along_rows(normal_y, 1) - along_rows(normal_y, -1))
        curvature = curvature + 0.5 * (
            along_z(normal_z, 1, fine_z) - along_z(normal_z, -1, fine_z)
        )
        level = shaped[major]
        delta_peak = jnp.exp(level * level * (-1.0 / (2.0 * SPREAD * SPREAD)))
        strength = (SURFACE / (SPREAD * 2.5066282746310002)) * curvature * delta_peak
        lane_spot = slice(major * LANES, (major + 1) * LANES)
        for direction in range(3):
            force = (normals[direction, major] * strength)[core]
            packed[pl.ds(direction * fine_chunk, fine_chunk), lane_spot] = force
        fraction = (0.5 + 0.5 * jnp.tanh(level * (1.0 / SPREAD)))[core]
        packed[pl.ds(3 * fine_chunk, fine_chunk), lane_spot] = fraction

    fine_from = lax.broadcasted_iota(jnp.int32, (majors * LANES, LANES), 0)
    flow_to = lanes_of((majors * LANES, LANES))
    fold_lanes = (
        flow_to == (fine_from // LANES) * flow_z + (fine_from % fine_z) // 2
    ).astype(jnp.bfloat16)
    top, rest = halves_of(packed[...])
    folded = plain_dot(top, fold_lanes) + plain_dot(rest, fold_lanes)
    fold_shape = (4 * flow_chunk, 4 * fine_chunk)
    fold_rows = (
        lanes_of(fold_shape) // 2 == lax.broadcasted_iota(jnp.int32, fold_shape, 0)
    ).astype(jnp.bfloat16)
    top, rest = halves_of(folded)
    means = 0.125 * (plain_dot(fold_rows, top) + plain_dot(fold_rows, rest))
    for output in range(4):
        mean = means[output * flow_chunk : (output + 1) * flow_chunk]
        results[output] = moved[output] + STEP_FLOW * mean if output < 3 else mean

    landing = pl.ds(pl.multiple_of(mine * flow_chunk, flow_chunk), flow_chunk)
    for chunk in range(chunks):
        push(results.at[chunk // halves], gathered.at[landing], chunk, ring, 3)
    pltpu.make_async_copy(gathered, gathered, take_sems.at[3]).wait()
    turned = gathered[...].T
    outcome = turned[:share]
    for part in range(1, halves):
        outcome = jnp.where(half == part, turned[part * share : (part + 1) * share], outcome)
    out_ref[...] = outcome
    for condition, copy in sent:
        if condition is None:
            copy.wait_send()
        else:
            pl.when(condition)(copy.wait_send)


def on_device_bricks(plan, flow_fields, level_set, band_tiles, nozzle_phase):
    flow_z, flow_x, flow_y = flow_fields.shape[1:]
    fine_z, fine_x, fine_y = level_set.shape[1:]
    groups, halves = plan["groups"], plan["halves"]
    chunks = groups * halves
    fine_chunk, flow_chunk = fine_y // chunks, flow_y // chunks
    tiles_z = band_tiles.shape[0]
    plan = dict(
        plan,
        fine_chunk=fine_chunk,
        flow_chunk=flow_chunk,
        fine_z=fine_z,
        flow_z=flow_z,
        tile_z=fine_z // tiles_z,
    )
    majors = fine_x // 2 * halves
    body = fine_chunk + 2 * ROWS
    tall = fine_chunk + 4 * ROWS
    vmem = pl.BlockSpec(memory_space=pltpu.VMEM)

    def room(*shape):
        return pltpu.VMEM(shape, jnp.float32)

    copies = 4 * chunks + 6
    result = pl.pallas_call(
        functools.partial(brick_kernel, plan),
        out_shape=jax.ShapeDtypeStruct((flow_x * flow_z, flow_y), jnp.float32),
        in_specs=[pl.BlockSpec(memory_space=pltpu.HBM)] * 4,
        out_specs=vmem,
        scratch_shapes=[
            room(flow_z, flow_x, flow_y),
            room(fine_z, fine_x, fine_y),
            pltpu.VMEM((band_tiles.shape[0], band_tiles.shape[2]), band_tiles.dtype),
            pltpu.VMEM(nozzle_phase.shape, nozzle_phase.dtype),
            room(flow_y, LANES),
            room(fine_x // 2, fine_y, LANES),
            room(fine_y, LANES),
            room(groups, halves, flow_chunk + 2 * ROWS, LANES),
            room(majors, tall, LANES),
            room(halves, body, LANES),
            room(3, majors, body, LANES),
            room(majors, tall, LANES),
            room(majors, tall, LANES),
            room(majors, body, LANES),
            room(3, majors, body, LANES),
            room(4 * fine_chunk, majors * LANES),
            room(4, flow_chunk, LANES),
            room(flow_y, LANES),
            pltpu.SemaphoreType.DMA((copies,)),
            pltpu.SemaphoreType.DMA((4,)),
            pltpu.SemaphoreType.DMA((4,)),
        ],
        compiler_params=pltpu.CompilerParams(
            collective_id=0, has_side_effects=True, vmem_limit_bytes=60 * 1024 * 1024
        ),
        name="jet_step",
    )(flow_fields[0], level_set[0], band_tiles[:, 0], nozzle_phase)
    return result.reshape(flow_x, flow_z, flow_y).transpose(1, 0, 2)[None]


def solution(mesh):
    placed = (
        P("grp", None, "gx", "gy"),
        P("grp", None, "gx", "gy"),
        P(None, "gx", "gy"),
        P("gx", "gy"),
    )
    plan = {"groups": mesh.shape["grp"], "halves": mesh.shape["gx"], "rings": mesh.shape["gy"]}

    def on_device(flow_fields, level_set, band_tiles, nozzle_phase):
        flow_z, flow_x, flow_y = flow_fields.shape[1:]
        chunks = plan["groups"] * plan["halves"]
        fits = (
            plan["halves"] * flow_x * flow_z == LANES
            and 2 * level_set.shape[1] == LANES
            and flow_y == LANES
            and flow_y % (chunks * 2 * ROWS) == 0
            and band_tiles.shape[1] == 1
            and plan["rings"] > 2
        )
        if fits:
            return on_device_bricks(plan, flow_fields, level_set, band_tiles, nozzle_phase)
        return on_device_general(flow_fields, level_set, band_tiles, nozzle_phase)

    return jax.shard_map(
        on_device, mesh=mesh, in_specs=placed, out_specs=P("grp", None, "gx", "gy"), check_vma=False
    )
```

```python
import functools

import jax
import jax.numpy as jnp
from jax import lax
from jax.experimental import pallas as pl
from jax.experimental.pallas import tpu as pltpu
from jax.sharding import PartitionSpec as P

SWEEPS = 3


WENO_EPS = 1e-06
STEP_FINE = 0.3
STEP_FLOW = 0.2
SURFACE = 6.0
SPREAD = 1.5
IMPLICIT = 0.5


def extended(block, sides, width):
    for axis, dim in sides:
        count = lax.axis_size(axis)
        forward = [(i, i + 1) for i in range(count - 1)]
        forward.append((count - 1, 0))
        backward = [(target, source) for source, target in forward]
        low = lax.ppermute(
            lax.slice_in_dim(block, block.shape[dim] - width, None, axis=dim), axis, forward
        )
        high = lax.ppermute(lax.slice_in_dim(block, 0, width, axis=dim), axis, backward)
        block = jnp.concatenate([low, block, high], axis=dim)
    return block


def weno_side(diff_one, diff_two, diff_three, diff_four, diff_five):
    cand_one = diff_one / 3.0 - 7.0 * diff_two / 6.0 + 11.0 * diff_three / 6.0
    cand_two = -diff_two / 6.0 + 5.0 * diff_three / 6.0 + diff_four / 3.0
    cand_three = diff_three / 3.0 + 5.0 * diff_four / 6.0 - diff_five / 6.0
    curve_one = diff_one - 2.0 * diff_two + diff_three
    slope_one = diff_one - 4.0 * diff_two + 3.0 * diff_three
    smooth_one = 13.0 / 12.0 * curve_one * curve_one + 0.25 * slope_one * slope_one
    curve_two = diff_two - 2.0 * diff_three + diff_four
    slope_two = diff_two - diff_four
    smooth_two = 13.0 / 12.0 * curve_two * curve_two + 0.25 * slope_two * slope_two
    curve_three = diff_three - 2.0 * diff_four + diff_five
    slope_three = 3.0 * diff_three - 4.0 * diff_four + diff_five
    smooth_three = 13.0 / 12.0 * curve_three * curve_three + 0.25 * slope_three * slope_three
    weight_one = 0.1 / ((WENO_EPS + smooth_one) * (WENO_EPS + smooth_one))
    weight_two = 0.6 / ((WENO_EPS + smooth_two) * (WENO_EPS + smooth_two))
    weight_three = 0.3 / ((WENO_EPS + smooth_three) * (WENO_EPS + smooth_three))
    return (weight_one * cand_one + weight_two * cand_two + weight_three * cand_three) / (
        weight_one + weight_two + weight_three
    )


def section_rate(padded, speeds, plane_rim):
    plane_count = padded.shape[0] - 2 * plane_rim
    row_count = padded.shape[1] - 6
    col_count = padded.shape[2] - 6

    def sample(offset, direction):
        if direction == 0:
            return padded[
                3 + offset : 3 + offset + plane_count, 3 : 3 + row_count, 3 : 3 + col_count
            ]
        if direction == 1:
            return padded[
                plane_rim : plane_rim + plane_count,
                3 + offset : 3 + offset + row_count,
                3 : 3 + col_count,
            ]
        return padded[
            plane_rim : plane_rim + plane_count,
            3 : 3 + row_count,
            3 + offset : 3 + offset + col_count,
        ]

    summed = jnp.zeros((plane_count, row_count, col_count), jnp.float32)
    for direction in range(3):
        differences = [
            sample(offset + 1, direction) - sample(offset, direction) for offset in range(-3, 3)
        ]
        minus_side = weno_side(
            differences[0], differences[1], differences[2], differences[3], differences[4]
        )
        plus_side = weno_side(
            differences[5], differences[4], differences[3], differences[2], differences[1]
        )
        upwind = jnp.where(speeds[direction] >= 0.0, minus_side, plus_side)
        summed = summed - speeds[direction] * upwind
    return summed


def refine(coarse):
    plane_count, height, breadth = coarse.shape
    spread_out = jnp.broadcast_to(
        coarse[:, None, :, None, :, None], (plane_count, 2, height, 2, breadth, 2)
    )
    return spread_out.reshape(2 * plane_count, 2 * height, 2 * breadth)


def coarsen(fine_field):
    plane_count, height, breadth = fine_field.shape
    blocks = fine_field.reshape(plane_count // 2, 2, height // 2, 2, breadth // 2, 2)
    return jnp.sum(blocks, axis=(1, 3, 5)) * 0.125


def band_cells(tile_flags):
    planes, height, breadth = tile_flags.shape
    spread_out = jnp.broadcast_to(
        tile_flags[:, None, :, None, :, None], (planes, 8, height, 4, breadth, 16)
    )
    return spread_out.reshape(planes * 8, height * 4, breadth * 16)


def with_nozzle(banded, phases):
    inflow = jnp.where(phases == 2, 1.5, jnp.where(phases == 1, -1.5, banded[0]))
    return jnp.concatenate([inflow[None], banded[1:]], axis=0)


def surface_finish(normal_x, normal_y, normal_z, curvature, surface_level):
    delta_peak = jnp.exp(-surface_level * surface_level / (2.0 * SPREAD * SPREAD)) / (
        SPREAD * 2.5066282746310002
    )
    strength = SURFACE * curvature * delta_peak
    fraction = 0.5 + 0.5 * jnp.tanh(surface_level / SPREAD)
    return jnp.stack(
        [
            coarsen(normal_x * strength),
            coarsen(normal_y * strength),
            coarsen(normal_z * strength),
            coarsen(fraction),
        ]
    )


def surface_slab(padded):
    grad_x = (padded[1:-1, 2:, 1:-1] - padded[1:-1, :-2, 1:-1]) * 0.5
    grad_y = (padded[1:-1, 1:-1, 2:] - padded[1:-1, 1:-1, :-2]) * 0.5
    grad_z = (padded[2:, 1:-1, 1:-1] - padded[:-2, 1:-1, 1:-1]) * 0.5
    inverse = 1.0 / jnp.sqrt(grad_x * grad_x + grad_y * grad_y + grad_z * grad_z + 1.0)
    normal_x = grad_x * inverse
    normal_y = grad_y * inverse
    normal_z = grad_z * inverse
    curvature = (normal_x[1:-1, 2:, 1:-1] - normal_x[1:-1, :-2, 1:-1]) * 0.5
    curvature = curvature + (normal_y[1:-1, 1:-1, 2:] - normal_y[1:-1, 1:-1, :-2]) * 0.5
    curvature = curvature + (normal_z[2:, 1:-1, 1:-1] - normal_z[:-2, 1:-1, 1:-1]) * 0.5
    return surface_finish(
        normal_x[1:-1, 1:-1, 1:-1],
        normal_y[1:-1, 1:-1, 1:-1],
        normal_z[1:-1, 1:-1, 1:-1],
        curvature,
        padded[2:-2, 2:-2, 2:-2],
    )


def centered(padded, direction):
    if direction == 0:
        middle = padded[:, 1:-1, 1:-1]
        return (jnp.roll(middle, -1, 0) - jnp.roll(middle, 1, 0)) * 0.5
    if direction == 1:
        return (padded[:, 2:, 1:-1] - padded[:, :-2, 1:-1]) * 0.5
    return (padded[:, 1:-1, 2:] - padded[:, 1:-1, :-2]) * 0.5


def predictor(padded_fields, component):
    moving = lax.dynamic_index_in_dim(padded_fields, component, 0, keepdims=False)
    inner_u = padded_fields[0, :, 1:-1, 1:-1]
    inner_v = padded_fields[1, :, 1:-1, 1:-1]
    inner_w = padded_fields[2, :, 1:-1, 1:-1]
    advect = -(
        inner_w * centered(moving, 0)
        + inner_u * centered(moving, 1)
        + inner_v * centered(moving, 2)
    )
    pressure = padded_fields[3]
    gradients = jnp.stack([centered(pressure, 1), centered(pressure, 2), centered(pressure, 0)])
    pushed = lax.dynamic_index_in_dim(gradients, component, 0, keepdims=False)
    return moving[:, 1:-1, 1:-1] + STEP_FLOW * (advect - pushed)


def sweep_once(padded, source):
    middle = padded[:, 1:-1, 1:-1]
    beside_all = (
        padded[:, 2:, 1:-1] + padded[:, :-2, 1:-1] + padded[:, 1:-1, 2:] + padded[:, 1:-1, :-2]
    )
    beside_all = beside_all + jnp.roll(middle, -1, 0) + jnp.roll(middle, 1, 0)
    return (source + IMPLICIT * beside_all) / (1.0 + 6.0 * IMPLICIT)


def spread_surface(level_set, band_tiles, nozzle_phase, inner_fields, is_level, group):
    fine_all = level_set[0]
    initial = lax.psum_scatter(
        jnp.where(is_level, fine_all, jnp.zeros_like(fine_all)),
        "grp",
        scatter_dimension=0,
        tiled=True,
    )
    coarse_planes = inner_fields.shape[1] // 4
    flow_slab = lax.dynamic_slice_in_dim(inner_fields, group * coarse_planes, coarse_planes, 1)
    speeds = (refine(flow_slab[2]), refine(flow_slab[0]), refine(flow_slab[1]))

    def run_section(current, keep_weight, blend_weight):
        padded = extended(current, (("grp", 0), ("gx", 1), ("gy", 2)), 3)
        return keep_weight * initial + blend_weight * (
            current + STEP_FINE * section_rate(padded, speeds, 3)
        )

    first_section = run_section(initial, 0.0, 1.0)
    second_section = run_section(first_section, 0.75, 0.25)
    third_section = run_section(second_section, 1.0 / 3.0, 2.0 / 3.0)
    tile_planes = band_tiles.shape[0] // 4
    tiles_here = lax.dynamic_slice_in_dim(band_tiles, group * tile_planes, tile_planes, 0)
    banded = jnp.where(band_cells(tiles_here) == 1, third_section, initial)
    shaped = jnp.where(group == 0, with_nozzle(banded, nozzle_phase), banded)
    surface_pad = extended(shaped, (("grp", 0), ("gx", 1), ("gy", 2)), 2)
    quarter = surface_slab(surface_pad)
    received = lax.all_to_all(quarter, "grp", split_axis=0, concat_axis=1, tiled=True)
    return (received, received[0])


def on_device_general(flow_fields, level_set, band_tiles, nozzle_phase):
    group = lax.axis_index("grp")
    component = jnp.minimum(group, 2)
    is_level = group == 3
    gathered = lax.all_gather(flow_fields, "grp", axis=0, tiled=True)
    padded_fields = extended(gathered, (("gx", 2), ("gy", 3)), 1)
    source = predictor(padded_fields, component)
    inner_fields = padded_fields[:, :, 1:-1, 1:-1]
    received, fraction = spread_surface(
        level_set, band_tiles, nozzle_phase, inner_fields, is_level, group
    )
    pushed = received[0]
    relaxed = source
    for sweep_number in range(SWEEPS):
        padded = extended(relaxed, (("gx", 1), ("gy", 2)), 1)
        relaxed = sweep_once(padded, source)
    updated = relaxed + STEP_FLOW * pushed
    result = jnp.where(is_level, fraction, updated)
    return result[None]


MESH = pl.DeviceIdType.MESH
LANES = 128
ROWS = 8
EXACT = lax.Precision.HIGHEST


def lanes_of(shape, dim=1):
    return lax.broadcasted_iota(jnp.int32, shape, dim)


def along_z(block, offset, period):
    spot = lanes_of(block.shape) % period
    plain = pltpu.roll(block, (-offset) % LANES, 1)
    if offset > 0:
        around = pltpu.roll(block, (period - offset) % LANES, 1)
        return jnp.where(spot < period - offset, plain, around)
    around = pltpu.roll(block, (-period - offset) % LANES, 1)
    return jnp.where(spot >= -offset, plain, around)


def along_rows(block, offset):
    return pltpu.roll(block, (-offset) % block.shape[0], 0)


def halves_of(block):
    top = block.astype(jnp.bfloat16)
    rest = (block - top.astype(jnp.float32)).astype(jnp.bfloat16)
    return top, rest


def plain_dot(left, right):
    return jnp.dot(left, right, preferred_element_type=jnp.float32)


def inverse_of(block):
    rough = pl.reciprocal(block, approx=True)
    return rough * (2.0 - block * rough)


def weno_flux(bends, near, speed, forward, pace):
    step_a = jnp.where(forward, bends[0], bends[4])
    step_b = jnp.where(forward, bends[1], bends[3])
    step_c = bends[2]
    step_d = jnp.where(forward, bends[3], bends[1])
    three = jnp.where(forward, near[0], near[1])

    def weight(curve, slope):
        inverse = inverse_of(
            (WENO_EPS * 12.0 / 13.0) + curve * curve + (3.0 / 13.0) * (slope * slope)
        )
        return inverse * inverse

    triple_c = 3.0 * step_c
    weight_one = weight(step_b - step_a, 3.0 * step_b - step_a)
    weight_two = 6.0 * weight(step_c - step_b, step_c + step_b)
    weight_three = 3.0 * weight(step_d - step_c, triple_c - step_d)
    mixed = (
        weight_one * (5.0 * step_b - 2.0 * step_a)
        + weight_two * (step_b + 2.0 * step_c)
        + weight_three * (step_c + triple_c - step_d)
    )
    total = weight_one + weight_two + weight_three
    return speed * three + (pace * mixed) * inverse_of(total)


def window(index, count, chunk, margin):
    low = index * chunk - margin
    high = (index + 1) * chunk + margin
    start, stop = max(low, 0), min(high, count * chunk)
    return start, stop - start, start - low


def brick_kernel(
    plan,
    flow_far,
    level_far,
    band_far,
    phase_far,
    out_ref,
    flow_ref,
    level_ref,
    band_ref,
    phase_ref,
    flow_turned,
    level_turned,
    marks_turned,
    flow_in,
    level_in,
    marks_in,
    speeds,
    stage_one,
    stage_two,
    shaped,
    normals,
    packed,
    results,
    gathered,
    send_sems,
    take_sems,
    load_sems,
):
    groups, halves, rings = plan["groups"], plan["halves"], plan["rings"]
    chunks = groups * halves
    fine_chunk, flow_chunk = plan["fine_chunk"], plan["flow_chunk"]
    fine_z, flow_z = plan["fine_z"], plan["flow_z"]
    fine_margin, mark_margin, flow_margin = 2 * ROWS, ROWS, ROWS
    fine_rows, flow_rows = chunks * fine_chunk, chunks * flow_chunk
    pairs = level_ref.shape[1] // 2
    majors = pairs * halves
    group = lax.axis_index("grp")
    half = lax.axis_index("gx")
    ring = lax.axis_index("gy")
    after = lax.rem(ring + 1, rings)
    before = lax.rem(ring + rings - 1, rings)
    mine = group * halves + half
    last = chunks - 1

    holder = group == groups - 1
    load_level = pltpu.make_async_copy(level_far, level_ref, load_sems.at[0])
    load_flow = pltpu.make_async_copy(flow_far, flow_ref, load_sems.at[1])
    load_band = pltpu.make_async_copy(band_far, band_ref, load_sems.at[2])
    load_phase = pltpu.make_async_copy(phase_far, phase_ref, load_sems.at[3])
    pl.when(holder)(load_level.start)
    load_flow.start()
    load_band.start()
    load_phase.start()

    barrier = pltpu.get_barrier_semaphore()

    def greet(target_group, target_half, target_ring):
        pl.semaphore_signal(
            barrier,
            inc=1,
            device_id=(target_group, target_half, target_ring),
            device_id_type=MESH,
        )

    for chunk in range(chunks):

        @pl.when(mine != chunk)
        def _(chunk=chunk):
            greet(chunk // halves, chunk % halves, ring)

    for edge_chunk, beyond in ((0, before), (last, after)):

        @pl.when(mine == edge_chunk)
        def _(beyond=beyond):
            for chunk in range(chunks):
                greet(chunk // halves, chunk % halves, beyond)

    @pl.when(holder)
    def _():
        load_level.wait()
        for pair in range(pairs):
            both = [level_ref[:, 2 * pair], level_ref[:, 2 * pair + 1]]
            level_turned[pair] = jnp.concatenate(both, axis=0).T

    load_flow.wait()
    columns = [flow_ref[:, column] for column in range(flow_ref.shape[1])]
    flow_turned[...] = jnp.concatenate(columns * halves, axis=0).T
    load_band.wait()
    load_phase.wait()
    tiles_z, tiles_y = band_ref.shape
    wide_shape = (tiles_y, fine_rows)
    widen = (
        lanes_of(wide_shape) // (fine_rows // tiles_y)
        == lax.broadcasted_iota(jnp.int32, wide_shape, 0)
    ).astype(jnp.float32)
    wide_band = jnp.dot(
        band_ref[...].astype(jnp.float32), widen, preferred_element_type=jnp.float32
    )
    spare = LANES - tiles_z - phase_ref.shape[0]
    marks_turned[...] = jnp.concatenate(
        [
            wide_band,
            phase_ref[...].astype(jnp.float32),
            jnp.zeros((spare, fine_rows), jnp.float32),
        ],
        axis=0,
    ).T

    pl.semaphore_wait(barrier, chunks + 1)

    sent = []

    def entry(source, target, chunk, ring_to, take, slot):
        remote = pltpu.make_async_remote_copy(
            src_ref=source,
            dst_ref=target,
            send_sem=send_sems.at[take * (chunks + 2) + slot],
            recv_sem=take_sems.at[take],
            device_id=(chunk // halves, chunk % halves, ring_to),
            device_id_type=MESH,
        )

        def local():
            pltpu.make_async_copy(source, target, take_sems.at[take]).start()

        return chunk, ring_to is ring, remote, local

    def act(entries, own_group, finish):
        for chunk, near, remote, local in entries:
            step = remote.wait_send if finish else remote.start
            if near and own_group in (None, chunk // halves):
                pl.when(mine != chunk)(step)
                if not finish:
                    pl.when(mine == chunk)(local)
            else:
                step()

    def guarded(entries, own_group, finish):
        if own_group is None:
            act(entries, own_group, finish)
        else:
            pl.when(group == own_group)(lambda: act(entries, own_group, finish))

    def brick_entries(source, target, chunk_rows, margin, take):
        entries = []
        for chunk in range(chunks):
            start, count, spot = window(chunk, chunks, chunk_rows, margin)
            rows, landed = pl.ds(start, count), pl.ds(spot, count)
            entries.append(entry(source(rows), target(landed), chunk, ring, take, chunk))
        rows = pl.ds(chunks * chunk_rows - margin, margin)
        landed = pl.ds(0, margin)
        entries.append(entry(source(rows), target(landed), 0, after, take, chunks))
        rows, landed = pl.ds(0, margin), pl.ds(margin + chunk_rows, margin)
        entries.append(entry(source(rows), target(landed), last, before, take, chunks + 1))
        return entries

    major_spot = pl.ds(half * pairs, pairs)
    level_entries = brick_entries(
        lambda rows: level_turned.at[:, rows],
        lambda rows: level_in.at[major_spot, rows],
        fine_chunk,
        fine_margin,
        0,
    )
    flow_entries = brick_entries(
        lambda rows: flow_turned.at[rows],
        lambda rows: flow_in.at[group, half, rows],
        flow_chunk,
        flow_margin,
        1,
    )
    mark_entries = brick_entries(
        lambda rows: marks_turned.at[rows],
        lambda rows: marks_in.at[half, rows],
        fine_chunk,
        mark_margin,
        2,
    )

    def first_round(finish):
        guarded(level_entries, groups - 1, finish)
        guarded(flow_entries, None, finish)
        for part in range(groups):
            picked = [one for one in mark_entries if one[0] // halves == part]
            guarded(picked, part, finish)

    first_round(False)

    body = fine_chunk + 2 * mark_margin
    offset = fine_margin - mark_margin
    edge = jnp.zeros((majors, offset, LANES), jnp.float32)
    for stage in (stage_one, stage_two):
        stage[:, pl.ds(0, offset)] = edge
        stage[:, pl.ds(offset + body, offset)] = edge

    pltpu.make_async_copy(flow_in, flow_in, take_sems.at[1]).wait()
    share = LANES // halves
    fields = []
    flow_lane = lanes_of((flow_chunk + 2 * flow_margin, LANES))
    for field in range(groups):
        merged = flow_in[field, 0]
        for part in range(1, halves):
            merged = jnp.where(flow_lane >= part * share, flow_in[field, part], merged)
        fields.append(merged)

    from_flow = lax.broadcasted_iota(jnp.int32, (LANES, majors * LANES), 0)
    to_fine = lanes_of((LANES, majors * LANES))
    fine_cell = (to_fine // LANES) * flow_z + (to_fine % fine_z) // 2
    spread_lanes = (from_flow == fine_cell).astype(jnp.bfloat16)
    flow_window = flow_chunk + 2 * flow_margin
    spread_shape = (3 * body, 3 * flow_window)
    spread_to = lax.broadcasted_iota(jnp.int32, spread_shape, 0)
    spread_rows = (
        lanes_of(spread_shape)
        == spread_to // body * flow_window
        + spread_to % body // 2
        + (flow_margin - mark_margin // 2)
    ).astype(jnp.bfloat16)
    wide = jnp.zeros((3 * body, majors * LANES), jnp.float32)
    for piece in halves_of(jnp.concatenate(fields[:3], axis=0)):
        tall = plain_dot(spread_rows, piece).astype(jnp.bfloat16)
        wide = wide + plain_dot(tall, spread_lanes)
    for direction in range(3):
        for major in range(majors):
            speeds[direction, major] = wide[
                direction * body : (direction + 1) * body, major * LANES : (major + 1) * LANES
            ]

    def flow_beside(block, direction, step):
        if direction == 0:
            return pltpu.roll(block, (-step * flow_z) % LANES, 1)
        if direction == 1:
            return along_rows(block, step)
        return along_z(block, step, flow_z)

    def flow_slope(block, direction):
        return 0.5 * (flow_beside(block, direction, 1) - flow_beside(block, direction, -1))

    moved = []
    for component in range(3):
        moving = fields[component]
        advect = fields[0] * flow_slope(moving, 0)
        advect = advect + fields[1] * flow_slope(moving, 1)
        advect = advect + fields[2] * flow_slope(moving, 2)
        source = moving - STEP_FLOW * (advect + flow_slope(fields[3], component))
        relaxed = source
        for sweep_number in range(SWEEPS):
            beside = jnp.zeros_like(relaxed)
            for direction in range(3):
                beside = beside + flow_beside(relaxed, direction, 1)
                beside = beside + flow_beside(relaxed, direction, -1)
            relaxed = (source + IMPLICIT * beside) * (1.0 / (1.0 + 6.0 * IMPLICIT))
        moved.append(relaxed[flow_margin : flow_margin + flow_chunk])

    pltpu.make_async_copy(level_in, level_in, take_sems.at[0]).wait()

    block_rows = 2 * ROWS

    def section(current, target, keep, blend):
        def one(major, carry):
            def far_major(step):
                return lax.rem(major + majors + step, majors)

            for start in range(0, body, block_rows):
                rows = pl.ds(offset + start, block_rows)
                tall = current[major, pl.ds(start, block_rows + 2 * offset)]
                middle = tall[offset : offset + block_rows]
                low_half = lanes_of(middle.shape) < fine_z
                whole = {step: current[far_major(step), rows] for step in (-2, -1, 1, 2)}
                whole[0] = middle
                swapped = {step: pltpu.roll(whole[step], fine_z, 1) for step in whole}

                def beside(direction, step):
                    if step == 0:
                        return middle
                    if direction == 1:
                        return tall[offset + step : offset + step + block_rows]
                    if direction == 2:
                        return along_z(middle, step, fine_z)
                    base = step // 2
                    if step % 2 == 0:
                        return whole[base]
                    return jnp.where(low_half, swapped[base], swapped[base + 1])

                rate = jnp.zeros_like(middle)
                for direction in range(3):
                    cells = [beside(direction, step) for step in range(-3, 4)]
                    diffs = [cells[i + 1] - cells[i] for i in range(6)]
                    bends = [diffs[i + 1] - diffs[i] for i in range(5)]
                    near = (diffs[2], diffs[3])
                    speed = speeds[direction, major, pl.ds(start, block_rows)]
                    forward = speed >= 0.0
                    pace = jnp.abs(speed) * (1.0 / 6.0)
                    rate = rate - weno_flux(bends, near, speed, forward, pace)
                moved_on = blend * (middle + STEP_FINE * rate)
                if keep:
                    moved_on = keep * level_in[major, rows] + moved_on
                target[major, rows] = moved_on
            return carry

        lax.fori_loop(0, majors, one, 0)

    section(level_in, stage_one, 0.0, 1.0)
    section(stage_one, stage_two, 0.75, 0.25)
    section(stage_two, stage_one, 1.0 / 3.0, 2.0 / 3.0)

    pltpu.make_async_copy(marks_in, marks_in, take_sems.at[2]).wait()
    mark_from = lax.broadcasted_iota(jnp.int32, (LANES, LANES), 0)
    mark_to = lanes_of((LANES, LANES))
    tile_z = plan["tile_z"]
    tile_count = fine_z // tile_z
    inside = pl.ds(offset, body)
    spread_band = (mark_from == (mark_to % fine_z) // tile_z).astype(jnp.float32)
    for part in range(halves):
        marks = marks_in[part]
        band = jnp.dot(marks, spread_band, preferred_element_type=jnp.float32)
        for pair in range(pairs):
            pick = jnp.logical_and(
                mark_from == tile_count + 2 * pair + mark_to // fine_z, mark_to % fine_z == 0
            ).astype(jnp.float32)
            phase = jnp.dot(marks, pick, preferred_element_type=jnp.float32)
            major = part * pairs + pair
            banded = jnp.where(band > 0.5, stage_one[major, inside], level_in[major, inside])
            shaped[major] = jnp.where(
                phase > 1.5, SPREAD, jnp.where(phase > 0.5, -SPREAD, banded)
            )

    low_half = lanes_of((body, LANES)) < fine_z

    def x_slope(ref, major):
        here = pltpu.roll(ref[major], fine_z, 1)
        up = pltpu.roll(ref[(major + 1) % majors], fine_z, 1)
        down = pltpu.roll(ref[(major + majors - 1) % majors], fine_z, 1)
        return 0.5 * (jnp.where(low_half, here, up) - jnp.where(low_half, down, here))

    for major in range(majors):
        level = shaped[major]
        slope_x = x_slope(shaped, major)
        slope_y = 0.5 * (along_rows(level, 1) - along_rows(level, -1))
        slope_z = 0.5 * (along_z(level, 1, fine_z) - along_z(level, -1, fine_z))
        inverse = lax.rsqrt(slope_x * slope_x + slope_y * slope_y + slope_z * slope_z + 1.0)
        normals[0, major] = slope_x * inverse
        normals[1, major] = slope_y * inverse
        normals[2, major] = slope_z * inverse

    core = slice(mark_margin, mark_margin + fine_chunk)
    for major in range(majors):
        normal_y, normal_z = normals[1, major], normals[2, major]
        curvature = x_slope(normals.at[0], major)
        curvature = curvature + 0.5 * (along_rows(normal_y, 1) - along_rows(normal_y, -1))
        curvature = curvature + 0.5 * (
            along_z(normal_z, 1, fine_z) - along_z(normal_z, -1, fine_z)
        )
        level = shaped[major]
        delta_peak = jnp.exp(level * level * (-1.0 / (2.0 * SPREAD * SPREAD)))
        strength = (SURFACE / (SPREAD * 2.5066282746310002)) * curvature * delta_peak
        lane_spot = slice(major * LANES, (major + 1) * LANES)
        for direction in range(3):
            force = (normals[direction, major] * strength)[core]
            packed[pl.ds(direction * fine_chunk, fine_chunk), lane_spot] = force
        fraction = (0.5 + 0.5 * jnp.tanh(level * (1.0 / SPREAD)))[core]
        packed[pl.ds(3 * fine_chunk, fine_chunk), lane_spot] = fraction

    fine_from = lax.broadcasted_iota(jnp.int32, (majors * LANES, LANES), 0)
    flow_to = lanes_of((majors * LANES, LANES))
    fold_lanes = (
        flow_to == (fine_from // LANES) * flow_z + (fine_from % fine_z) // 2
    ).astype(jnp.bfloat16)
    top, rest = halves_of(packed[...])
    folded = plain_dot(top, fold_lanes) + plain_dot(rest, fold_lanes)
    fold_shape = (4 * flow_chunk, 4 * fine_chunk)
    fold_rows = (
        lanes_of(fold_shape) // 2 == lax.broadcasted_iota(jnp.int32, fold_shape, 0)
    ).astype(jnp.bfloat16)
    top, rest = halves_of(folded)
    means = 0.125 * (plain_dot(fold_rows, top) + plain_dot(fold_rows, rest))
    for output in range(4):
        mean = means[output * flow_chunk : (output + 1) * flow_chunk]
        results[output] = moved[output] + STEP_FLOW * mean if output < 3 else mean

    landing = pl.ds(pl.multiple_of(mine * flow_chunk, flow_chunk), flow_chunk)
    result_entries = [
        entry(results.at[chunk // halves], gathered.at[landing], chunk, ring, 3, chunk)
        for chunk in range(chunks)
    ]
    act(result_entries, None, False)
    first_round(True)
    act(result_entries, None, True)
    pltpu.make_async_copy(gathered, gathered, take_sems.at[3]).wait()
    turned = gathered[...].T
    outcome = turned[:share]
    for part in range(1, halves):
        outcome = jnp.where(half == part, turned[part * share : (part + 1) * share], outcome)
    out_ref[...] = outcome


def on_device_bricks(plan, flow_fields, level_set, band_tiles, nozzle_phase):
    flow_z, flow_x, flow_y = flow_fields.shape[1:]
    fine_z, fine_x, fine_y = level_set.shape[1:]
    groups, halves = plan["groups"], plan["halves"]
    chunks = groups * halves
    fine_chunk, flow_chunk = fine_y // chunks, flow_y // chunks
    tiles_z = band_tiles.shape[0]
    plan = dict(
        plan,
        fine_chunk=fine_chunk,
        flow_chunk=flow_chunk,
        fine_z=fine_z,
        flow_z=flow_z,
        tile_z=fine_z // tiles_z,
    )
    majors = fine_x // 2 * halves
    body = fine_chunk + 2 * ROWS
    tall = fine_chunk + 4 * ROWS
    vmem = pl.BlockSpec(memory_space=pltpu.VMEM)

    def room(*shape):
        return pltpu.VMEM(shape, jnp.float32)

    copies = 4 * (chunks + 2)
    result = pl.pallas_call(
        functools.partial(brick_kernel, plan),
        out_shape=jax.ShapeDtypeStruct((flow_x * flow_z, flow_y), jnp.float32),
        in_specs=[pl.BlockSpec(memory_space=pltpu.HBM)] * 4,
        out_specs=vmem,
        scratch_shapes=[
            room(flow_z, flow_x, flow_y),
            room(fine_z, fine_x, fine_y),
            pltpu.VMEM((band_tiles.shape[0], band_tiles.shape[2]), band_tiles.dtype),
            pltpu.VMEM(nozzle_phase.shape, nozzle_phase.dtype),
            room(flow_y, LANES),
            room(fine_x // 2, fine_y, LANES),
            room(fine_y, LANES),
            room(groups, halves, flow_chunk + 2 * ROWS, LANES),
            room(majors, tall, LANES),
            room(halves, body, LANES),
            room(3, majors, body, LANES),
            room(majors, tall, LANES),
            room(majors, tall, LANES),
            room(majors, body, LANES),
            room(3, majors, body, LANES),
            room(4 * fine_chunk, majors * LANES),
            room(4, flow_chunk, LANES),
            room(flow_y, LANES),
            pltpu.SemaphoreType.DMA((copies,)),
            pltpu.SemaphoreType.DMA((4,)),
            pltpu.SemaphoreType.DMA((4,)),
        ],
        compiler_params=pltpu.CompilerParams(
            collective_id=0, has_side_effects=True, vmem_limit_bytes=60 * 1024 * 1024
        ),
        name="jet_step",
    )(flow_fields[0], level_set[0], band_tiles[:, 0], nozzle_phase)
    return result.reshape(flow_x, flow_z, flow_y).transpose(1, 0, 2)[None]


def solution(mesh):
    placed = (
        P("grp", None, "gx", "gy"),
        P("grp", None, "gx", "gy"),
        P(None, "gx", "gy"),
        P("gx", "gy"),
    )
    plan = {"groups": mesh.shape["grp"], "halves": mesh.shape["gx"], "rings": mesh.shape["gy"]}

    def on_device(flow_fields, level_set, band_tiles, nozzle_phase):
        flow_z, flow_x, flow_y = flow_fields.shape[1:]
        chunks = plan["groups"] * plan["halves"]
        fits = (
            plan["halves"] * flow_x * flow_z == LANES
            and 2 * level_set.shape[1] == LANES
            and flow_y == LANES
            and flow_y % (chunks * 2 * ROWS) == 0
            and band_tiles.shape[1] == 1
            and plan["rings"] > 2
        )
        if fits:
            return on_device_bricks(plan, flow_fields, level_set, band_tiles, nozzle_phase)
        return on_device_general(flow_fields, level_set, band_tiles, nozzle_phase)

    return jax.shard_map(
        on_device, mesh=mesh, in_specs=placed, out_specs=P("grp", None, "gx", "gy"), check_vma=False
    )
```
